32 devices in a mesh: sect: 2 (over y), node: 4 (over z), fn: 2 (over x), sub: 2 (over core).
Axes of the slice: x: 2, y: 2, z: 4, core: 2. Of those that a mesh axis runs over, the one named last changes fastest.
Arguments:
- volume_grad: bfloat16 [2048, 32, 128], P(('sect', 'node', 'fn', 'sub')), parts along dimension 0, may hold values from -0.5 to 0.5
- volume_coords: float32 [2048, 3, 128], P(('sect', 'node', 'fn', 'sub')), parts along dimension 0, may hold values from -2.1366198 to 3
- support: int32 [2048, 32], P(('sect', 'node', 'fn', 'sub')), parts along dimension 0, may hold values from 0 to 31
- control_coords: float32 [64, 3, 128], P(('sect', 'node')), parts along dimension 0, may hold values from -2.1366198 to 3
- neighbours: int32 [64, 4], P(('sect', 'node')), parts along dimension 0, may hold values from 0 to 31
- block_inverse: float32 [64, 128, 128], P(('sect', 'node')), parts along dimension 0, may hold values from -0.09375 to 0.09375
Outputs:
- control_gradient: float32 [64, 32, 128], P(('sect', 'node')), parts along dimension 0
- adjoint: float32 [64, 32, 128], P(('sect', 'node')), parts along dimension 0
The draws below stay inside these ranges and needn't reach their ends.
There are 2 independent parts, one for each index of `sect`. The reference program is written for one: setup_inputs(seed, part) draws one part's arguments, and reference() takes and returns one part's arrays. A program takes and returns all parts, laid end to end along the dimension named above; each array names one. Nothing has to cross between parts.
All inputs are finite; a program needn't handle non-finite values.
Results may differ from the reference program's by a relative error of at most 0.0034.
Values may be sent and summed in bfloat16 or wider, within the bound.
No kernel may reach another device: no remote copies, remote signals or barrier semaphores. Data moves between devices by JAX's collectives and lax.ppermute only.
A program may use at most 64 MiB of HBM per device.

```python
import math
import jax
import jax.numpy as jnp
from jax import lax

FUNC = 32
BLOCK = 128
SUPPORT = 32
COUPLED = 4
SWEEPS = 2
NSB = 1024
NCB = 32


ARC_LENGTH = 4.0


AXIAL_DEPTH = 3.0


LAYER_THICKNESS = 1.5


def cycle_shape():
    window = min(SUPPORT, NCB)
    spacing = ARC_LENGTH / window
    cycle_radius = NCB * spacing / (2.0 * math.pi)
    return (window, spacing, cycle_radius)


def cycle_positions(key):
    return jax.random.permutation(jax.random.fold_in(key, 101), NCB).astype(jnp.int32)


def cycle_holder(key):
    positions = cycle_positions(key)
    return jnp.zeros((NCB,), jnp.int32).at[positions].set(jnp.arange(NCB, dtype=jnp.int32))


def window_centers(key):
    first_starts = jax.random.permutation(jax.random.fold_in(key, 202), NCB).astype(jnp.int32)
    random_starts = jax.random.randint(jax.random.fold_in(key, 303), (NSB,), 0, NCB, dtype=jnp.int32)
    shell_index = jnp.arange(NSB, dtype=jnp.int32)
    return jnp.where(shell_index < NCB, first_starts[shell_index % NCB], random_starts)


def draw_support(key, part):
    window, spacing, cycle_radius = cycle_shape()
    holder = cycle_holder(key)
    centers = window_centers(key)
    listed = jnp.arange(SUPPORT, dtype=jnp.int32) % window - window // 2
    cycle_slots = (centers[:, None] + listed[None, :]) % NCB
    return holder[cycle_slots]


def draw_volume_coords(key, part):
    window, spacing, cycle_radius = cycle_shape()
    centers = window_centers(key).astype(jnp.float32)
    along = jax.random.uniform(jax.random.fold_in(key, 404), (NSB, BLOCK), jnp.float32)
    across = jax.random.uniform(jax.random.fold_in(key, 505), (NSB, BLOCK), jnp.float32)
    height = jax.random.uniform(jax.random.fold_in(key, 606), (NSB, BLOCK), jnp.float32)
    arc_place = centers[:, None] * spacing + ARC_LENGTH * (along - 0.5)
    angle = arc_place / cycle_radius
    radial = cycle_radius + LAYER_THICKNESS * across
    return jnp.stack([radial * jnp.cos(angle), radial * jnp.sin(angle), AXIAL_DEPTH * height], axis=1)


def draw_control_coords(key, part):
    window, spacing, cycle_radius = cycle_shape()
    positions = cycle_positions(key).astype(jnp.float32)
    along = jax.random.uniform(jax.random.fold_in(key, 707), (NCB, BLOCK), jnp.float32)
    height = jax.random.uniform(jax.random.fold_in(key, 808), (NCB, BLOCK), jnp.float32)
    surface = jax.random.uniform(jax.random.fold_in(key, 909), (NCB, BLOCK), jnp.float32)
    shock_share = 0.5
    on_shock = jnp.where(surface < shock_share, 1.0, 0.0)
    arc_place = (positions[:, None] + 0.5) * spacing + ARC_LENGTH * (along - 0.5)
    angle = arc_place / cycle_radius
    radial = cycle_radius + LAYER_THICKNESS * on_shock
    return jnp.stack([radial * jnp.cos(angle), radial * jnp.sin(angle), AXIAL_DEPTH * height], axis=1)


def draw_neighbours(key, part):
    window, spacing, cycle_radius = cycle_shape()
    positions = cycle_positions(key)
    holder = cycle_holder(key)
    reach_most = max(1, window // 2)
    steps_away = jax.random.randint(jax.random.fold_in(key, 111), (NCB, COUPLED), 1, reach_most + 1, dtype=jnp.int32)
    signs_drawn = jax.random.randint(jax.random.fold_in(key, 222), (NCB, COUPLED), 0, 2, dtype=jnp.int32) * 2 - 1
    offsets = steps_away * signs_drawn
    offsets = offsets.at[:, 0].set(1)
    return holder[(positions[:, None] + offsets) % NCB]


def level_of(key, extent, split, low, largest):
    def one(axis_at, parts):
        draws = jax.random.uniform(jax.random.fold_in(jax.random.fold_in(key, 6), axis_at), (parts,), jnp.float32, low / len(split), largest / len(split))
        return jnp.repeat(jnp.exp(draws), extent[axis_at] // parts).reshape((-1,) + (1,) * (len(extent) - axis_at - 1))

    loudness = one(*split[0])
    for cut in split[1:]:
        loudness = loudness * one(*cut)
    return loudness


def normal_values(rng, shape, spread, bound, cuts=(), kind=jnp.bfloat16):
    gain = level_of(rng, shape, cuts, -0.22, 0.18) if cuts else 1.0
    values = jax.random.normal(rng, shape, jnp.float32) * spread * gain
    return jnp.minimum(jnp.maximum(values, -bound), bound).astype(kind)


def setup_inputs(seed: int = 0, part: int = 0) -> dict:
    key_list = jax.random.split(jax.random.key(seed), 7)
    part_splits = jax.random.split(jax.random.fold_in(key_list[6], part), 7)
    volume_grad = normal_values(part_splits[0], (NSB, FUNC, BLOCK), (12.0 / (NSB * SUPPORT * BLOCK / NCB) ** 0.5), 0.5, ((0, 16),))
    volume_coords = draw_volume_coords(jax.random.fold_in(jax.random.fold_in(key_list[6], part), 71), part)
    support = draw_support(jax.random.fold_in(jax.random.fold_in(key_list[6], part), 71), part)
    control_coords = draw_control_coords(jax.random.fold_in(jax.random.fold_in(key_list[6], part), 71), part)
    neighbours = draw_neighbours(jax.random.fold_in(jax.random.fold_in(key_list[6], part), 71), part)
    block_inverse = normal_values(part_splits[5], (NCB, BLOCK, BLOCK), 4096 ** -0.5, 0.09375, ((0, 4),), jnp.float32)
    return dict(volume_grad=volume_grad, volume_coords=volume_coords, support=support, control_coords=control_coords, neighbours=neighbours, block_inverse=block_inverse)


RADIUS = 1.2

def wendland(points, centers):
    diff = points[..., :, :, None] - centers[..., :, None, :]
    dist = jnp.sqrt(lax.optimization_barrier(jnp.sum(diff * diff, axis=-3)))
    ratio = dist / RADIUS
    inside = jnp.maximum(1.0 - ratio, 0.0)
    return (inside ** 4 * (4.0 * ratio + 1.0)).astype(jnp.bfloat16)

def reference(volume_grad, volume_coords, support, control_coords, neighbours, block_inverse):
    group = 32
    count = volume_grad.shape[0] // group
    grads = volume_grad.reshape(count, group, FUNC, BLOCK)
    coords = volume_coords.reshape(count, group, 3, BLOCK)
    lists = support.reshape(count, group, SUPPORT)

    def step(total, items):
        block_grads, block_coords, block_lists = items
        centers = control_coords[block_lists]
        tiles_phi = wendland(block_coords[:, None], centers)
        tiles = jnp.einsum('gfi,gkij->gkfj', block_grads.astype(jnp.float32), tiles_phi.astype(jnp.float32))
        total = total.at[block_lists.reshape(-1)].add(tiles.reshape(-1, FUNC, BLOCK))
        return (total, None)
    empty = jnp.zeros((NCB, FUNC, BLOCK), jnp.float32)
    control_gradient, _ = lax.scan(step, empty, (grads, coords, lists))
    adjoint = jnp.einsum('cfi,cij->cfj', control_gradient, block_inverse, precision=lax.Precision.HIGHEST)
    pair_phi = wendland(control_coords[neighbours], control_coords[:, None])
    for sweep in range(SWEEPS):
        values = adjoint.astype(jnp.bfloat16)
        near = values[neighbours]
        coupling = jnp.einsum('ckfi,ckij->cfj', near.astype(jnp.float32), pair_phi.astype(jnp.float32))
        adjoint = jnp.einsum('cfi,cij->cfj', control_gradient - coupling, block_inverse, precision=lax.Precision.HIGHEST)
    return (control_gradient, adjoint)
```

```python
import functools

import jax
import jax.numpy as jnp
from jax import lax
from jax.experimental import pallas as pl
from jax.experimental.pallas import tpu as pltpu
from jax.sharding import PartitionSpec as P

SWEEPS = 2
RADIUS = 1.2
C = 4.0**0.2
GEO = 64
CHUNKS = 4
f32, bf16 = jnp.float32, jnp.bfloat16


def params():
    return pltpu.CompilerParams(vmem_limit_bytes=56 << 20)


def phi_of(square):
    root = jnp.maximum(square, 1e-12)
    root = root * lax.rsqrt(root)
    inside = jnp.maximum(C - root, 0.0)
    twice = inside * inside
    return ((twice * twice) * (1.25 * C - inside)).astype(bf16)


def split3(v):
    a = v.astype(bf16).astype(f32)
    b = (v - a).astype(bf16).astype(f32)
    return (a, b, v - a - b)


def coords_of(ref):
    scale = C / RADIUS
    return [ref[:, d, :] * scale for d in range(3)]


def left_rows(ref):
    xyz = coords_of(ref)
    rows = []
    for v in xyz:
        parts = split3(v)
        rows += [parts[a] for a in range(3) for b in range(3)]
    rows += list(split3(sum(v * v for v in xyz)))
    return rows + [jnp.ones_like(xyz[0])] * 3


def right_rows(ref):
    xyz = coords_of(ref)
    rows = []
    for v in xyz:
        parts = split3(v)
        rows += [-2.0 * parts[b] for a in range(3) for b in range(3)]
    rows += [jnp.ones_like(xyz[0])] * 3
    return rows + list(split3(sum(v * v for v in xyz)))


def fill_rows(scratch, rows):
    scratch[...] = jnp.zeros_like(scratch)
    for g, row in enumerate(rows):
        scratch[:, g, :] = row


def shell_features_kernel(coords_ref, out_ref, scratch):
    fill_rows(scratch, left_rows(coords_ref))
    blocks = coords_ref.shape[0]
    head = out_ref.shape[2] - GEO

    def one(s, _):
        lane = lax.broadcasted_iota(jnp.int32, (128, head), 1)
        out_ref[s, :, 0:head] = jnp.where(lane == s, 1.0, 0.0).astype(bf16)
        out_ref[s, :, head:] = scratch[s].T.astype(bf16)
        return 0

    lax.fori_loop(0, blocks, one, 0)


def control_features_kernel(coords_ref, left_ref, right_ref, scratch):
    fill_rows(scratch, left_rows(coords_ref))
    blocks = coords_ref.shape[0]

    def one(c, _):
        left_ref[c] = scratch[c].T.astype(bf16)
        return 0

    lax.fori_loop(0, blocks, one, 0)
    fill_rows(scratch, right_rows(coords_ref))
    right_ref[...] = scratch[...].astype(bf16)


def chunk_kernel(
    chunk, per, tile, side_ref, left_ref, right_ref, grad_ref, support_ref, keep_ref, send_ref,
    rhs, total, d0, d1, p0, p1,
):
    blocks = grad_ref.shape[0]
    head = rhs.shape[1] - GEO
    steps = blocks // tile
    pairs = per // 2
    whole = pairs * steps
    counts = []
    listed = support_ref[...]
    for c in range(per):
        hit = jnp.where(listed == chunk * per + c, 1, 0)
        counts.append(jnp.sum(hit, axis=1, keepdims=True))
    most = counts[0]
    for c in range(1, per):
        most = jnp.maximum(most, counts[c])
    most = jnp.max(most)
    layers = jnp.int32(0)
    for b in range(support_ref.shape[1].bit_length()):
        layers = layers + jnp.where(most >= (1 << b), 1, 0)
    total[...] = jnp.zeros_like(total)
    for j in range(pairs):
        for q in range(2):
            rhs[j, head:, q * 128 : (q + 1) * 128] = right_ref[2 * j + q]

    def distances(t, d):
        j, i = t // steps, t % steps
        left = left_ref[pl.ds(i * tile, tile)].reshape(tile * 128, head + GEO)
        d[...] = jnp.dot(left, rhs[j], preferred_element_type=f32)

    def values(d, p):
        p[...] = phi_of(d[...])

    def products(t, p, weight):
        j, i = t // steps, t % steps
        g = jnp.concatenate([grad_ref[i * tile + q] for q in range(tile)], axis=1)
        total[j] += weight * jnp.dot(g, p[...], preferred_element_type=f32)

    def layer(b, weight):
        for c in range(per):
            bit = jnp.bitwise_and(lax.shift_right_logical(counts[c], b), 1)
            far = jnp.where(jnp.broadcast_to(bit, (blocks, 128)) == 1, 0.0, 16384.0)
            if head > blocks:
                far = jnp.concatenate([far, jnp.zeros((head - blocks, 128), f32)], axis=0)
            rhs[c // 2, 0:head, (c % 2) * 128 : (c % 2 + 1) * 128] = far.astype(bf16)
        p1[...] = jnp.zeros_like(p1)
        distances(0, d0)

        def two(h, _):
            t = 2 * h
            distances(t + 1, d1)
            values(d0, p0)
            products(jnp.maximum(t - 1, 0), p1, weight)
            distances(jnp.minimum(t + 2, whole - 1), d0)
            values(d1, p1)
            products(t, p0, weight)
            return 0

        lax.fori_loop(0, whole // 2, two, 0)
        products(whole - 1, p1, weight)
        return weight * 2.0

    lax.fori_loop(0, layers, layer, jnp.float32(1.0))
    side = side_ref[0]
    half = per // 2
    for c in range(half):
        for q in range(2):
            pass
    quarter = pairs // 2
    for j in range(quarter):
        mine = total[side * quarter + j]
        other = total[(1 - side) * quarter + j]
        for q in range(2):
            keep_ref[2 * j + q] = mine[:, q * 128 : (q + 1) * 128]
            send_ref[2 * j + q] = other[:, q * 128 : (q + 1) * 128]


def pairs_kernel(near_ref, left_ref, right_ref, inverse_ref, phi_ref, parts_ref):
    blocks, coupled = near_ref.shape

    def one(c, _):
        for k in range(coupled):
            d = jnp.dot(left_ref[near_ref[c, k]], right_ref[c], preferred_element_type=f32)
            phi_ref[c, k * 128 : (k + 1) * 128, :] = phi_of(d)
        inv = inverse_ref[c]
        high = inv.astype(bf16)
        parts_ref[c, 0:128, :] = high
        parts_ref[c, 128:256, :] = (inv - high.astype(f32)).astype(bf16)
        return 0

    lax.fori_loop(0, blocks, one, 0, unroll=2)


def solve_kernel(
    count, me_ref, near_ref, *refs
):
    halves = refs[: 2 * count]
    phi_ref, parts_ref, grad_out, adjoint_out, grads, values0, values1 = refs[2 * count :]
    blocks, coupled = near_ref.shape
    own = grad_out.shape[0]
    half = halves[0].shape[0]
    for h in range(2 * count):
        grads[h * half : (h + 1) * half] = halves[h][...]
    first = me_ref[0] * own

    def through(x, c):
        high = x.astype(bf16)
        low = (x - high.astype(f32)).astype(bf16)
        both = jnp.concatenate(
            [jnp.concatenate([high, high], axis=1), jnp.concatenate([low, jnp.zeros_like(low)], axis=1)],
            axis=0,
        )
        out = jnp.dot(both, parts_ref[c], preferred_element_type=f32)
        rows = x.shape[0]
        return out[:rows] + out[rows:]

    def start(c, _):
        values0[c] = through(grads[c], c).astype(bf16)
        return 0

    lax.fori_loop(0, blocks, start, 0, unroll=4)

    def swept(old, c):
        near = jnp.concatenate([old[near_ref[c, k]] for k in range(coupled)], axis=1)
        coupling = jnp.dot(near, phi_ref[c], preferred_element_type=f32)
        return through(grads[c] - coupling, c)

    old, new = values0, values1
    for sweep in range(SWEEPS - 1):
        def one(c, _, old=old, new=new):
            new[c] = swept(old, c).astype(bf16)
            return 0

        lax.fori_loop(0, blocks, one, 0, unroll=4)
        old, new = new, old

    def last(c, _):
        grad_out[c] = grads[first + c]
        adjoint_out[c] = swept(old, first + c)
        return 0

    lax.fori_loop(0, own, last, 0, unroll=4)


def exchange(x, axis, size, step):
    return lax.ppermute(x, axis, [(i, i ^ step) for i in range(size)])


def gather(x, axis, size):
    me = lax.axis_index(axis)
    out = jnp.zeros((size,) + x.shape, x.dtype)
    out = lax.dynamic_update_index_in_dim(out, x, me, 0)
    for step in range(1, size):
        out = lax.dynamic_update_index_in_dim(out, exchange(x, axis, size, step), me ^ step, 0)
    return out.reshape((size * x.shape[0],) + x.shape[1:])


def add_over(x, axis, size):
    step = 1
    while step < size:
        x = x + exchange(x, axis, size, step)
        step *= 2
    return x


def local(sizes, volume_grad, volume_coords, support, control_coords, neighbours, block_inverse):
    nodes, fns, subs = sizes["node"], sizes["fn"], sizes["sub"]
    blocks, funcs, width = volume_grad.shape
    side = lax.axis_index("sub").astype(jnp.int32).reshape(1)
    me = lax.axis_index("node").astype(jnp.int32).reshape(1)
    all_coords = gather(control_coords, "node", nodes)
    controls = all_coords.shape[0]
    head = -(-(blocks + GEO) // 128) * 128 - GEO

    left = pl.pallas_call(
        shell_features_kernel,
        out_shape=jax.ShapeDtypeStruct((blocks, width, head + GEO), bf16),
        scratch_shapes=[pltpu.VMEM((blocks, GEO, width), f32)],
        compiler_params=params(),
        name="shell_features",
    )(volume_coords)
    control_left, control_right = pl.pallas_call(
        control_features_kernel,
        out_shape=(
            jax.ShapeDtypeStruct((controls, width, GEO), bf16),
            jax.ShapeDtypeStruct((controls, GEO, width), bf16),
        ),
        scratch_shapes=[pltpu.VMEM((controls, GEO, width), f32)],
        compiler_params=params(),
        name="control_features",
    )(all_coords)

    all_near = gather(neighbours, "node", nodes)
    all_inverse = gather(block_inverse, "node", nodes)

    per = controls // CHUNKS
    half = per // 2
    tile = 4
    vmem = pl.BlockSpec(memory_space=pltpu.VMEM)
    smem = pl.BlockSpec(memory_space=pltpu.SMEM)
    halves = []
    for chunk in range(CHUNKS):
        entries = blocks * per * width * width
        keep, send = pl.pallas_call(
            functools.partial(chunk_kernel, chunk, per, tile),
            out_shape=[jax.ShapeDtypeStruct((half, funcs, width), f32)] * 2,
            in_specs=[smem, vmem, vmem, vmem, vmem],
            out_specs=[vmem, vmem],
            scratch_shapes=[
                pltpu.VMEM((per // 2, head + GEO, 2 * width), bf16),
                pltpu.VMEM((per // 2, funcs, 2 * width), f32),
                pltpu.VMEM((tile * width, 2 * width), f32),
                pltpu.VMEM((tile * width, 2 * width), f32),
                pltpu.VMEM((tile * width, 2 * width), bf16),
                pltpu.VMEM((tile * width, 2 * width), bf16),
            ],
            compiler_params=params(),
            cost_estimate=pl.CostEstimate(
                flops=entries * 400, bytes_accessed=4 << 20, transcendentals=entries
            ),
            name=f"chunk_{chunk}",
        )(side, left, control_right[chunk * per : (chunk + 1) * per], volume_grad, support)
        part = keep + exchange(send, "sub", subs, 1)
        part = add_over(part, "fn", fns)
        part = add_over(part, "node", nodes)
        other = exchange(part, "sub", subs, 1)
        halves.append(jnp.where(side[0] == 0, part, other))
        halves.append(jnp.where(side[0] == 0, other, part))

    coupled = neighbours.shape[1]
    phi, parts = pl.pallas_call(
        pairs_kernel,
        out_shape=[
            jax.ShapeDtypeStruct((controls, coupled * width, width), bf16),
            jax.ShapeDtypeStruct((controls, 2 * width, width), bf16),
        ],
        in_specs=[smem, vmem, vmem, vmem],
        out_specs=[vmem, vmem],
        compiler_params=params(),
        name="pairs",
    )(all_near, control_left, control_right, all_inverse)

    own = control_coords.shape[0]
    return tuple(
        pl.pallas_call(
            functools.partial(solve_kernel, CHUNKS),
            out_shape=[jax.ShapeDtypeStruct((own, funcs, width), f32)] * 2,
            in_specs=[smem, smem] + [vmem] * (2 * CHUNKS + 2),
            out_specs=[vmem, vmem],
            scratch_shapes=[
                pltpu.VMEM((controls, funcs, width), f32),
                pltpu.VMEM((controls, funcs, width), bf16),
                pltpu.VMEM((controls, funcs, width), bf16),
            ],
            compiler_params=params(),
            name="solve",
        )(me, all_near, *halves, phi, parts)
    )


def solution(mesh):
    return jax.shard_map(
        functools.partial(local, dict(mesh.shape)),
        mesh=mesh,
        in_specs=(
            P(("sect", "node", "fn", "sub"), None, None),
            P(("sect", "node", "fn", "sub"), None, None),
            P(("sect", "node", "fn", "sub"), None),
            P(("sect", "node"), None, None),
            P(("sect", "node"), None),
            P(("sect", "node"), None, None),
        ),
        out_specs=(P(("sect", "node"), None, None), P(("sect", "node"), None, None)),
        check_vma=False,
    )
```

```python
import functools
import math

import jax
import jax.numpy as jnp
from jax import lax
from jax.experimental import pallas as pl
from jax.experimental.pallas import tpu as pltpu
from jax.sharding import PartitionSpec as P

SWEEPS = 2
RADIUS = 1.2
SCALE = 4.0 / RADIUS
GEO = 32
TILE = 4
STEPS = 4
f32, bf16 = jnp.float32, jnp.bfloat16
VMEM = pl.BlockSpec(memory_space=pltpu.VMEM)
SMEM = pl.BlockSpec(memory_space=pltpu.SMEM)
ANY = pl.BlockSpec(memory_space=pl.ANY)
HBM = pl.BlockSpec(memory_space=pltpu.HBM)


def call(kernel, name, out, scratch, operands, specs, cost=None):
    size = 0
    for x in [*out, *scratch, *operands]:
        if len(x.shape) < 2:
            continue
        size += math.prod(x.shape[:-1]) * max(x.shape[-1], 128) * jnp.dtype(x.dtype).itemsize
    return pl.pallas_call(
        kernel,
        out_shape=out,
        in_specs=specs,
        out_specs=[VMEM] * len(out),
        scratch_shapes=scratch,
        compiler_params=pltpu.CompilerParams(vmem_limit_bytes=size + (4 << 20)),
        cost_estimate=cost,
        name=name,
    )(*operands)


def shape(dims, kind):
    return jax.ShapeDtypeStruct(dims, kind)


def root_of(square):
    root = jnp.maximum(square, 1e-12)
    return root * lax.rsqrt(root)


def split3(v):
    a = v.astype(bf16).astype(f32)
    b = (v - a).astype(bf16).astype(f32)
    return (a, b, v - a - b)


def pairs_of_parts():
    return [(a, b) for a in range(3) for b in range(3) if a + b < 4]


def left_rows(xyz):
    rows = []
    for v in xyz:
        parts = split3(v)
        rows += [parts[a] for a, b in pairs_of_parts()]
    rows += list(split3(sum(v * v for v in xyz)))
    return rows + [jnp.ones_like(xyz[0])] * 3


def right_rows(xyz):
    rows = []
    for v in xyz:
        parts = split3(v)
        rows += [-2.0 * parts[b] for a, b in pairs_of_parts()]
    rows += [jnp.ones_like(xyz[0])] * 3
    return rows + list(split3(sum(v * v for v in xyz)))


def place(whole, me, own, pieces):
    whole[me] = own[...] * SCALE
    for step, piece in enumerate(pieces, 1):
        whole[me ^ step] = piece[...] * SCALE


def some(whole, first, per):
    own = whole.shape[2]
    spans = []
    at = first
    while at < first + per:
        node, low = at // own, at % own
        high = min(own, low + first + per - at)
        spans.append((node, low, high))
        at += high - low
    return [
        jnp.concatenate([whole[node, d, low:high] for node, low, high in spans], axis=0)
        for d in range(3)
    ]


def fill_rows(scratch, rows):
    for g, row in enumerate(rows):
        scratch[:, g, :] = row
    for g in range(len(rows), scratch.shape[1]):
        scratch[:, g, :] = jnp.zeros_like(rows[0])


def prepare_kernel(
    controls, side_ref, volume_hbm, listed_hbm, grad_hbm, control_hbm, inverse_hbm, near_hbm, *refs
):
    left_ref, counts_ref, grad_ref, control_ref, parcel_ref = refs[:5]
    coords, listed, scratch, tally, inverse, near, sems = refs[5:]
    half = inverse.shape[0]
    mine = pl.ds(side_ref[0] * half, half)
    copies = [
        pltpu.make_async_copy(source, target, sems.at[n])
        for n, (source, target) in enumerate(
            [
                (volume_hbm, coords),
                (listed_hbm, listed),
                (inverse_hbm.at[mine], inverse),
                (near_hbm, near),
                (control_hbm, control_ref),
                (grad_hbm, grad_ref),
            ]
        )
    ]
    for copy in copies:
        copy.start()
    copies[0].wait()
    fill_rows(scratch, left_rows([coords[d] * SCALE for d in range(3)]))
    blocks, width, depth = left_ref.shape
    lane = lax.broadcasted_iota(jnp.int32, (width, depth), 1)

    def one(s, _):
        turned = scratch[s].T
        turned = jnp.concatenate([turned, jnp.zeros((width, depth - GEO), f32)], axis=1)
        left_ref[s] = jnp.where(lane == s + GEO, 1.0, turned).astype(bf16)
        return 0

    lax.fori_loop(0, blocks, one, 0, unroll=8)
    copies[1].wait()
    chosen = listed[...]
    tally[...] = jnp.zeros_like(tally)
    for c in range(controls):
        tally[c : c + 1, 0:blocks] = jnp.sum(
            jnp.where(chosen == c, 1.0, 0.0), axis=0, keepdims=True
        )
    counts_ref[...] = tally[...].T
    copies[2].wait()
    copies[3].wait()
    for q in range(half):
        parcel_ref[q * 128 : (q + 1) * 128] = inverse[q].astype(bf16)
    tail = jnp.concatenate(
        [
            near[...].astype(f32),
            jnp.zeros((near.shape[0], width - near.shape[1]), f32),
        ],
        axis=1,
    )
    tail = jnp.concatenate([tail, jnp.zeros((16 - near.shape[0], width), f32)], axis=0)
    parcel_ref[half * 128 :] = tail.astype(bf16)
    copies[4].wait()
    copies[5].wait()


def chunk_kernel(first, per, copied, waits, nodes, listed, *refs):
    refs = list(refs)

    def take(n):
        taken = refs[:n]
        del refs[:n]
        return taken

    side_ref, me_ref, left_ref, grad_ref, counts_ref = take(5)
    pieces = take(nodes)
    before = take(2 * (copied > 0))
    take(waits)
    keep_ref, send_ref = take(2)
    coords, features, rhs, total, result, d0, d1, p0, p1 = refs
    blocks = grad_ref.shape[0]
    depth = rhs.shape[1]
    steps = blocks // TILE
    pairs = per // 2
    whole = pairs * steps
    size = TILE * 128
    counts = counts_ref[0:blocks, first : first + per].astype(jnp.int32)
    most = jnp.max(counts)
    layers = jnp.int32(0)
    for b in range(listed.bit_length()):
        layers = layers + jnp.where(most >= (1 << b), 1, 0)
    result[...] = jnp.zeros_like(result)
    place(coords, me_ref[0], pieces[0], pieces[1:])
    fill_rows(features, right_rows(some(coords, first, per)))
    rhs[...] = jnp.zeros_like(rhs)
    for c in range(per):
        rhs[c // 2, 0:GEO, (c % 2) * 128 : (c % 2 + 1) * 128] = features[c].astype(bf16)

    def distances(t, d):
        j, i = t // steps, t % steps
        left = left_ref[pl.ds(i * TILE, TILE)].reshape(size, depth)
        d[...] = jnp.dot(left, rhs[j], preferred_element_type=f32)

    def values(d, p):
        root = root_of(d[...])
        inside = jnp.maximum(4.0 - root, 0.0)
        twice = inside * inside
        p[0:size] = (twice * twice).astype(bf16)
        p[size:] = root.astype(bf16)

    def products(t, p):
        j, i = t // steps, t % steps
        g = jnp.concatenate([grad_ref[i * TILE + q] for q in range(TILE)], axis=1)
        even, odd = p[0:size], p[0:size] * p[size:]
        total[j] += (
            jnp.dot(g, even, preferred_element_type=f32)
            + jnp.dot(g, odd, preferred_element_type=f32)
        )

    def layer(b, weight):
        for c in range(per):
            bit = jnp.bitwise_and(lax.shift_right_logical(counts[:, c : c + 1], b), 1)
            far = jnp.where(jnp.broadcast_to(bit, (blocks, 128)) == 1, 0.0, 65536.0)
            rhs[c // 2, GEO : GEO + blocks, (c % 2) * 128 : (c % 2 + 1) * 128] = far.astype(bf16)
        total[...] = jnp.zeros_like(total)
        p1[...] = jnp.zeros_like(p1)
        distances(0, d0)

        def turn(h, _):
            for u in range(STEPS):
                t = STEPS * h + u
                d, p = (d0, p0) if u % 2 == 0 else (d1, p1)
                later, done = (d1, p1) if u % 2 == 0 else (d0, p0)
                values(d, p)
                products(jnp.maximum(t - 1, 0), done)
                distances(jnp.minimum(t + 1, whole - 1), later)
            return 0

        lax.fori_loop(0, whole // STEPS, turn, 0)
        products(whole - 1, p1)
        result[...] += weight * total[...]
        return weight * 2.0

    lax.fori_loop(0, layers, layer, jnp.float32(1.0 / 256.0))
    side = side_ref[0]
    if before:
        keep_ref[0:copied] = before[0][...]
        send_ref[0:copied] = before[1][...]
    half = pairs // 2
    for j in range(half):
        mine = result[side * half + j]
        other = result[(1 - side) * half + j]
        for q in range(2):
            keep_ref[copied + 2 * j + q] = mine[:, q * 128 : (q + 1) * 128]
            send_ref[copied + 2 * j + q] = other[:, q * 128 : (q + 1) * 128]


def features_kernel(nodes, waits, *refs):
    side_ref, me_ref, inverse_ref = refs[:3]
    pieces = refs[3 : 3 + nodes]
    parcels = refs[3 + nodes : 3 + nodes + 2 * (nodes - 1)]
    left_ref, right_ref, high_ref, low_ref, coords, features = refs[-6:]
    own = inverse_ref.shape[0]
    half = own // 2
    side, me = side_ref[0], me_ref[0]
    for c in range(own):
        inv = inverse_ref[c]
        high = inv.astype(bf16)
        at = (c % 2) * 128
        high_ref[me * half + c // 2, :, at : at + 128] = high
        low_ref[c // 2, :, at : at + 128] = (inv - high.astype(f32)).astype(bf16)
    for step in range(1, nodes):
        for whose in range(2):
            parcel = parcels[whose * (nodes - 1) + step - 1]
            core = (1 - 2 * whose) * side + whose
            for c in range(half):
                pair = (me ^ step) * half + core * (half // 2) + c // 2
                at = (c % 2) * 128
                high_ref[pair, :, at : at + 128] = parcel[c * 128 : (c + 1) * 128]

    place(coords, me, pieces[0], pieces[1:])
    blocks = left_ref.shape[0]
    xyz = some(coords, 0, blocks)
    fill_rows(features, right_rows(xyz))
    right_ref[...] = features[...].astype(bf16)
    fill_rows(features, left_rows(xyz))

    def turn_left(c, _):
        left_ref[c] = features[c].T.astype(bf16)
        return 0

    lax.fori_loop(0, blocks, turn_left, 0, unroll=8)


def pairs_kernel(near_ref, left_ref, right_ref, *refs):
    phi_ref, d0, d1 = refs[-3:]
    blocks = right_ref.shape[0]
    _, coupled, own = near_ref.shape

    def distances(c, d):
        points = [left_ref[near_ref[c // own, k, c % own]] for k in range(coupled)]
        d[...] = jnp.dot(jnp.concatenate(points, axis=0), right_ref[c], preferred_element_type=f32)

    def values(pair, q, d):
        root = root_of(d[...])
        inside = jnp.maximum(1.0 - 0.25 * root, 0.0)
        twice = inside * inside
        phi_ref[pair, :, q * 128 : (q + 1) * 128] = ((twice * twice) * (1.0 + root)).astype(bf16)

    distances(0, d0)

    def turn(h, _):
        for u in range(STEPS):
            c = STEPS * h + u
            values(2 * h + u // 2, u % 2, d0 if u % 2 == 0 else d1)
            distances(jnp.minimum(c + 1, blocks - 1), d1 if u % 2 == 0 else d0)
        return 0

    lax.fori_loop(0, blocks // STEPS, turn, 0)


def add_kernel(x_ref, y_ref, *refs):
    refs[-1][...] = x_ref[...] + y_ref[...]


def solve_kernel(chains, *refs):
    side_ref, me_ref, near_ref = refs[:3]
    halves = refs[3 : 3 + 2 * len(chains)]
    phi_ref, high_ref, low_ref, grad_out, adjoint_out, grads, values0, values1 = refs[
        3 + 2 * len(chains) :
    ]
    pairs = high_ref.shape[0]
    _, coupled, own = near_ref.shape
    side = side_ref[0]
    for n, groups in enumerate(chains):
        at = 0
        for first, per in groups:
            half = per // 2
            grads[pl.ds(first + side * half, half)] = halves[2 * n][at : at + half]
            grads[pl.ds(first + (1 - side) * half, half)] = halves[2 * n + 1][at : at + half]
            at += half

    def through(two, weights, exact):
        rows = []
        for x in two:
            high = x.astype(bf16)
            low = (x - high.astype(f32)).astype(bf16)
            rows.append(jnp.concatenate([high, high], axis=1) if exact else high)
            rows.append(jnp.concatenate([low, jnp.zeros_like(low)], axis=1) if exact else low)
        out = jnp.dot(jnp.concatenate(rows, axis=0), weights, preferred_element_type=f32)
        n = two[0].shape[0]
        return [
            out[2 * q * n : (2 * q + 1) * n, q * 128 : (q + 1) * 128]
            + out[(2 * q + 1) * n : (2 * q + 2) * n, q * 128 : (q + 1) * 128]
            for q in range(2)
        ]

    def start(pair, _):
        done = through([grads[2 * pair], grads[2 * pair + 1]], high_ref[pair], False)
        for q in range(2):
            values0[2 * pair + q] = done[q].astype(bf16)
        return 0

    lax.fori_loop(0, pairs, start, 0, unroll=8)

    def rest(old, pair):
        near = []
        for q in range(2):
            c = 2 * pair + q
            near.append(
                jnp.concatenate(
                    [old[near_ref[c // own, k, c % own]] for k in range(coupled)], axis=1
                )
            )
        n = near[0].shape[0]
        coupling = jnp.dot(
            jnp.concatenate(near, axis=0), phi_ref[pair], preferred_element_type=f32
        )
        return [
            grads[2 * pair + q] - coupling[q * n : (q + 1) * n, q * 128 : (q + 1) * 128]
            for q in range(2)
        ]

    old, new = values0, values1
    for sweep in range(SWEEPS - 1):
        def one(pair, _, old=old, new=new):
            done = through(rest(old, pair), high_ref[pair], False)
            for q in range(2):
                new[2 * pair + q] = done[q].astype(bf16)
            return 0

        lax.fori_loop(0, pairs, one, 0, unroll=8)
        old, new = new, old

    first = me_ref[0] * (own // 2)
    for pair in range(own // 2):
        weights = jnp.concatenate([high_ref[first + pair], low_ref[pair]], axis=0)
        done = through(rest(old, first + pair), weights, True)
        for q in range(2):
            grad_out[2 * pair + q] = grads[2 * (first + pair) + q]
            adjoint_out[2 * pair + q] = done[q]


def exchange(x, axis, size, step):
    return lax.ppermute(x, axis, [(i, i ^ step) for i in range(size)])


def doubling(size):
    return [1 << b for b in range(size.bit_length() - 1)]


def local(sizes, volume_grad, volume_coords, support, control_coords, neighbours, block_inverse):
    nodes, fns, subs = sizes["node"], sizes["fn"], sizes["sub"]
    blocks, funcs, width = volume_grad.shape
    own, coupled = neighbours.shape
    controls = own * nodes
    depth = -(-(blocks + GEO) // 128) * 128
    side = lax.axis_index("sub").astype(jnp.int32).reshape(1)
    me = lax.axis_index("node").astype(jnp.int32).reshape(1)

    coords = control_coords.transpose(1, 0, 2)
    pieces = [exchange(coords, "node", nodes, step) for step in range(1, nodes)]
    left, counts, grads, own_coords, parcel = call(
        functools.partial(prepare_kernel, controls),
        "prepare",
        [
            shape((blocks, width, depth), bf16),
            shape((width, width), f32),
            shape(volume_grad.shape, volume_grad.dtype),
            shape(coords.shape, f32),
            shape((own // 2 * width + 16, width), bf16),
        ],
        [
            pltpu.VMEM((3, blocks, width), f32),
            pltpu.VMEM(support.T.shape, jnp.int32),
            pltpu.VMEM((blocks, GEO, width), f32),
            pltpu.VMEM((width, width), f32),
            pltpu.VMEM((own // 2, width, width), f32),
            pltpu.VMEM((coupled, own), jnp.int32),
            pltpu.SemaphoreType.DMA((6,)),
        ],
        [
            side,
            volume_coords.transpose(1, 0, 2),
            support.T,
            volume_grad,
            coords,
            block_inverse,
            neighbours.T,
        ],
        [SMEM] + [HBM] * 6,
    )
    pieces = [own_coords] + pieces
    parcels = [exchange(parcel, "node", nodes, step) for step in range(1, nodes)]

    def evaluate(first, per, before, after):
        entries = blocks * per * width * width
        copied = before[0].shape[0] if before else 0
        operands = [side, me, left, grads, counts, *pieces, *before]
        out = [shape((copied + per // 2, funcs, width), f32)] * 2
        return call(
            functools.partial(
                chunk_kernel,
                first,
                per,
                copied,
                len(after),
                nodes,
                support.shape[1],
            ),
            f"evaluate_{first}",
            out,
            [
                pltpu.VMEM((nodes, 3, own, width), f32),
                pltpu.VMEM((per, GEO, width), f32),
                pltpu.VMEM((per // 2, depth, 2 * width), bf16),
                pltpu.VMEM((per // 2, funcs, 2 * width), f32),
                pltpu.VMEM((per // 2, funcs, 2 * width), f32),
                pltpu.VMEM((TILE * width, 2 * width), f32),
                pltpu.VMEM((TILE * width, 2 * width), f32),
                pltpu.VMEM((2 * TILE * width, 2 * width), bf16),
                pltpu.VMEM((2 * TILE * width, 2 * width), bf16),
            ],
            operands + after,
            [SMEM, SMEM] + [VMEM] * (len(operands) - 2) + [ANY] * len(after),
            pl.CostEstimate(flops=entries * 400, bytes_accessed=4 << 20, transcendentals=entries),
        )

    def add(x, y, after):
        return call(
            add_kernel,
            "add",
            [shape(x.shape, x.dtype)],
            [],
            [x, y, *after],
            [VMEM, VMEM] + [ANY] * len(after),
        )[0]

    eighth = controls // 8
    groups = [(0, 4 * eighth)] + [((4 + n) * eighth, eighth) for n in range(4)]
    chains = [groups[:1], groups[1:3], groups[3:]]

    def over_node(x):
        for step in doubling(nodes):
            x = add(x, exchange(x, "node", nodes, step), [])
        return x

    def over_fn(x):
        for step in doubling(fns):
            x = add(x, exchange(x, "fn", fns, step), [])
        return x

    keep, send = evaluate(*groups[0], [], [])
    a0 = add(keep, exchange(send, "sub", subs, 1), [])
    one = evaluate(*groups[1], [], [send])
    a1 = over_fn(a0)
    theirs = [exchange(piece, "sub", subs, 1) for piece in parcels]
    two = evaluate(*groups[2], list(one), [a0])
    steps = doubling(nodes)
    a2 = a1
    for step in steps[: len(steps) // 2]:
        a2 = add(a2, exchange(a2, "node", nodes, step), [])
    b0 = add(two[0], exchange(two[1], "sub", subs, 1), [])
    three = evaluate(*groups[3], [], [a1, two[1]])
    a3 = a2
    for step in steps[len(steps) // 2 :]:
        a3 = add(a3, exchange(a3, "node", nodes, step), [])
    b1 = over_fn(b0)
    four = evaluate(*groups[4], list(three), [a2, b0])
    a4 = exchange(a3, "sub", subs, 1)
    b2 = over_node(b1)
    b3 = exchange(b2, "sub", subs, 1)
    c0 = add(four[0], exchange(four[1], "sub", subs, 1), [])

    rows = own // 2 * width
    near = jnp.zeros((nodes, coupled, own), jnp.int32)
    near = lax.dynamic_update_index_in_dim(near, neighbours.T, me[0], 0)
    for step in range(1, nodes):
        told = parcels[step - 1][rows : rows + coupled, :own].astype(jnp.int32)
        near = lax.dynamic_update_index_in_dim(near, told, me[0] ^ step, 0)
    operands = [side, me, block_inverse, *pieces, *parcels, *theirs]
    control_left, control_right, high, low = call(
        functools.partial(features_kernel, nodes, 1),
        "control_features",
        [
            shape((controls, width, GEO), bf16),
            shape((controls, GEO, width), bf16),
            shape((controls // 2, width, 2 * width), bf16),
            shape((own // 2, width, 2 * width), bf16),
        ],
        [
            pltpu.VMEM((nodes, 3, own, width), f32),
            pltpu.VMEM((controls, GEO, width), f32),
        ],
        operands + [c0],
        [SMEM, SMEM] + [VMEM] * (len(operands) - 2) + [ANY],
        pl.CostEstimate(flops=10 << 30, bytes_accessed=1 << 20, transcendentals=0),
    )
    c1 = c0
    for step in doubling(fns):
        c1 = add(c1, exchange(c1, "fn", fns, step), [high])
    (phi,) = call(
        pairs_kernel,
        "pairs",
        [shape((controls // 2, coupled * width, 2 * width), bf16)],
        [
            pltpu.VMEM((coupled * width, width), f32),
            pltpu.VMEM((coupled * width, width), f32),
        ],
        [near, control_left, control_right, c1],
        [SMEM, VMEM, VMEM, ANY],
        pl.CostEstimate(flops=20 << 30, bytes_accessed=1 << 20, transcendentals=2 << 20),
    )
    c2 = c1
    for step in doubling(nodes):
        c2 = add(c2, exchange(c2, "node", nodes, step), [phi])
    c3 = exchange(c2, "sub", subs, 1)

    halves = [a3, a4, b2, b3, c2, c3]
    return tuple(
        call(
            functools.partial(solve_kernel, chains),
            "solve",
            [shape((own, funcs, width), f32)] * 2,
            [
                pltpu.VMEM((controls, funcs, width), f32),
                pltpu.VMEM((controls, funcs, width), bf16),
                pltpu.VMEM((controls, funcs, width), bf16),
            ],
            [side, me, near, *halves, phi, high, low],
            [SMEM, SMEM, SMEM] + [VMEM] * (len(halves) + 3),
        )
    )


def solution(mesh):
    return jax.shard_map(
        functools.partial(local, dict(mesh.shape)),
        mesh=mesh,
        in_specs=(
            P(("sect", "node", "fn", "sub"), None, None),
            P(("sect", "node", "fn", "sub"), None, None),
            P(("sect", "node", "fn", "sub"), None),
            P(("sect", "node"), None, None),
            P(("sect", "node"), None),
            P(("sect", "node"), None, None),
        ),
        out_specs=(P(("sect", "node"), None, None), P(("sect", "node"), None, None)),
        check_vma=False,
    )
```

```python
import functools
import math

import jax
import jax.numpy as jnp
from jax import lax
from jax.experimental import pallas as pl
from jax.experimental.pallas import tpu as pltpu
from jax.sharding import PartitionSpec as P

SWEEPS = 2
RADIUS = 1.2
SCALE = 4.0 / RADIUS
GEO = 32
TILE = 4
STEPS = 4
f32, bf16 = jnp.float32, jnp.bfloat16
VMEM = pl.BlockSpec(memory_space=pltpu.VMEM)
SMEM = pl.BlockSpec(memory_space=pltpu.SMEM)
ANY = pl.BlockSpec(memory_space=pl.ANY)
HBM = pl.BlockSpec(memory_space=pltpu.HBM)


def call(kernel, name, out, scratch, operands, specs, cost=None):
    size = 0
    for x in [*out, *scratch, *operands]:
        if len(x.shape) < 2:
            continue
        size += math.prod(x.shape[:-1]) * max(x.shape[-1], 128) * jnp.dtype(x.dtype).itemsize
    return pl.pallas_call(
        kernel,
        out_shape=out,
        in_specs=specs,
        out_specs=[VMEM] * len(out),
        scratch_shapes=scratch,
        compiler_params=pltpu.CompilerParams(vmem_limit_bytes=size + (4 << 20)),
        cost_estimate=cost,
        name=name,
    )(*operands)


def shape(dims, kind):
    return jax.ShapeDtypeStruct(dims, kind)


def root_of(square):
    root = jnp.maximum(square, 1e-12)
    return root * lax.rsqrt(root)


def split3(v):
    a = v.astype(bf16).astype(f32)
    b = (v - a).astype(bf16).astype(f32)
    return (a, b, v - a - b)


def pairs_of_parts():
    return [(a, b) for a in range(3) for b in range(3) if a + b < 4]


def left_rows(xyz):
    rows = []
    for v in xyz:
        parts = split3(v)
        rows += [parts[a] for a, b in pairs_of_parts()]
    rows += list(split3(sum(v * v for v in xyz)))
    return rows + [jnp.ones_like(xyz[0])] * 3


def right_rows(xyz):
    rows = []
    for v in xyz:
        parts = split3(v)
        rows += [-2.0 * parts[b] for a, b in pairs_of_parts()]
    rows += [jnp.ones_like(xyz[0])] * 3
    return rows + list(split3(sum(v * v for v in xyz)))


def told(ref, count):
    rows = ref[ref.shape[0] - 10 * count :].astype(f32)
    part = [rows[n * count : (n + 1) * count] for n in range(10)]
    xyz = [((part[3 * d + 2] + part[3 * d + 1]) + part[3 * d]) * SCALE for d in range(3)]
    return xyz, part[9]


def fill_rows(scratch, rows):
    for g, row in enumerate(rows):
        scratch[:, g, :] = row
    for g in range(len(rows), scratch.shape[1]):
        scratch[:, g, :] = jnp.zeros_like(rows[0])


def prepare_kernel(
    side_ref, volume_hbm, listed_hbm, grad_hbm, control_hbm, inverse_hbm, near_hbm, *refs
):
    left_ref, counts_ref, grad_ref, parcel_ref = refs[:4]
    coords, listed, scratch, tally, inverse, control, near, sems = refs[4:]
    half = inverse.shape[0]
    own = 2 * half
    mine = pl.ds(side_ref[0] * half, half)
    copies = [
        pltpu.make_async_copy(source, target, sems.at[n])
        for n, (source, target) in enumerate(
            [
                (volume_hbm, coords),
                (listed_hbm, listed),
                (inverse_hbm.at[mine], inverse),
                (near_hbm, near),
                (control_hbm, control),
                (grad_hbm, grad_ref),
            ]
        )
    ]
    for copy in copies:
        copy.start()
    copies[0].wait()
    fill_rows(scratch, left_rows([coords[d] * SCALE for d in range(3)]))
    blocks, width, depth = left_ref.shape
    lane = lax.broadcasted_iota(jnp.int32, (width, depth), 1)

    def one(s, _):
        turned = scratch[s].T
        turned = jnp.concatenate([turned, jnp.zeros((width, depth - GEO), f32)], axis=1)
        left_ref[s] = jnp.where(lane == s + GEO, 1.0, turned).astype(bf16)
        return 0

    lax.fori_loop(0, blocks, one, 0, unroll=8)
    copies[1].wait()
    chosen = listed[...]
    nodes = counts_ref.shape[0]
    tally[...] = jnp.zeros_like(tally)
    for c in range(nodes * own):
        tally[c : c + 1, 0:blocks] = jnp.sum(
            jnp.where(chosen == c, 1.0, 0.0), axis=0, keepdims=True
        )
    for n in range(nodes):
        turned = tally[n * own : (n + 1) * own, :].T[0:blocks]
        counts_ref[n] = jnp.concatenate([turned, jnp.zeros((blocks, width - own), f32)], axis=1)
    for copy in copies[2:]:
        copy.wait()
    for q in range(half):
        parcel_ref[q * 128 : (q + 1) * 128] = inverse[q].astype(bf16)
    rows = [part for d in range(3) for part in split3(control[d])]
    numbers = near[...].astype(f32)
    numbers = jnp.concatenate([numbers, jnp.zeros((near.shape[0], width - own), f32)], axis=1)
    rows.append(jnp.concatenate([numbers, jnp.zeros((own - near.shape[0], width), f32)], axis=0))
    parcel_ref[half * 128 :] = jnp.concatenate(rows, axis=0).astype(bf16)


def chunk_kernel(step, listed, *refs):
    side_ref, me_ref, left_ref, grad_ref, counts_ref, parcel_ref = refs[:6]
    keep_ref, send_ref, features, rhs, total, result, d0, d1, p0, p1 = refs[-10:]
    blocks = grad_ref.shape[0]
    per = features.shape[0]
    depth = rhs.shape[1]
    steps = blocks // TILE
    pairs = per // 2
    whole = pairs * steps
    size = TILE * 128
    counts = counts_ref[me_ref[0] ^ step][:, 0:per].astype(jnp.int32)
    most = jnp.max(counts)
    layers = jnp.int32(0)
    for b in range(listed.bit_length()):
        layers = layers + jnp.where(most >= (1 << b), 1, 0)
    result[...] = jnp.zeros_like(result)
    fill_rows(features, right_rows(told(parcel_ref, per)[0]))
    rhs[...] = jnp.zeros_like(rhs)
    for c in range(per):
        rhs[c // 2, 0:GEO, (c % 2) * 128 : (c % 2 + 1) * 128] = features[c].astype(bf16)

    def distances(t, d):
        j, i = t // steps, t % steps
        left = left_ref[pl.ds(i * TILE, TILE)].reshape(size, depth)
        d[...] = jnp.dot(left, rhs[j], preferred_element_type=f32)

    def values(d, p):
        root = root_of(d[...])
        inside = jnp.maximum(4.0 - root, 0.0)
        twice = inside * inside
        p[0:size] = (twice * twice).astype(bf16)
        p[size:] = root.astype(bf16)

    def products(t, p):
        j, i = t // steps, t % steps
        g = jnp.concatenate([grad_ref[i * TILE + q] for q in range(TILE)], axis=1)
        even, odd = p[0:size], p[0:size] * p[size:]
        total[j] += (
            jnp.dot(g, even, preferred_element_type=f32)
            + jnp.dot(g, odd, preferred_element_type=f32)
        )

    def layer(b, weight):
        for c in range(per):
            bit = jnp.bitwise_and(lax.shift_right_logical(counts[:, c : c + 1], b), 1)
            far = jnp.where(jnp.broadcast_to(bit, (blocks, 128)) == 1, 0.0, 65536.0)
            rhs[c // 2, GEO : GEO + blocks, (c % 2) * 128 : (c % 2 + 1) * 128] = far.astype(bf16)
        total[...] = jnp.zeros_like(total)
        p1[...] = jnp.zeros_like(p1)
        distances(0, d0)

        def turn(h, _):
            for u in range(STEPS):
                t = STEPS * h + u
                d, p = (d0, p0) if u % 2 == 0 else (d1, p1)
                later, done = (d1, p1) if u % 2 == 0 else (d0, p0)
                values(d, p)
                products(jnp.maximum(t - 1, 0), done)
                distances(jnp.minimum(t + 1, whole - 1), later)
            return 0

        lax.fori_loop(0, whole // STEPS, turn, 0)
        products(whole - 1, p1)
        result[...] += weight * total[...]
        return weight * 2.0

    lax.fori_loop(0, layers, layer, jnp.float32(1.0 / 256.0))
    side = side_ref[0]
    half = pairs // 2
    for j in range(half):
        mine = result[side * half + j]
        other = result[(1 - side) * half + j]
        for q in range(2):
            keep_ref[2 * j + q] = mine[:, q * 128 : (q + 1) * 128]
            send_ref[2 * j + q] = other[:, q * 128 : (q + 1) * 128]


def features_kernel(nodes, side_ref, me_ref, inverse_hbm, *refs):
    parcels = refs[:nodes]
    others = refs[nodes : 2 * nodes - 1]
    left_ref, right_ref, high_ref, low_ref, near_ref, coords, features, inverse, sem = refs[-9:]
    copy = pltpu.make_async_copy(inverse_hbm, inverse, sem.at[0])
    copy.start()
    own = inverse.shape[0]
    half = own // 2
    side, me = side_ref[0], me_ref[0]
    for step in range(nodes):
        xyz, numbers = told(parcels[step], own)
        for d in range(3):
            coords[d, me ^ step] = xyz[d]
        near_ref[me ^ step] = numbers.astype(jnp.int32)
    for step in range(1, nodes):
        for core, parcel in ((side, parcels[step]), (1 - side, others[step - 1])):
            for c in range(half):
                pair = (me ^ step) * half + core * (half // 2) + c // 2
                at = (c % 2) * 128
                high_ref[pair, :, at : at + 128] = parcel[c * 128 : (c + 1) * 128]
    blocks = left_ref.shape[0]
    xyz = [coords[d].reshape(blocks, 128) for d in range(3)]
    fill_rows(features, right_rows(xyz))
    right_ref[...] = features[...].astype(bf16)
    fill_rows(features, left_rows(xyz))

    def turn_left(c, _):
        left_ref[c] = features[c].T.astype(bf16)
        return 0

    lax.fori_loop(0, blocks, turn_left, 0, unroll=8)
    copy.wait()
    for c in range(own):
        inv = inverse[c]
        high = inv.astype(bf16)
        at = (c % 2) * 128
        high_ref[me * half + c // 2, :, at : at + 128] = high
        low_ref[c // 2, :, at : at + 128] = (inv - high.astype(f32)).astype(bf16)


def pairs_kernel(near_ref, left_ref, right_ref, *refs):
    phi_ref, d0, d1 = refs[-3:]
    blocks = right_ref.shape[0]
    own = near_ref.shape[1]
    coupled = phi_ref.shape[1] // 128

    def distances(c, d):
        points = [left_ref[near_ref[c // own, k, c % own]] for k in range(coupled)]
        d[...] = jnp.dot(jnp.concatenate(points, axis=0), right_ref[c], preferred_element_type=f32)

    def values(pair, q, d):
        root = root_of(d[...])
        inside = jnp.maximum(1.0 - 0.25 * root, 0.0)
        twice = inside * inside
        phi_ref[pair, :, q * 128 : (q + 1) * 128] = ((twice * twice) * (1.0 + root)).astype(bf16)

    distances(0, d0)

    def turn(h, _):
        for u in range(STEPS):
            c = STEPS * h + u
            values(2 * h + u // 2, u % 2, d0 if u % 2 == 0 else d1)
            distances(jnp.minimum(c + 1, blocks - 1), d1 if u % 2 == 0 else d0)
        return 0

    lax.fori_loop(0, blocks // STEPS, turn, 0)


def add_kernel(x_ref, y_ref, *refs):
    refs[-1][...] = x_ref[...] + y_ref[...]


def finish_kernel(x_ref, y_ref, *refs):
    both = x_ref[...] + y_ref[...]
    refs[-2][...] = both
    refs[-1][...] = both.astype(bf16)


def solve_kernel(nodes, side_ref, me_ref, near_ref, *refs):
    mine, theirs = refs[:nodes], refs[nodes : 2 * nodes]
    phi_ref, high_ref, low_ref, grad_out, adjoint_out, grads, values0, values1 = refs[2 * nodes :]
    pairs = high_ref.shape[0]
    own = near_ref.shape[1]
    coupled = phi_ref.shape[1] // 128
    side, me = side_ref[0], me_ref[0]
    half = own // 2
    for step in range(nodes):
        at = (me ^ step) * own
        grads[pl.ds(at + side * half, half)] = mine[step][...].astype(f32)
        grads[pl.ds(at + (1 - side) * half, half)] = theirs[step][...].astype(f32)

    def through(two, weights, exact):
        rows = []
        for x in two:
            high = x.astype(bf16)
            low = (x - high.astype(f32)).astype(bf16)
            rows.append(jnp.concatenate([high, high], axis=1) if exact else high)
            rows.append(jnp.concatenate([low, jnp.zeros_like(low)], axis=1) if exact else low)
        out = jnp.dot(jnp.concatenate(rows, axis=0), weights, preferred_element_type=f32)
        n = two[0].shape[0]
        return [
            out[2 * q * n : (2 * q + 1) * n, q * 128 : (q + 1) * 128]
            + out[(2 * q + 1) * n : (2 * q + 2) * n, q * 128 : (q + 1) * 128]
            for q in range(2)
        ]

    def start(pair, _):
        done = through([grads[2 * pair], grads[2 * pair + 1]], high_ref[pair], False)
        for q in range(2):
            values0[2 * pair + q] = done[q].astype(bf16)
        return 0

    lax.fori_loop(0, pairs, start, 0, unroll=8)

    def rest(old, pair):
        near = []
        for q in range(2):
            c = 2 * pair + q
            near.append(
                jnp.concatenate(
                    [old[near_ref[c // own, k, c % own]] for k in range(coupled)], axis=1
                )
            )
        n = near[0].shape[0]
        coupling = jnp.dot(
            jnp.concatenate(near, axis=0), phi_ref[pair], preferred_element_type=f32
        )
        return [
            grads[2 * pair + q] - coupling[q * n : (q + 1) * n, q * 128 : (q + 1) * 128]
            for q in range(2)
        ]

    old, new = values0, values1
    for sweep in range(SWEEPS - 1):
        def one(pair, _, old=old, new=new):
            done = through(rest(old, pair), high_ref[pair], False)
            for q in range(2):
                new[2 * pair + q] = done[q].astype(bf16)
            return 0

        lax.fori_loop(0, pairs, one, 0, unroll=8)
        old, new = new, old

    first = me * half
    for pair in range(own // 2):
        weights = jnp.concatenate([high_ref[first + pair], low_ref[pair]], axis=0)
        done = through(rest(old, first + pair), weights, True)
        for q in range(2):
            grad_out[2 * pair + q] = grads[2 * (first + pair) + q]
            adjoint_out[2 * pair + q] = done[q]


def exchange(x, axis, size, step):
    return lax.ppermute(x, axis, [(i, i ^ step) for i in range(size)])


def doubling(size):
    return [1 << b for b in range(size.bit_length() - 1)]


def local(sizes, volume_grad, volume_coords, support, control_coords, neighbours, block_inverse):
    nodes, fns, subs = sizes["node"], sizes["fn"], sizes["sub"]
    blocks, funcs, width = volume_grad.shape
    own, coupled = neighbours.shape
    controls = own * nodes
    depth = -(-(blocks + GEO) // 128) * 128
    side = lax.axis_index("sub").astype(jnp.int32).reshape(1)
    me = lax.axis_index("node").astype(jnp.int32).reshape(1)

    def hbm(x):
        return pltpu.with_memory_space_constraint(x, pltpu.HBM)

    operands = [
        hbm(x)
        for x in (
            volume_coords.transpose(1, 0, 2),
            support.T,
            volume_grad,
            control_coords.transpose(1, 0, 2),
            block_inverse,
            neighbours.T,
        )
    ]
    half = own // 2
    left, counts, grads, parcel = call(
        prepare_kernel,
        "prepare",
        [
            shape((blocks, width, depth), bf16),
            shape((nodes, blocks, width), f32),
            shape(volume_grad.shape, volume_grad.dtype),
            shape((half * width + 10 * own, width), bf16),
        ],
        [
            pltpu.VMEM((3, blocks, width), f32),
            pltpu.VMEM(support.T.shape, jnp.int32),
            pltpu.VMEM((blocks, GEO, width), f32),
            pltpu.VMEM((controls, width), f32),
            pltpu.VMEM((half, width, width), f32),
            pltpu.VMEM((3, own, width), f32),
            pltpu.VMEM((coupled, own), jnp.int32),
            pltpu.SemaphoreType.DMA((6,)),
        ],
        [side, *operands],
        [SMEM] + [HBM] * 6,
    )
    parcels = [parcel] + [exchange(parcel, "node", nodes, step) for step in range(1, nodes)]

    def evaluate(step, after):
        entries = blocks * own * width * width
        operands = [side, me, left, grads, counts, parcels[step]]
        return call(
            functools.partial(chunk_kernel, step, support.shape[1]),
            f"evaluate_{step}",
            [shape((half, funcs, width), f32)] * 2,
            [
                pltpu.VMEM((own, GEO, width), f32),
                pltpu.VMEM((half, depth, 2 * width), bf16),
                pltpu.VMEM((half, funcs, 2 * width), f32),
                pltpu.VMEM((half, funcs, 2 * width), f32),
                pltpu.VMEM((TILE * width, 2 * width), f32),
                pltpu.VMEM((TILE * width, 2 * width), f32),
                pltpu.VMEM((2 * TILE * width, 2 * width), bf16),
                pltpu.VMEM((2 * TILE * width, 2 * width), bf16),
            ],
            operands + after,
            [SMEM, SMEM] + [VMEM] * 4 + [ANY] * len(after),
            pl.CostEstimate(flops=entries * 400, bytes_accessed=4 << 20, transcendentals=entries),
        )

    def add(x, y, after=(), kernel=add_kernel, name="add", kinds=(f32,)):
        done = call(
            kernel,
            name,
            [shape(x.shape, kind) for kind in kinds],
            [],
            [x, y, *after],
            [VMEM, VMEM] + [ANY] * len(after),
        )
        return done if len(done) > 1 else done[0]

    keep, send = evaluate(0, [])
    last = send
    held = None
    arrived = None
    hold = []
    for step in range(nodes - 1, 0, -1):
        mine, other = evaluate(step, [last] + hold)
        if held is None:
            held = add(keep, exchange(send, "sub", subs, 1), [other])
        else:
            held = add(held, arrived, [other])
        part = add(mine, exchange(other, "sub", subs, 1))
        arrived = exchange(part, "node", nodes, step)
        last, hold = other, [part]

    others = [exchange(x, "sub", subs, 1) for x in parcels[1:]]
    operands = [side, me, hbm(block_inverse), *parcels, *others]
    control_left, control_right, high, low, near = call(
        functools.partial(features_kernel, nodes),
        "control_features",
        [
            shape((controls, width, GEO), bf16),
            shape((controls, GEO, width), bf16),
            shape((controls // 2, width, 2 * width), bf16),
            shape((half, width, 2 * width), bf16),
            shape((nodes, own, width), jnp.int32),
        ],
        [
            pltpu.VMEM((3, nodes, own, width), f32),
            pltpu.VMEM((controls, GEO, width), f32),
            pltpu.VMEM((own, width, width), f32),
            pltpu.SemaphoreType.DMA((1,)),
        ],
        operands + hold,
        [SMEM, SMEM, HBM] + [VMEM] * (2 * nodes - 1) + [ANY],
        pl.CostEstimate(flops=10 << 30, bytes_accessed=1 << 20, transcendentals=0),
    )
    held = add(held, arrived, [high])
    (phi,) = call(
        pairs_kernel,
        "pairs",
        [shape((controls // 2, coupled * width, 2 * width), bf16)],
        [
            pltpu.VMEM((coupled * width, width), f32),
            pltpu.VMEM((coupled * width, width), f32),
        ],
        [near, control_left, control_right, held],
        [SMEM, VMEM, VMEM, ANY],
        pl.CostEstimate(flops=20 << 30, bytes_accessed=1 << 20, transcendentals=2 << 20),
    )
    *steps, final = doubling(fns)
    for step in steps:
        held = add(held, exchange(held, "fn", fns, step))
    held, rounded = add(
        held, exchange(held, "fn", fns, final), [phi], finish_kernel, "finish", (f32, bf16)
    )
    mine = [held] + [exchange(rounded, "node", nodes, step) for step in range(1, nodes)]
    theirs = [exchange(x, "sub", subs, 1) for x in mine]
    return tuple(
        call(
            functools.partial(solve_kernel, nodes),
            "solve",
            [shape((own, funcs, width), f32)] * 2,
            [
                pltpu.VMEM((controls, funcs, width), f32),
                pltpu.VMEM((controls, funcs, width), bf16),
                pltpu.VMEM((controls, funcs, width), bf16),
            ],
            [side, me, near, *mine, *theirs, phi, high, low],
            [SMEM, SMEM, SMEM] + [VMEM] * (2 * nodes + 3),
        )
    )


def solution(mesh):
    return jax.shard_map(
        functools.partial(local, dict(mesh.shape)),
        mesh=mesh,
        in_specs=(
            P(("sect", "node", "fn", "sub"), None, None),
            P(("sect", "node", "fn", "sub"), None, None),
            P(("sect", "node", "fn", "sub"), None),
            P(("sect", "node"), None, None),
            P(("sect", "node"), None),
            P(("sect", "node"), None, None),
        ),
        out_specs=(P(("sect", "node"), None, None), P(("sect", "node"), None, None)),
        check_vma=False,
    )
```

```python
import functools
import math

import jax
import jax.numpy as jnp
from jax import lax
from jax.experimental import pallas as pl
from jax.experimental.pallas import tpu as pltpu
from jax.sharding import PartitionSpec as P

SWEEPS = 2
RADIUS = 1.2
C = 4.0**0.2
SCALE = C / RADIUS
GEO = 32
TILE = 4
STEPS = 8
f32, bf16 = jnp.float32, jnp.bfloat16
VMEM = pl.BlockSpec(memory_space=pltpu.VMEM)
SMEM = pl.BlockSpec(memory_space=pltpu.SMEM)
ANY = pl.BlockSpec(memory_space=pl.ANY)
HBM = pl.BlockSpec(memory_space=pltpu.HBM)


def call(kernel, name, out, scratch, operands, specs, cost=None, aliases=None):
    size = 0
    for x in [*out, *scratch, *operands]:
        if len(x.shape) < 2:
            continue
        size += math.prod(x.shape[:-1]) * max(x.shape[-1], 128) * jnp.dtype(x.dtype).itemsize
    return pl.pallas_call(
        kernel,
        out_shape=out,
        in_specs=specs,
        out_specs=[VMEM] * len(out),
        scratch_shapes=scratch,
        compiler_params=pltpu.CompilerParams(vmem_limit_bytes=size + (4 << 20)),
        cost_estimate=cost,
        input_output_aliases=aliases or {},
        name=name,
    )(*operands)


def shape(dims, kind):
    return jax.ShapeDtypeStruct(dims, kind)


def weight_of(square, safe):
    square = jnp.maximum(square, 1e-12) if safe else square
    root = square * lax.rsqrt(square)
    inside = jnp.maximum(C - root, 0.0)
    twice = inside * inside
    return ((twice * twice) * (0.25 * C + root)).astype(bf16)


def split3(v):
    a = v.astype(bf16).astype(f32)
    b = (v - a).astype(bf16).astype(f32)
    return (a, b, v - a - b)


def pairs_of_parts():
    return [(a, b) for a in range(3) for b in range(3) if a + b < 4]


def left_rows(xyz):
    rows = []
    for v in xyz:
        parts = split3(v)
        rows += [parts[a] for a, b in pairs_of_parts()]
    rows += list(split3(sum(v * v for v in xyz)))
    return rows + [jnp.ones_like(xyz[0])] * 3


def right_rows(xyz):
    rows = []
    for v in xyz:
        parts = split3(v)
        rows += [-2.0 * parts[b] for a, b in pairs_of_parts()]
    rows += [jnp.ones_like(xyz[0])] * 3
    return rows + list(split3(sum(v * v for v in xyz)))


def told(ref, count):
    rows = ref[ref.shape[0] - 10 * count :].astype(f32)
    part = [rows[n * count : (n + 1) * count] for n in range(10)]
    xyz = [((part[3 * d + 2] + part[3 * d + 1]) + part[3 * d]) * SCALE for d in range(3)]
    return xyz, part[9]


def fill_rows(scratch, rows):
    for g, row in enumerate(rows):
        scratch[:, g, :] = row
    for g in range(len(rows), scratch.shape[1]):
        scratch[:, g, :] = jnp.zeros_like(rows[0])


def prepare_kernel(
    side_ref, volume_hbm, listed_hbm, grad_hbm, control_hbm, inverse_hbm, near_hbm, *refs
):
    left_ref, counts_ref, grad_ref, parcel_ref = refs[:4]
    coords, listed, scratch, tally, inverse, control, near, sems = refs[4:]
    half = inverse.shape[0]
    own = 2 * half
    mine = pl.ds(side_ref[0] * half, half)
    copies = [
        pltpu.make_async_copy(source, target, sems.at[n])
        for n, (source, target) in enumerate(
            [
                (volume_hbm, coords),
                (listed_hbm, listed),
                (inverse_hbm.at[mine], inverse),
                (near_hbm, near),
                (control_hbm, control),
                (grad_hbm, grad_ref),
            ]
        )
    ]
    for copy in copies:
        copy.start()
    copies[0].wait()
    fill_rows(scratch, left_rows([coords[d] * SCALE for d in range(3)]))
    blocks, width, depth = left_ref.shape
    lane = lax.broadcasted_iota(jnp.int32, (width, depth), 1)

    def one(s, _):
        turned = scratch[s].T
        turned = jnp.concatenate([turned, jnp.zeros((width, depth - GEO), f32)], axis=1)
        left_ref[s] = jnp.where(lane == s + GEO, 1.0, turned).astype(bf16)
        return 0

    lax.fori_loop(0, blocks, one, 0, unroll=8)
    copies[1].wait()
    chosen = listed[...]
    nodes = counts_ref.shape[0]
    tally[...] = jnp.zeros_like(tally)
    for c in range(nodes * own):
        tally[c : c + 1, 0:blocks] = jnp.sum(
            jnp.where(chosen == c, 1.0, 0.0), axis=0, keepdims=True
        )
    for n in range(nodes):
        turned = tally[n * own : (n + 1) * own, :].T[0:blocks]
        counts_ref[n] = jnp.concatenate([turned, jnp.zeros((blocks, width - own), f32)], axis=1)
    for copy in copies[2:]:
        copy.wait()
    for q in range(half):
        parcel_ref[q * 128 : (q + 1) * 128] = inverse[q].astype(bf16)
    rows = [part for d in range(3) for part in split3(control[d])]
    numbers = near[...].astype(f32)
    numbers = jnp.concatenate([numbers, jnp.zeros((near.shape[0], width - own), f32)], axis=1)
    rows.append(jnp.concatenate([numbers, jnp.zeros((own - near.shape[0], width), f32)], axis=0))
    parcel_ref[half * 128 :] = jnp.concatenate(rows, axis=0).astype(bf16)


def chunk_kernel(nodes_done, listed, *refs):
    side_ref, me_ref, left_ref, grad_ref, counts_ref = refs[:5]
    parcels = refs[5 : 5 + len(nodes_done)]
    keep_ref, send_ref, features, rhs, total, result, d0, d1, p0, p1 = refs[-10:]
    blocks = grad_ref.shape[0]
    per = features.shape[0]
    own = per // len(nodes_done)
    depth = rhs.shape[1]
    steps = blocks // TILE
    pairs = per // 2
    whole = pairs * steps
    size = TILE * 128
    counts = [
        counts_ref[me_ref[0] ^ step][:, 0:own].astype(jnp.int32) for step in nodes_done
    ]
    most = counts[0]
    for other in counts[1:]:
        most = jnp.maximum(most, other)
    most = jnp.max(most)
    layers = jnp.int32(0)
    for b in range(listed.bit_length()):
        layers = layers + jnp.where(most >= (1 << b), 1, 0)
    result[...] = jnp.zeros_like(result)
    for n, parcel in enumerate(parcels):
        rows = right_rows(told(parcel, own)[0])
        fill_rows(features.at[n * own : (n + 1) * own], rows)
    rhs[...] = jnp.zeros_like(rhs)
    for c in range(per):
        rhs[c // 2, 0:GEO, (c % 2) * 128 : (c % 2 + 1) * 128] = features[c].astype(bf16)

    def distances(t, d):
        j, i = t // steps, t % steps
        left = left_ref[pl.ds(i * TILE, TILE)].reshape(size, depth)
        d[...] = jnp.dot(left, rhs[j], preferred_element_type=f32)

    def values(d, p, safe):
        p[...] = weight_of(d[...], safe)

    def products(t, p):
        j, i = t // steps, t % steps
        g = jnp.concatenate([grad_ref[i * TILE + q] for q in range(TILE)], axis=1)
        total[j] += jnp.dot(g, p[...], preferred_element_type=f32)

    def layer(safe, turns, b, weight):
        for c in range(per):
            count = counts[c // own][:, c % own : c % own + 1]
            bit = jnp.bitwise_and(lax.shift_right_logical(count, b), 1)
            far = jnp.where(jnp.broadcast_to(bit, (blocks, 128)) == 1, 0.0, 65536.0)
            rhs[c // 2, GEO : GEO + blocks, (c % 2) * 128 : (c % 2 + 1) * 128] = far.astype(bf16)
        total[...] = jnp.zeros_like(total)
        p1[...] = jnp.zeros_like(p1)
        distances(0, d0)

        def turn(h, _):
            for u in range(turns):
                t = turns * h + u
                d, p = (d0, p0) if u % 2 == 0 else (d1, p1)
                later, done = (d1, p1) if u % 2 == 0 else (d0, p0)
                values(d, p, safe)
                distances(jnp.minimum(t + 1, whole - 1), later)
                products(jnp.maximum(t - 1, 0), done)
            return 0

        lax.fori_loop(0, whole // turns, turn, 0)
        products(whole - 1, p1)
        result[...] += weight * total[...]
        return weight * 2.0

    lax.fori_loop(0, layers, functools.partial(layer, False, STEPS), jnp.float32(1.0))
    failed = jnp.max(jnp.where(result[...] != result[...], 1, 0))

    def again(_, carry):
        result[...] = jnp.zeros_like(result)
        lax.fori_loop(0, layers, functools.partial(layer, True, 2), jnp.float32(1.0))
        return carry

    lax.fori_loop(0, failed, again, 0)
    side = side_ref[0]
    half = own // 4
    for n in range(len(nodes_done)):
        for j in range(half):
            mine = result[n * 2 * half + side * half + j]
            other = result[n * 2 * half + (1 - side) * half + j]
            for q in range(2):
                keep_ref[n * 2 * half + 2 * j + q] = mine[:, q * 128 : (q + 1) * 128]
                send_ref[n * 2 * half + 2 * j + q] = other[:, q * 128 : (q + 1) * 128]


def features_kernel(nodes, side_ref, me_ref, inverse_hbm, *refs):
    parcels = refs[:nodes]
    others = refs[nodes : 2 * nodes - 1]
    left_ref, right_ref, high_ref, low_ref, near_ref, coords, features, inverse, sem = refs[-9:]
    copy = pltpu.make_async_copy(inverse_hbm, inverse, sem.at[0])
    copy.start()
    own = inverse.shape[0]
    half = own // 2
    side, me = side_ref[0], me_ref[0]
    for step in range(nodes):
        xyz, numbers = told(parcels[step], own)
        for d in range(3):
            coords[d, me ^ step] = xyz[d]
        near_ref[me ^ step] = numbers.astype(jnp.int32)
    for step in range(1, nodes):
        for core, parcel in ((side, parcels[step]), (1 - side, others[step - 1])):
            for c in range(half):
                pair = (me ^ step) * half + core * (half // 2) + c // 2
                at = (c % 2) * 128
                high_ref[pair, :, at : at + 128] = parcel[c * 128 : (c + 1) * 128]
    blocks = left_ref.shape[0]
    xyz = [coords[d].reshape(blocks, 128) for d in range(3)]
    fill_rows(features, right_rows(xyz))
    right_ref[...] = features[...].astype(bf16)
    fill_rows(features, left_rows(xyz))

    def turn_left(c, _):
        left_ref[c] = features[c].T.astype(bf16)
        return 0

    lax.fori_loop(0, blocks, turn_left, 0, unroll=8)
    copy.wait()
    for c in range(own):
        inv = inverse[c]
        high = inv.astype(bf16)
        at = (c % 2) * 128
        high_ref[me * half + c // 2, :, at : at + 128] = high
        low_ref[c // 2, :, at : at + 128] = (inv - high.astype(f32)).astype(bf16)


def pairs_kernel(low, high, near_ref, left_ref, right_ref, *refs):
    phi_ref, d0, d1 = refs[-3:]
    own = near_ref.shape[1]
    coupled = phi_ref.shape[1] // 128

    def distances(pair, d):
        for q in range(2):
            c = 2 * pair + q
            points = [left_ref[near_ref[c // own, k, c % own]] for k in range(coupled)]
            d[:, q * 128 : (q + 1) * 128] = jnp.dot(
                jnp.concatenate(points, axis=0), right_ref[c], preferred_element_type=f32
            )

    distances(low, d0)

    def turn(h, _):
        for u in range(4):
            pair = low + 4 * h + u
            d, later = (d0, d1) if u % 2 == 0 else (d1, d0)
            phi_ref[pair] = weight_of(d[...], True)
            distances(jnp.minimum(pair + 1, high - 1), later)
        return 0

    lax.fori_loop(0, (high - low) // 4, turn, 0)


def sum_kernel(count, made, *refs):
    terms = [x[...] for x in refs[:count]]
    while len(terms) > 1:
        terms = [sum(terms[n + 1 : n + 2], terms[n]) for n in range(0, len(terms), 2)]
    (total,) = terms
    at = 0
    for out in refs[len(refs) - made :]:
        if at == total.shape[0]:
            at = 0
        n = out.shape[0]
        out[...] = total[at : at + n].astype(out.dtype)
        at += n


def join_kernel(*refs):
    *pieces, _, out = refs
    n = pieces[0].shape[0]
    for at, piece in enumerate(pieces):
        out[at * n : (at + 1) * n] = piece[...]


def solve_kernel(nodes, side_ref, me_ref, near_ref, *refs):
    phi_ref, high_ref, low_ref, grad_out, adjoint_out, grads, sums, values0, values1 = refs[4:]
    pairs = high_ref.shape[0]
    own = near_ref.shape[1]
    coupled = phi_ref.shape[1] // 128
    side, me = side_ref[0], me_ref[0]
    half = own // 2
    for core, (held, joined) in ((side, refs[0:2]), (1 - side, refs[2:4])):
        grads[pl.ds(me * own + core * half, half)] = held[...]
        for step in range(1, nodes):
            piece = joined[(step - 1) * half : step * half].astype(f32)
            grads[pl.ds((me ^ step) * own + core * half, half)] = piece

    def through(two, weights, exact):
        rows = []
        for x in two:
            high = x.astype(bf16)
            low = (x - high.astype(f32)).astype(bf16)
            rows.append(jnp.concatenate([high, high], axis=1) if exact else high)
            rows.append(jnp.concatenate([low, jnp.zeros_like(low)], axis=1) if exact else low)
        out = jnp.dot(jnp.concatenate(rows, axis=0), weights, preferred_element_type=f32)
        n = two[0].shape[0]
        return [
            out[2 * q * n : (2 * q + 1) * n, q * 128 : (q + 1) * 128]
            + out[(2 * q + 1) * n : (2 * q + 2) * n, q * 128 : (q + 1) * 128]
            for q in range(2)
        ]

    def start(pair, _):
        done = through([grads[2 * pair], grads[2 * pair + 1]], high_ref[pair], False)
        for q in range(2):
            values0[2 * pair + q] = done[q].astype(bf16)
        return 0

    lax.fori_loop(0, pairs, start, 0, unroll=min(pairs, 16))

    def rest(old, pair):
        near = []
        for q in range(2):
            c = 2 * pair + q
            near.append(
                jnp.concatenate(
                    [old[near_ref[c // own, k, c % own]] for k in range(coupled)], axis=1
                )
            )
        n = near[0].shape[0]
        coupling = jnp.dot(
            jnp.concatenate(near, axis=0), phi_ref[pair], preferred_element_type=f32
        )
        return [
            grads[2 * pair + q] - coupling[q * n : (q + 1) * n, q * 128 : (q + 1) * 128]
            for q in range(2)
        ]

    old, new = values0, values1
    for sweep in range(SWEEPS - 1):

        def left_over(pair, _, old=old):
            two = rest(old, pair)
            for q in range(2):
                sums[2 * pair + q] = two[q]
            return 0

        def apply(pair, _, new=new):
            done = through([sums[2 * pair], sums[2 * pair + 1]], high_ref[pair], False)
            for q in range(2):
                new[2 * pair + q] = done[q].astype(bf16)
            return 0

        lax.fori_loop(0, pairs, left_over, 0, unroll=min(pairs, 16))
        lax.fori_loop(0, pairs, apply, 0, unroll=min(pairs, 16))
        old, new = new, old

    first = me * half
    last = [rest(old, first + pair) for pair in range(half)]
    for pair in range(half):
        weights = jnp.concatenate([high_ref[first + pair], low_ref[pair]], axis=0)
        done = through(last[pair], weights, True)
        for q in range(2):
            grad_out[2 * pair + q] = grads[2 * (first + pair) + q]
            adjoint_out[2 * pair + q] = done[q]


def exchange(x, axis, size, step):
    return lax.ppermute(x, axis, [(i, i ^ step) for i in range(size)])


def local(sizes, volume_grad, volume_coords, support, control_coords, neighbours, block_inverse):
    nodes, fns, subs = sizes["node"], sizes["fn"], sizes["sub"]
    blocks, funcs, width = volume_grad.shape
    own, coupled = neighbours.shape
    controls = own * nodes
    depth = -(-(blocks + GEO) // 128) * 128
    side = lax.axis_index("sub").astype(jnp.int32).reshape(1)
    me = lax.axis_index("node").astype(jnp.int32).reshape(1)

    def hbm(x):
        return pltpu.with_memory_space_constraint(x, pltpu.HBM)

    operands = [
        hbm(x)
        for x in (
            volume_coords.transpose(1, 0, 2),
            support.T,
            volume_grad,
            control_coords.transpose(1, 0, 2),
            block_inverse,
            neighbours.T,
        )
    ]
    half = own // 2
    left, counts, grads, parcel = call(
        prepare_kernel,
        "prepare",
        [
            shape((blocks, width, depth), bf16),
            shape((nodes, blocks, width), f32),
            shape(volume_grad.shape, volume_grad.dtype),
            shape((half * width + 10 * own, width), bf16),
        ],
        [
            pltpu.VMEM((3, blocks, width), f32),
            pltpu.VMEM(support.T.shape, jnp.int32),
            pltpu.VMEM((blocks, GEO, width), f32),
            pltpu.VMEM((controls, width), f32),
            pltpu.VMEM((half, width, width), f32),
            pltpu.VMEM((3, own, width), f32),
            pltpu.VMEM((coupled, own), jnp.int32),
            pltpu.SemaphoreType.DMA((6,)),
        ],
        [side, *operands],
        [SMEM] + [HBM] * 6,
    )
    parcels = [parcel] + [exchange(parcel, "node", nodes, step) for step in range(1, nodes)]

    def evaluate(nodes_done, after):
        per = own * len(nodes_done)
        entries = blocks * per * width * width
        operands = [side, me, left, grads, counts, *(parcels[step] for step in nodes_done)]
        return call(
            functools.partial(chunk_kernel, nodes_done, support.shape[1]),
            f"evaluate_{nodes_done[0]}",
            [shape((per // 2, funcs, width), f32)] * 2,
            [
                pltpu.VMEM((per, GEO, width), f32),
                pltpu.VMEM((per // 2, depth, 2 * width), bf16),
                pltpu.VMEM((per // 2, funcs, 2 * width), f32),
                pltpu.VMEM((per // 2, funcs, 2 * width), f32),
                pltpu.VMEM((TILE * width, 2 * width), f32),
                pltpu.VMEM((TILE * width, 2 * width), f32),
                pltpu.VMEM((TILE * width, 2 * width), bf16),
                pltpu.VMEM((TILE * width, 2 * width), bf16),
            ],
            operands + after,
            [SMEM, SMEM] + [VMEM] * (len(operands) - 2) + [ANY] * len(after),
            pl.CostEstimate(flops=entries * 400, bytes_accessed=4 << 20, transcendentals=entries),
        )

    def add(terms, after=(), parts=1, kinds=(f32,)):
        dims = (terms[0].shape[0] // parts,) + terms[0].shape[1:]
        done = call(
            functools.partial(sum_kernel, len(terms), parts * len(kinds)),
            "sum",
            [shape(dims, kind) for kind in kinds for _ in range(parts)],
            [],
            [*terms, *after],
            [VMEM] * len(terms) + [ANY] * len(after),
        )
        return done if len(done) > 1 else done[0]

    far = list(range(nodes - 1, 1, -1))
    keep, send = evaluate([0], [])
    kept, sent = evaluate(far, [send])
    held = add([keep, exchange(send, "sub", subs, 1)], [sent])
    parts = add([kept, exchange(sent, "sub", subs, 1)], parts=len(far))
    arrived = [exchange(x, "node", nodes, step) for step, x in zip(far, parts)]
    others = [exchange(x, "sub", subs, 1) for x in parcels[1:]]
    kept, sent = evaluate([1], [*parts, held, *others])
    held = add([held, *arrived], [sent])
    part = add([kept, exchange(sent, "sub", subs, 1)])
    arrived = exchange(part, "node", nodes, 1)

    operands = [side, me, hbm(block_inverse), *parcels, *others]
    control_left, control_right, high, low, near = call(
        functools.partial(features_kernel, nodes),
        "control_features",
        [
            shape((controls, width, GEO), bf16),
            shape((controls, GEO, width), bf16),
            shape((controls // 2, width, 2 * width), bf16),
            shape((half, width, 2 * width), bf16),
            shape((nodes, own, width), jnp.int32),
        ],
        [
            pltpu.VMEM((3, nodes, own, width), f32),
            pltpu.VMEM((controls, GEO, width), f32),
            pltpu.VMEM((own, width, width), f32),
            pltpu.SemaphoreType.DMA((1,)),
        ],
        operands + [part],
        [SMEM, SMEM, HBM] + [VMEM] * (2 * nodes - 1) + [ANY],
        pl.CostEstimate(flops=10 << 30, bytes_accessed=1 << 20, transcendentals=0),
    )
    middle = controls // 4

    def couple(low_pair, high_pair, before, after):
        operands = [near, control_left, control_right, *before]
        return call(
            functools.partial(pairs_kernel, low_pair, high_pair),
            f"pairs_{low_pair}",
            [shape((controls // 2, coupled * width, 2 * width), bf16)],
            [
                pltpu.VMEM((coupled * width, 2 * width), f32),
                pltpu.VMEM((coupled * width, 2 * width), f32),
            ],
            [*operands, *after],
            [SMEM] + [VMEM] * (len(operands) - 1) + [ANY] * len(after),
            pl.CostEstimate(flops=10 << 30, bytes_accessed=1 << 20, transcendentals=1 << 20),
            {3: 0} if before else None,
        )[0]

    held = add([held, arrived], [high])
    phi = couple(0, middle, [], [held])
    terms = [held] + [exchange(held, "fn", fns, turn) for turn in range(1, fns)]
    held, rounded = add(terms, [phi], kinds=(f32, bf16))
    pieces = [exchange(rounded, "node", nodes, step) for step in range(1, nodes)]
    phi = couple(middle, controls // 2, [phi], [rounded])
    joined = call(
        join_kernel,
        "join",
        [shape(((nodes - 1) * half, funcs, width), bf16)],
        [],
        [*pieces, phi],
        [VMEM] * len(pieces) + [ANY],
    )[0]
    mine = [held, joined]
    theirs = [exchange(x, "sub", subs, 1) for x in mine]
    return tuple(
        call(
            functools.partial(solve_kernel, nodes),
            "solve",
            [shape((own, funcs, width), f32)] * 2,
            [
                pltpu.VMEM((controls, funcs, width), f32),
                pltpu.VMEM((controls, funcs, width), f32),
                pltpu.VMEM((controls, funcs, width), bf16),
                pltpu.VMEM((controls, funcs, width), bf16),
            ],
            [side, me, near, *mine, *theirs, phi, high, low],
            [SMEM, SMEM, SMEM] + [VMEM] * 7,
        )
    )


def solution(mesh):
    return jax.shard_map(
        functools.partial(local, dict(mesh.shape)),
        mesh=mesh,
        in_specs=(
            P(("sect", "node", "fn", "sub"), None, None),
            P(("sect", "node", "fn", "sub"), None, None),
            P(("sect", "node", "fn", "sub"), None),
            P(("sect", "node"), None, None),
            P(("sect", "node"), None),
            P(("sect", "node"), None, None),
        ),
        out_specs=(P(("sect", "node"), None, None), P(("sect", "node"), None, None)),
        check_vma=False,
    )
```

```python
import functools
import math

import jax
import jax.numpy as jnp
from jax import lax
from jax.experimental import pallas as pl
from jax.experimental.pallas import tpu as pltpu
from jax.sharding import PartitionSpec as P

SWEEPS = 2
RADIUS = 1.2
C = 4.0**0.2
SCALE = C / RADIUS
GEO = 32
TILE = 4
STEPS = 16
f32, bf16 = jnp.float32, jnp.bfloat16
VMEM = pl.BlockSpec(memory_space=pltpu.VMEM)
SMEM = pl.BlockSpec(memory_space=pltpu.SMEM)
ANY = pl.BlockSpec(memory_space=pl.ANY)
HBM = pl.BlockSpec(memory_space=pltpu.HBM)


def call(kernel, name, out, scratch, operands, specs, cost=None, aliases=None):
    size = 0
    for x in [*out, *scratch, *operands]:
        if len(x.shape) < 2:
            continue
        size += math.prod(x.shape[:-1]) * max(x.shape[-1], 128) * jnp.dtype(x.dtype).itemsize
    return pl.pallas_call(
        kernel,
        out_shape=out,
        in_specs=specs,
        out_specs=[VMEM] * len(out),
        scratch_shapes=scratch,
        compiler_params=pltpu.CompilerParams(vmem_limit_bytes=size + (4 << 20)),
        cost_estimate=cost,
        input_output_aliases=aliases or {},
        name=name,
    )(*operands)


def shape(dims, kind):
    return jax.ShapeDtypeStruct(dims, kind)


def weight_of(square, safe):
    square = jnp.maximum(square, 1e-12) if safe else square
    root = square * lax.rsqrt(square)
    inside = jnp.maximum(C - root, 0.0)
    twice = inside * inside
    return ((twice * twice) * (0.25 * C + root)).astype(bf16)


def split3(v):
    a = v.astype(bf16).astype(f32)
    b = (v - a).astype(bf16).astype(f32)
    return (a, b, v - a - b)


def pairs_of_parts():
    return [(a, b) for a in range(3) for b in range(3) if a + b < 4]


def left_rows(xyz):
    rows = []
    for v in xyz:
        parts = split3(v)
        rows += [parts[a] for a, b in pairs_of_parts()]
    rows += list(split3(sum(v * v for v in xyz)))
    return rows + [jnp.ones_like(xyz[0])] * 3


def right_rows(xyz):
    rows = []
    for v in xyz:
        parts = split3(v)
        rows += [-2.0 * parts[b] for a, b in pairs_of_parts()]
    rows += [jnp.ones_like(xyz[0])] * 3
    return rows + list(split3(sum(v * v for v in xyz)))


def told(ref, count):
    rows = ref[ref.shape[0] - 10 * count :].astype(f32)
    part = [rows[n * count : (n + 1) * count] for n in range(10)]
    xyz = [((part[3 * d + 2] + part[3 * d + 1]) + part[3 * d]) * SCALE for d in range(3)]
    return xyz, part[9]


def fill_rows(scratch, rows, first=0):
    blocks = scratch.shape[0] // GEO
    n = rows[0].shape[0]
    for g in range(GEO):
        row = rows[g] if g < len(rows) else jnp.zeros_like(rows[0])
        scratch[g * blocks + first : g * blocks + first + n] = row


def rows_of(scratch, block):
    return scratch[pl.ds(block, GEO, stride=scratch.shape[0] // GEO), :]


def prepare_kernel(
    side_ref, volume_hbm, listed_hbm, grad_hbm, control_hbm, inverse_hbm, near_hbm, *refs
):
    left_ref, counts_ref, grad_ref, parcel_ref = refs[:4]
    coords, listed, scratch, tally, inverse, control, near, sems = refs[4:]
    half = inverse.shape[0]
    own = 2 * half
    mine = pl.ds(side_ref[0] * half, half)
    copies = [
        pltpu.make_async_copy(source, target, sems.at[n])
        for n, (source, target) in enumerate(
            [
                (volume_hbm, coords),
                (listed_hbm, listed),
                (inverse_hbm.at[mine], inverse),
                (near_hbm, near),
                (control_hbm, control),
                (grad_hbm, grad_ref),
            ]
        )
    ]
    for copy in copies:
        copy.start()
    copies[0].wait()
    fill_rows(scratch, left_rows([coords[d] * SCALE for d in range(3)]))
    blocks, width, depth = left_ref.shape
    lane = lax.broadcasted_iota(jnp.int32, (width, depth), 1)

    def one(s, _):
        turned = rows_of(scratch, s).T
        turned = jnp.concatenate([turned, jnp.zeros((width, depth - GEO), f32)], axis=1)
        left_ref[s] = jnp.where(lane == s + GEO, 1.0, turned).astype(bf16)
        return 0

    lax.fori_loop(0, blocks, one, 0, unroll=8)
    copies[1].wait()
    chosen = listed[...]
    nodes = counts_ref.shape[0]
    tally[...] = jnp.zeros_like(tally)
    for c in range(nodes * own):
        tally[c : c + 1, 0:blocks] = jnp.sum(
            jnp.where(chosen == c, 1.0, 0.0), axis=0, keepdims=True
        )
    for n in range(nodes):
        turned = tally[n * own : (n + 1) * own, :].T[0:blocks]
        counts_ref[n] = jnp.concatenate([turned, jnp.zeros((blocks, width - own), f32)], axis=1)
    for copy in copies[2:]:
        copy.wait()
    for q in range(half):
        parcel_ref[q * 128 : (q + 1) * 128] = inverse[q].astype(bf16)
    rows = [part for d in range(3) for part in split3(control[d])]
    numbers = near[...].astype(f32)
    numbers = jnp.concatenate([numbers, jnp.zeros((near.shape[0], width - own), f32)], axis=1)
    rows.append(jnp.concatenate([numbers, jnp.zeros((own - near.shape[0], width), f32)], axis=0))
    parcel_ref[half * 128 :] = jnp.concatenate(rows, axis=0).astype(bf16)


def chunk_kernel(nodes_done, listed, *refs):
    side_ref, me_ref, left_ref, grad_ref, counts_ref = refs[:5]
    parcels = refs[5 : 5 + len(nodes_done)]
    keep_ref, send_ref, features, rhs, total, result, d0, d1, p0, p1 = refs[-10:]
    blocks = grad_ref.shape[0]
    per = features.shape[0] // GEO
    own = per // len(nodes_done)
    depth = rhs.shape[1]
    steps = blocks // TILE
    pairs = per // 2
    whole = pairs * steps
    size = TILE * 128
    counts = [
        counts_ref[me_ref[0] ^ step][:, 0:own].astype(jnp.int32) for step in nodes_done
    ]
    most = counts[0]
    for other in counts[1:]:
        most = jnp.maximum(most, other)
    most = jnp.max(most)
    layers = jnp.int32(0)
    for b in range(listed.bit_length()):
        layers = layers + jnp.where(most >= (1 << b), 1, 0)
    result[...] = jnp.zeros_like(result)
    for n, parcel in enumerate(parcels):
        fill_rows(features, right_rows(told(parcel, own)[0]), n * own)
    rhs[...] = jnp.zeros_like(rhs)
    for c in range(per):
        rhs[c // 2, 0:GEO, (c % 2) * 128 : (c % 2 + 1) * 128] = rows_of(features, c).astype(
            bf16
        )

    def distances(t, d):
        j, i = t // steps, t % steps
        left = left_ref[pl.ds(i * TILE, TILE)].reshape(size, depth)
        d[...] = jnp.dot(left, rhs[j], preferred_element_type=f32)

    def values(d, p, safe):
        p[...] = weight_of(d[...], safe)

    def products(t, p):
        j, i = t // steps, t % steps
        g = jnp.concatenate([grad_ref[i * TILE + q] for q in range(TILE)], axis=1)
        total[j] += jnp.dot(g, p[...], preferred_element_type=f32)

    def layer(safe, turns, b, weight):
        for c in range(per):
            count = counts[c // own][:, c % own : c % own + 1]
            bit = jnp.bitwise_and(lax.shift_right_logical(count, b), 1)
            far = jnp.where(jnp.broadcast_to(bit, (blocks, 128)) == 1, 0.0, 65536.0)
            rhs[c // 2, GEO : GEO + blocks, (c % 2) * 128 : (c % 2 + 1) * 128] = far.astype(bf16)
        total[...] = jnp.zeros_like(total)
        p1[...] = jnp.zeros_like(p1)
        distances(0, d0)

        def turn(h, _):
            for u in range(turns):
                t = turns * h + u
                d, p = (d0, p0) if u % 2 == 0 else (d1, p1)
                later, done = (d1, p1) if u % 2 == 0 else (d0, p0)
                values(d, p, safe)
                distances(jnp.minimum(t + 1, whole - 1), later)
                products(jnp.maximum(t - 1, 0), done)
            return 0

        lax.fori_loop(0, whole // turns, turn, 0)
        products(whole - 1, p1)
        result[...] += weight * total[...]
        return weight * 2.0

    lax.fori_loop(0, layers, functools.partial(layer, False, STEPS), jnp.float32(1.0))
    failed = jnp.max(jnp.where(result[...] != result[...], 1, 0))

    def again(_, carry):
        result[...] = jnp.zeros_like(result)
        lax.fori_loop(0, layers, functools.partial(layer, True, 2), jnp.float32(1.0))
        return carry

    lax.fori_loop(0, failed, again, 0)
    side = side_ref[0]
    half = own // 4
    for n in range(len(nodes_done)):
        for j in range(half):
            mine = result[n * 2 * half + side * half + j]
            other = result[n * 2 * half + (1 - side) * half + j]
            for q in range(2):
                keep_ref[n * 2 * half + 2 * j + q] = mine[:, q * 128 : (q + 1) * 128]
                send_ref[n * 2 * half + 2 * j + q] = other[:, q * 128 : (q + 1) * 128]


def features_kernel(nodes, side_ref, me_ref, inverse_hbm, *refs):
    parcels = refs[:nodes]
    others = refs[nodes : 2 * nodes - 1]
    left_ref, right_ref, high_ref, low_ref, near_ref = refs[-10:-5]
    coords, features, rows, inverse, sem = refs[-5:]
    copy = pltpu.make_async_copy(inverse_hbm, inverse, sem.at[0])
    copy.start()
    own = inverse.shape[0]
    half = own // 2
    side, me = side_ref[0], me_ref[0]
    for step in range(nodes):
        xyz, numbers = told(parcels[step], own)
        for d in range(3):
            coords[d, me ^ step] = xyz[d]
        near_ref[me ^ step] = numbers.astype(jnp.int32)
    for step in range(1, nodes):
        for core, parcel in ((side, parcels[step]), (1 - side, others[step - 1])):
            for c in range(half):
                pair = (me ^ step) * half + core * (half // 2) + c // 2
                at = (c % 2) * 128
                high_ref[pair, :, at : at + 128] = parcel[c * 128 : (c + 1) * 128]
    blocks = left_ref.shape[0]
    xyz = [coords[d].reshape(blocks, 128) for d in range(3)]
    fill_rows(features, right_rows(xyz))
    fill_rows(rows, left_rows(xyz))

    def turn_left(c, _):
        left_ref[c] = rows_of(rows, c).T.astype(bf16)
        right_ref[c] = rows_of(features, c).astype(bf16)
        return 0

    lax.fori_loop(0, blocks, turn_left, 0, unroll=8)
    copy.wait()
    for c in range(own):
        inv = inverse[c]
        high = inv.astype(bf16)
        at = (c % 2) * 128
        high_ref[me * half + c // 2, :, at : at + 128] = high
        low_ref[c // 2, :, at : at + 128] = (inv - high.astype(f32)).astype(bf16)


def pairs_kernel(low, high, near_ref, left_ref, right_ref, *refs):
    phi_ref, d0, d1 = refs[-3:]
    own = near_ref.shape[1]
    coupled = phi_ref.shape[1] // 128

    def distances(pair, d):
        for q in range(2):
            c = 2 * pair + q
            points = [left_ref[near_ref[c // own, k, c % own]] for k in range(coupled)]
            d[:, q * 128 : (q + 1) * 128] = jnp.dot(
                jnp.concatenate(points, axis=0), right_ref[c], preferred_element_type=f32
            )

    distances(low, d0)
    turns = high - low if high - low <= 8 else 4

    def turn(h, _):
        for u in range(turns):
            pair = low + turns * h + u
            d, later = (d0, d1) if u % 2 == 0 else (d1, d0)
            phi_ref[pair] = weight_of(d[...], True)
            distances(jnp.minimum(pair + 1, high - 1), later)
        return 0

    lax.fori_loop(0, (high - low) // turns, turn, 0)


def sum_kernel(count, made, *refs):
    terms = [x[...] for x in refs[:count]]
    while len(terms) > 1:
        terms = [sum(terms[n + 1 : n + 2], terms[n]) for n in range(0, len(terms), 2)]
    (total,) = terms
    at = 0
    for out in refs[len(refs) - made :]:
        if at == total.shape[0]:
            at = 0
        n = out.shape[0]
        out[...] = total[at : at + n].astype(out.dtype)
        at += n


def join_kernel(*refs):
    *pieces, _, out = refs
    n = pieces[0].shape[0]
    for at, piece in enumerate(pieces):
        out[at * n : (at + 1) * n] = piece[...]


def solve_kernel(nodes, side_ref, me_ref, near_ref, *refs):
    phi_ref, high_ref, low_ref, grad_out, adjoint_out, grads, sums, values0, values1 = refs[4:]
    pairs = high_ref.shape[0]
    own = near_ref.shape[1]
    coupled = phi_ref.shape[1] // 128
    side, me = side_ref[0], me_ref[0]
    half = own // 2
    for core, (held, joined) in ((side, refs[0:2]), (1 - side, refs[2:4])):
        grads[pl.ds(me * own + core * half, half)] = held[...]
        for step in range(1, nodes):
            piece = joined[(step - 1) * half : step * half].astype(f32)
            grads[pl.ds((me ^ step) * own + core * half, half)] = piece

    def through(two, weights, exact):
        rows = []
        for x in two:
            high = x.astype(bf16)
            low = (x - high.astype(f32)).astype(bf16)
            rows.append(jnp.concatenate([high, high], axis=1) if exact else high)
            rows.append(jnp.concatenate([low, jnp.zeros_like(low)], axis=1) if exact else low)
        out = jnp.dot(jnp.concatenate(rows, axis=0), weights, preferred_element_type=f32)
        n = two[0].shape[0]
        return [
            out[2 * q * n : (2 * q + 1) * n, q * 128 : (q + 1) * 128]
            + out[(2 * q + 1) * n : (2 * q + 2) * n, q * 128 : (q + 1) * 128]
            for q in range(2)
        ]

    def start(pair, _):
        done = through([grads[2 * pair], grads[2 * pair + 1]], high_ref[pair], False)
        for q in range(2):
            values0[2 * pair + q] = done[q].astype(bf16)
        return 0

    lax.fori_loop(0, pairs, start, 0, unroll=min(pairs, 16))

    def rest(old, pair):
        near = []
        for q in range(2):
            c = 2 * pair + q
            near.append(
                jnp.concatenate(
                    [old[near_ref[c // own, k, c % own]] for k in range(coupled)], axis=1
                )
            )
        n = near[0].shape[0]
        coupling = jnp.dot(
            jnp.concatenate(near, axis=0), phi_ref[pair], preferred_element_type=f32
        )
        return [
            grads[2 * pair + q] - coupling[q * n : (q + 1) * n, q * 128 : (q + 1) * 128]
            for q in range(2)
        ]

    old, new = values0, values1
    for sweep in range(SWEEPS - 1):

        def left_over(pair, _, old=old):
            two = rest(old, pair)
            for q in range(2):
                sums[2 * pair + q] = two[q]
            return 0

        def apply(pair, _, new=new):
            done = through([sums[2 * pair], sums[2 * pair + 1]], high_ref[pair], False)
            for q in range(2):
                new[2 * pair + q] = done[q].astype(bf16)
            return 0

        lax.fori_loop(0, pairs, left_over, 0, unroll=min(pairs, 16))
        lax.fori_loop(0, pairs, apply, 0, unroll=min(pairs, 16))
        old, new = new, old

    first = me * half
    last = [rest(old, first + pair) for pair in range(half)]
    for pair in range(half):
        weights = jnp.concatenate([high_ref[first + pair], low_ref[pair]], axis=0)
        done = through(last[pair], weights, True)
        for q in range(2):
            grad_out[2 * pair + q] = grads[2 * (first + pair) + q]
            adjoint_out[2 * pair + q] = done[q]


def exchange(x, axis, size, step):
    return lax.ppermute(x, axis, [(i, i ^ step) for i in range(size)])


def local(sizes, volume_grad, volume_coords, support, control_coords, neighbours, block_inverse):
    nodes, fns, subs = sizes["node"], sizes["fn"], sizes["sub"]
    blocks, funcs, width = volume_grad.shape
    own, coupled = neighbours.shape
    controls = own * nodes
    depth = -(-(blocks + GEO) // 128) * 128
    side = lax.axis_index("sub").astype(jnp.int32).reshape(1)
    me = lax.axis_index("node").astype(jnp.int32).reshape(1)

    def hbm(x):
        return pltpu.with_memory_space_constraint(x, pltpu.HBM)

    operands = [
        hbm(x)
        for x in (
            volume_coords.transpose(1, 0, 2),
            support.T,
            volume_grad,
            control_coords.transpose(1, 0, 2),
            block_inverse,
            neighbours.T,
        )
    ]
    half = own // 2
    left, counts, grads, parcel = call(
        prepare_kernel,
        "prepare",
        [
            shape((blocks, width, depth), bf16),
            shape((nodes, blocks, width), f32),
            shape(volume_grad.shape, volume_grad.dtype),
            shape((half * width + 10 * own, width), bf16),
        ],
        [
            pltpu.VMEM((3, blocks, width), f32),
            pltpu.VMEM(support.T.shape, jnp.int32),
            pltpu.VMEM((blocks * GEO, width), f32),
            pltpu.VMEM((controls, width), f32),
            pltpu.VMEM((half, width, width), f32),
            pltpu.VMEM((3, own, width), f32),
            pltpu.VMEM((coupled, own), jnp.int32),
            pltpu.SemaphoreType.DMA((6,)),
        ],
        [side, *operands],
        [SMEM] + [HBM] * 6,
    )
    parcels = [parcel] + [exchange(parcel, "node", nodes, step) for step in range(1, nodes)]

    def evaluate(nodes_done, after):
        per = own * len(nodes_done)
        entries = blocks * per * width * width
        operands = [side, me, left, grads, counts, *(parcels[step] for step in nodes_done)]
        return call(
            functools.partial(chunk_kernel, nodes_done, support.shape[1]),
            f"evaluate_{nodes_done[0]}",
            [shape((per // 2, funcs, width), f32)] * 2,
            [
                pltpu.VMEM((per * GEO, width), f32),
                pltpu.VMEM((per // 2, depth, 2 * width), bf16),
                pltpu.VMEM((per // 2, funcs, 2 * width), f32),
                pltpu.VMEM((per // 2, funcs, 2 * width), f32),
                pltpu.VMEM((TILE * width, 2 * width), f32),
                pltpu.VMEM((TILE * width, 2 * width), f32),
                pltpu.VMEM((TILE * width, 2 * width), bf16),
                pltpu.VMEM((TILE * width, 2 * width), bf16),
            ],
            operands + after,
            [SMEM, SMEM] + [VMEM] * (len(operands) - 2) + [ANY] * len(after),
            pl.CostEstimate(flops=entries * 400, bytes_accessed=4 << 20, transcendentals=entries),
        )

    def add(terms, after=(), parts=1, kinds=(f32,)):
        dims = (terms[0].shape[0] // parts,) + terms[0].shape[1:]
        done = call(
            functools.partial(sum_kernel, len(terms), parts * len(kinds)),
            "sum",
            [shape(dims, kind) for kind in kinds for _ in range(parts)],
            [],
            [*terms, *after],
            [VMEM] * len(terms) + [ANY] * len(after),
        )
        return done if len(done) > 1 else done[0]

    far = list(range(nodes - 1, 1, -1))
    keep, send = evaluate([0], [])
    kept, sent = evaluate(far, [send])
    others = [exchange(x, "sub", subs, 1) for x in parcels[1:]]
    swapped = exchange(sent, "sub", subs, 1)
    operands = [side, me, hbm(block_inverse), *parcels, *others]
    control_left, control_right, high, low, near = call(
        functools.partial(features_kernel, nodes),
        "control_features",
        [
            shape((controls, width, GEO), bf16),
            shape((controls, GEO, width), bf16),
            shape((controls // 2, width, 2 * width), bf16),
            shape((half, width, 2 * width), bf16),
            shape((nodes, own, width), jnp.int32),
        ],
        [
            pltpu.VMEM((3, nodes, own, width), f32),
            pltpu.VMEM((controls * GEO, width), f32),
            pltpu.VMEM((controls * GEO, width), f32),
            pltpu.VMEM((own, width, width), f32),
            pltpu.SemaphoreType.DMA((1,)),
        ],
        operands + [sent],
        [SMEM, SMEM, HBM] + [VMEM] * (2 * nodes - 1) + [ANY],
        pl.CostEstimate(flops=10 << 30, bytes_accessed=1 << 20, transcendentals=0),
    )
    held = add([keep, exchange(send, "sub", subs, 1)], [sent])
    parts = add([kept, swapped], [high], parts=len(far))
    arrived = [exchange(x, "node", nodes, step) for step, x in zip(far, parts)]
    kept, sent = evaluate([1], [*parts, held])
    held = add([held, *arrived], [sent])
    part = add([kept, exchange(sent, "sub", subs, 1)], [held])
    arrived = exchange(part, "node", nodes, 1)

    cuts = [0, 3 * controls // 16, 6 * controls // 16, controls // 2]

    def couple(low_pair, high_pair, before, after):
        operands = [near, control_left, control_right, *before]
        return call(
            functools.partial(pairs_kernel, low_pair, high_pair),
            f"pairs_{low_pair}",
            [shape((controls // 2, coupled * width, 2 * width), bf16)],
            [
                pltpu.VMEM((coupled * width, 2 * width), f32),
                pltpu.VMEM((coupled * width, 2 * width), f32),
            ],
            [*operands, *after],
            [SMEM] + [VMEM] * (len(operands) - 1) + [ANY] * len(after),
            pl.CostEstimate(flops=10 << 30, bytes_accessed=1 << 20, transcendentals=1 << 20),
            {3: 0} if before else None,
        )[0]

    phi = couple(cuts[0], cuts[1], [], [part])
    held = add([held, arrived], [phi])
    phi = couple(cuts[1], cuts[2], [phi], [held])
    terms = [held] + [exchange(held, "fn", fns, turn) for turn in range(1, fns)]
    held, rounded = add(terms, [phi], kinds=(f32, bf16))
    pieces = [exchange(rounded, "node", nodes, step) for step in range(1, nodes)]
    phi = couple(cuts[2], cuts[3], [phi], [rounded])
    joined = call(
        join_kernel,
        "join",
        [shape(((nodes - 1) * half, funcs, width), bf16)],
        [],
        [*pieces, phi],
        [VMEM] * len(pieces) + [ANY],
    )[0]
    mine = [held, joined]
    theirs = [exchange(x, "sub", subs, 1) for x in mine]
    return tuple(
        call(
            functools.partial(solve_kernel, nodes),
            "solve",
            [shape((own, funcs, width), f32)] * 2,
            [
                pltpu.VMEM((controls, funcs, width), f32),
                pltpu.VMEM((controls, funcs, width), f32),
                pltpu.VMEM((controls, funcs, width), bf16),
                pltpu.VMEM((controls, funcs, width), bf16),
            ],
            [side, me, near, *mine, *theirs, phi, high, low],
            [SMEM, SMEM, SMEM] + [VMEM] * 7,
        )
    )


def solution(mesh):
    return jax.shard_map(
        functools.partial(local, dict(mesh.shape)),
        mesh=mesh,
        in_specs=(
            P(("sect", "node", "fn", "sub"), None, None),
            P(("sect", "node", "fn", "sub"), None, None),
            P(("sect", "node", "fn", "sub"), None),
            P(("sect", "node"), None, None),
            P(("sect", "node"), None),
            P(("sect", "node"), None, None),
        ),
        out_specs=(P(("sect", "node"), None, None), P(("sect", "node"), None, None)),
        check_vma=False,
    )
```

```python
import functools
import math

import jax
import jax.numpy as jnp
from jax import lax
from jax.experimental import pallas as pl
from jax.experimental.pallas import tpu as pltpu
from jax.sharding import PartitionSpec as P

SWEEPS = 2
RADIUS = 1.2
C = 4.0**0.2
SCALE = C / RADIUS
GEO = 32
TILE = 4
STEPS = 16
f32, bf16 = jnp.float32, jnp.bfloat16
VMEM = pl.BlockSpec(memory_space=pltpu.VMEM)
SMEM = pl.BlockSpec(memory_space=pltpu.SMEM)
ANY = pl.BlockSpec(memory_space=pl.ANY)
HBM = pl.BlockSpec(memory_space=pltpu.HBM)


def call(kernel, name, out, scratch, operands, specs, cost=None, aliases=None):
    size = 0
    for x in [*out, *scratch, *operands]:
        if len(x.shape) < 2:
            continue
        size += math.prod(x.shape[:-1]) * max(x.shape[-1], 128) * jnp.dtype(x.dtype).itemsize
    return pl.pallas_call(
        kernel,
        out_shape=out,
        in_specs=specs,
        out_specs=[VMEM] * len(out),
        scratch_shapes=scratch,
        compiler_params=pltpu.CompilerParams(vmem_limit_bytes=size + (4 << 20)),
        cost_estimate=cost,
        input_output_aliases=aliases or {},
        name=name,
    )(*operands)


def shape(dims, kind):
    return jax.ShapeDtypeStruct(dims, kind)


def weight_of(square, safe):
    square = jnp.maximum(square, 1e-12) if safe else square
    root = square * lax.rsqrt(square)
    inside = jnp.maximum(C - root, 0.0)
    twice = inside * inside
    return ((twice * twice) * (0.25 * C + root)).astype(bf16)


def split3(v):
    a = v.astype(bf16).astype(f32)
    b = (v - a).astype(bf16).astype(f32)
    return (a, b, v - a - b)


def pairs_of_parts():
    return [(a, b) for a in range(3) for b in range(3) if a + b < 4]


def left_rows(xyz):
    rows = []
    for v in xyz:
        parts = split3(v)
        rows += [parts[a] for a, b in pairs_of_parts()]
    rows += list(split3(sum(v * v for v in xyz)))
    return rows + [jnp.ones_like(xyz[0])] * 3


def right_rows(xyz):
    rows = []
    for v in xyz:
        parts = split3(v)
        rows += [-2.0 * parts[b] for a, b in pairs_of_parts()]
    rows += [jnp.ones_like(xyz[0])] * 3
    return rows + list(split3(sum(v * v for v in xyz)))


def told(ref, count):
    rows = ref[ref.shape[0] - 10 * count :].astype(f32)
    part = [rows[n * count : (n + 1) * count] for n in range(10)]
    xyz = [((part[3 * d + 2] + part[3 * d + 1]) + part[3 * d]) * SCALE for d in range(3)]
    return xyz, part[9]


def fill_rows(scratch, rows, first=0):
    blocks = scratch.shape[0] // GEO
    n = rows[0].shape[0]
    for g in range(GEO):
        row = rows[g] if g < len(rows) else jnp.zeros_like(rows[0])
        scratch[g * blocks + first : g * blocks + first + n] = row


def rows_of(scratch, block):
    return scratch[pl.ds(block, GEO, stride=scratch.shape[0] // GEO), :]


def prepare_kernel(
    side_ref, volume_hbm, listed_hbm, grad_hbm, control_hbm, inverse_hbm, near_hbm, *refs
):
    left_ref, counts_ref, grad_ref, parcel_ref = refs[:4]
    coords, listed, scratch, tally, inverse, control, near, sems = refs[4:]
    half = inverse.shape[0]
    own = 2 * half
    mine = pl.ds(side_ref[0] * half, half)
    copies = [
        pltpu.make_async_copy(source, target, sems.at[n])
        for n, (source, target) in enumerate(
            [
                (volume_hbm, coords),
                (listed_hbm, listed),
                (inverse_hbm.at[mine], inverse),
                (near_hbm, near),
                (control_hbm, control),
                (grad_hbm, grad_ref),
            ]
        )
    ]
    for copy in copies:
        copy.start()
    copies[0].wait()
    fill_rows(scratch, left_rows([coords[d] * SCALE for d in range(3)]))
    blocks, width, depth = left_ref.shape
    lane = lax.broadcasted_iota(jnp.int32, (width, depth), 1)

    def one(s, _):
        turned = rows_of(scratch, s).T
        turned = jnp.concatenate([turned, jnp.zeros((width, depth - GEO), f32)], axis=1)
        left_ref[s] = jnp.where(lane == s + GEO, 1.0, turned).astype(bf16)
        return 0

    lax.fori_loop(0, blocks, one, 0, unroll=8)
    copies[1].wait()
    chosen = listed[...]
    nodes = counts_ref.shape[0]
    tally[...] = jnp.zeros_like(tally)
    for c in range(nodes * own):
        tally[c : c + 1, 0:blocks] = jnp.sum(
            jnp.where(chosen == c, 1.0, 0.0), axis=0, keepdims=True
        )
    for n in range(nodes):
        turned = tally[n * own : (n + 1) * own, :].T[0:blocks]
        counts_ref[n] = jnp.concatenate([turned, jnp.zeros((blocks, width - own), f32)], axis=1)
    for copy in copies[2:]:
        copy.wait()
    for q in range(half):
        parcel_ref[q * 128 : (q + 1) * 128] = inverse[q].astype(bf16)
    rows = [part for d in range(3) for part in split3(control[d])]
    numbers = near[...].astype(f32)
    numbers = jnp.concatenate([numbers, jnp.zeros((near.shape[0], width - own), f32)], axis=1)
    rows.append(jnp.concatenate([numbers, jnp.zeros((own - near.shape[0], width), f32)], axis=0))
    parcel_ref[half * 128 :] = jnp.concatenate(rows, axis=0).astype(bf16)


def chunk_kernel(nodes_done, listed, *refs):
    side_ref, me_ref, left_ref, grad_ref, counts_ref = refs[:5]
    parcels = refs[5 : 5 + len(nodes_done)]
    keep_ref, send_ref, features, rhs, total, result, d0, d1, p0, p1 = refs[-10:]
    blocks = grad_ref.shape[0]
    per = features.shape[0] // GEO
    own = per // len(nodes_done)
    depth = rhs.shape[1]
    steps = blocks // TILE
    pairs = per // 2
    whole = pairs * steps
    size = TILE * 128
    counts = [
        counts_ref[me_ref[0] ^ step][:, 0:own].astype(jnp.int32) for step in nodes_done
    ]
    most = counts[0]
    for other in counts[1:]:
        most = jnp.maximum(most, other)
    most = jnp.max(most)
    layers = jnp.int32(0)
    for b in range(listed.bit_length()):
        layers = layers + jnp.where(most >= (1 << b), 1, 0)
    result[...] = jnp.zeros_like(result)
    for n, parcel in enumerate(parcels):
        fill_rows(features, right_rows(told(parcel, own)[0]), n * own)
    rhs[...] = jnp.zeros_like(rhs)
    for c in range(per):
        rhs[c // 2, 0:GEO, (c % 2) * 128 : (c % 2 + 1) * 128] = rows_of(features, c).astype(
            bf16
        )

    def distances(t, d):
        j, i = t // steps, t % steps
        left = left_ref[pl.ds(i * TILE, TILE)].reshape(size, depth)
        d[...] = jnp.dot(left, rhs[j], preferred_element_type=f32)

    def values(d, p, safe):
        p[...] = weight_of(d[...], safe)

    def products(t, p):
        j, i = t // steps, t % steps
        g = jnp.concatenate([grad_ref[i * TILE + q] for q in range(TILE)], axis=1)
        total[j] += jnp.dot(g, p[...], preferred_element_type=f32)

    def layer(safe, turns, b, weight):
        for c in range(per):
            count = counts[c // own][:, c % own : c % own + 1]
            bit = jnp.bitwise_and(lax.shift_right_logical(count, b), 1)
            far = jnp.where(jnp.broadcast_to(bit, (blocks, 128)) == 1, 0.0, 65536.0)
            rhs[c // 2, GEO : GEO + blocks, (c % 2) * 128 : (c % 2 + 1) * 128] = far.astype(bf16)
        total[...] = jnp.zeros_like(total)
        p1[...] = jnp.zeros_like(p1)
        distances(0, d0)

        def turn(h, _):
            for u in range(turns):
                t = turns * h + u
                d, p = (d0, p0) if u % 2 == 0 else (d1, p1)
                later, done = (d1, p1) if u % 2 == 0 else (d0, p0)
                values(d, p, safe)
                distances(jnp.minimum(t + 1, whole - 1), later)
                products(jnp.maximum(t - 1, 0), done)
            return 0

        lax.fori_loop(0, whole // turns, turn, 0)
        products(whole - 1, p1)
        result[...] += weight * total[...]
        return weight * 2.0

    lax.fori_loop(0, layers, functools.partial(layer, False, STEPS), jnp.float32(1.0))
    failed = jnp.max(jnp.where(result[...] != result[...], 1, 0))

    def again(_, carry):
        result[...] = jnp.zeros_like(result)
        lax.fori_loop(0, layers, functools.partial(layer, True, 2), jnp.float32(1.0))
        return carry

    lax.fori_loop(0, failed, again, 0)
    side = side_ref[0]
    half = own // 4
    for n in range(len(nodes_done)):
        for j in range(half):
            mine = result[n * 2 * half + side * half + j]
            other = result[n * 2 * half + (1 - side) * half + j]
            for q in range(2):
                keep_ref[n * 2 * half + 2 * j + q] = mine[:, q * 128 : (q + 1) * 128]
                send_ref[n * 2 * half + 2 * j + q] = other[:, q * 128 : (q + 1) * 128]


def features_kernel(nodes, side_ref, me_ref, inverse_hbm, *refs):
    parcels = refs[:nodes]
    others = refs[nodes]
    rows_each = parcels[0].shape[0]
    left_ref, right_ref, high_ref, low_ref, near_ref = refs[-10:-5]
    coords, features, rows, inverse, sem = refs[-5:]
    copy = pltpu.make_async_copy(inverse_hbm, inverse, sem.at[0])
    copy.start()
    own = inverse.shape[0]
    half = own // 2
    side, me = side_ref[0], me_ref[0]
    for step in range(nodes):
        xyz, numbers = told(parcels[step], own)
        for d in range(3):
            coords[d, me ^ step] = xyz[d]
        near_ref[me ^ step] = numbers.astype(jnp.int32)
    for step in range(1, nodes):
        for core, parcel in (
            (side, parcels[step]),
            (1 - side, others.at[(step - 1) * rows_each : step * rows_each]),
        ):
            for c in range(half):
                pair = (me ^ step) * half + core * (half // 2) + c // 2
                at = (c % 2) * 128
                high_ref[pair, :, at : at + 128] = parcel[c * 128 : (c + 1) * 128]
    blocks = left_ref.shape[0]
    xyz = [coords[d].reshape(blocks, 128) for d in range(3)]
    fill_rows(features, right_rows(xyz))
    fill_rows(rows, left_rows(xyz))

    def turn_left(c, _):
        left_ref[c] = rows_of(rows, c).T.astype(bf16)
        right_ref[c] = rows_of(features, c).astype(bf16)
        return 0

    lax.fori_loop(0, blocks, turn_left, 0, unroll=8)
    copy.wait()
    for c in range(own):
        inv = inverse[c]
        high = inv.astype(bf16)
        at = (c % 2) * 128
        high_ref[me * half + c // 2, :, at : at + 128] = high
        low_ref[c // 2, :, at : at + 128] = (inv - high.astype(f32)).astype(bf16)


def pairs_kernel(low, high, near_ref, left_ref, right_ref, *refs):
    phi_ref, d0, d1 = refs[-3:]
    own = near_ref.shape[1]
    coupled = phi_ref.shape[1] // 128

    def distances(pair, d):
        for q in range(2):
            c = 2 * pair + q
            points = [left_ref[near_ref[c // own, k, c % own]] for k in range(coupled)]
            d[:, q * 128 : (q + 1) * 128] = jnp.dot(
                jnp.concatenate(points, axis=0), right_ref[c], preferred_element_type=f32
            )

    distances(low, d0)
    turns = high - low if high - low <= 12 else 4

    def turn(h, _):
        for u in range(turns):
            pair = low + turns * h + u
            d, later = (d0, d1) if u % 2 == 0 else (d1, d0)
            phi_ref[pair] = weight_of(d[...], True)
            distances(jnp.minimum(pair + 1, high - 1), later)
        return 0

    lax.fori_loop(0, (high - low) // turns, turn, 0)


def sum_kernel(count, made, *refs):
    terms = [x[...] for x in refs[:count]]
    while len(terms) > 1:
        terms = [sum(terms[n + 1 : n + 2], terms[n]) for n in range(0, len(terms), 2)]
    (total,) = terms
    at = 0
    for out in refs[len(refs) - made :]:
        if at == total.shape[0]:
            at = 0
        n = out.shape[0]
        out[...] = total[at : at + n].astype(out.dtype)
        at += n


def join_kernel(count, *refs):
    out = refs[-1]
    at = 0
    for piece in refs[:count]:
        out[at : at + piece.shape[0]] = piece[...]
        at += piece.shape[0]


def solve_kernel(nodes, side_ref, me_ref, near_ref, *refs):
    phi_ref, high_ref, low_ref, grad_out, adjoint_out, grads, sums, values0, values1 = refs[4:]
    pairs = high_ref.shape[0]
    own = near_ref.shape[1]
    coupled = phi_ref.shape[1] // 128
    side, me = side_ref[0], me_ref[0]
    half = own // 2
    for core, (held, joined) in ((side, refs[0:2]), (1 - side, refs[2:4])):
        grads[pl.ds(me * own + core * half, half)] = held[...]
        for step in range(1, nodes):
            piece = joined[(step - 1) * half : step * half].astype(f32)
            grads[pl.ds((me ^ step) * own + core * half, half)] = piece

    def through(two, weights, exact):
        rows = []
        for x in two:
            high = x.astype(bf16)
            low = (x - high.astype(f32)).astype(bf16)
            rows.append(jnp.concatenate([high, high], axis=1) if exact else high)
            rows.append(jnp.concatenate([low, jnp.zeros_like(low)], axis=1) if exact else low)
        out = jnp.dot(jnp.concatenate(rows, axis=0), weights, preferred_element_type=f32)
        n = two[0].shape[0]
        return [
            out[2 * q * n : (2 * q + 1) * n, q * 128 : (q + 1) * 128]
            + out[(2 * q + 1) * n : (2 * q + 2) * n, q * 128 : (q + 1) * 128]
            for q in range(2)
        ]

    def start(pair, _):
        done = through([grads[2 * pair], grads[2 * pair + 1]], high_ref[pair], False)
        for q in range(2):
            values0[2 * pair + q] = done[q].astype(bf16)
        return 0

    lax.fori_loop(0, pairs, start, 0, unroll=min(pairs, 16))

    def rest(old, pair):
        near = []
        for q in range(2):
            c = 2 * pair + q
            near.append(
                jnp.concatenate(
                    [old[near_ref[c // own, k, c % own]] for k in range(coupled)], axis=1
                )
            )
        n = near[0].shape[0]
        coupling = jnp.dot(
            jnp.concatenate(near, axis=0), phi_ref[pair], preferred_element_type=f32
        )
        return [
            grads[2 * pair + q] - coupling[q * n : (q + 1) * n, q * 128 : (q + 1) * 128]
            for q in range(2)
        ]

    old, new = values0, values1
    for sweep in range(SWEEPS - 1):

        def left_over(pair, _, old=old):
            two = rest(old, pair)
            for q in range(2):
                sums[2 * pair + q] = two[q]
            return 0

        def apply(pair, _, new=new):
            done = through([sums[2 * pair], sums[2 * pair + 1]], high_ref[pair], False)
            for q in range(2):
                new[2 * pair + q] = done[q].astype(bf16)
            return 0

        lax.fori_loop(0, pairs, left_over, 0, unroll=min(pairs, 16))
        lax.fori_loop(0, pairs, apply, 0, unroll=min(pairs, 16))
        old, new = new, old

    first = me * half
    last = [rest(old, first + pair) for pair in range(half)]
    for pair in range(half):
        weights = jnp.concatenate([high_ref[first + pair], low_ref[pair]], axis=0)
        done = through(last[pair], weights, True)
        for q in range(2):
            grad_out[2 * pair + q] = grads[2 * (first + pair) + q]
            adjoint_out[2 * pair + q] = done[q]


def exchange(x, axis, size, step):
    return lax.ppermute(x, axis, [(i, i ^ step) for i in range(size)])


def across(x, nodes, fns, step, turn):
    pairs = [(n * fns + f, (n ^ step) * fns + (f ^ turn)) for n in range(nodes) for f in range(fns)]
    return lax.ppermute(x, ("node", "fn"), pairs)


def local(sizes, volume_grad, volume_coords, support, control_coords, neighbours, block_inverse):
    nodes, fns, subs = sizes["node"], sizes["fn"], sizes["sub"]
    blocks, funcs, width = volume_grad.shape
    own, coupled = neighbours.shape
    controls = own * nodes
    depth = -(-(blocks + GEO) // 128) * 128
    side = lax.axis_index("sub").astype(jnp.int32).reshape(1)
    me = lax.axis_index("node").astype(jnp.int32).reshape(1)

    def hbm(x):
        return pltpu.with_memory_space_constraint(x, pltpu.HBM)

    operands = [
        hbm(x)
        for x in (
            volume_coords.transpose(1, 0, 2),
            support.T,
            volume_grad,
            control_coords.transpose(1, 0, 2),
            block_inverse,
            neighbours.T,
        )
    ]
    half = own // 2
    left, counts, grads, parcel = call(
        prepare_kernel,
        "prepare",
        [
            shape((blocks, width, depth), bf16),
            shape((nodes, blocks, width), f32),
            shape(volume_grad.shape, volume_grad.dtype),
            shape((half * width + 10 * own, width), bf16),
        ],
        [
            pltpu.VMEM((3, blocks, width), f32),
            pltpu.VMEM(support.T.shape, jnp.int32),
            pltpu.VMEM((blocks * GEO, width), f32),
            pltpu.VMEM((controls, width), f32),
            pltpu.VMEM((half, width, width), f32),
            pltpu.VMEM((3, own, width), f32),
            pltpu.VMEM((coupled, own), jnp.int32),
            pltpu.SemaphoreType.DMA((6,)),
        ],
        [side, *operands],
        [SMEM] + [HBM] * 6,
    )
    parcels = [parcel] + [exchange(parcel, "node", nodes, step) for step in range(1, nodes)]

    def evaluate(nodes_done, after):
        per = own * len(nodes_done)
        entries = blocks * per * width * width
        operands = [side, me, left, grads, counts, *(parcels[step] for step in nodes_done)]
        return call(
            functools.partial(chunk_kernel, nodes_done, support.shape[1]),
            f"evaluate_{nodes_done[0]}",
            [shape((per // 2, funcs, width), f32)] * 2,
            [
                pltpu.VMEM((per * GEO, width), f32),
                pltpu.VMEM((per // 2, depth, 2 * width), bf16),
                pltpu.VMEM((per // 2, funcs, 2 * width), f32),
                pltpu.VMEM((per // 2, funcs, 2 * width), f32),
                pltpu.VMEM((TILE * width, 2 * width), f32),
                pltpu.VMEM((TILE * width, 2 * width), f32),
                pltpu.VMEM((TILE * width, 2 * width), bf16),
                pltpu.VMEM((TILE * width, 2 * width), bf16),
            ],
            operands + after,
            [SMEM, SMEM] + [VMEM] * (len(operands) - 2) + [ANY] * len(after),
            pl.CostEstimate(flops=entries * 400, bytes_accessed=4 << 20, transcendentals=entries),
        )

    def add(terms, after=(), parts=1, kinds=(f32,)):
        dims = (terms[0].shape[0] // parts,) + terms[0].shape[1:]
        done = call(
            functools.partial(sum_kernel, len(terms), parts * len(kinds)),
            "sum",
            [shape(dims, kind) for kind in kinds for _ in range(parts)],
            [],
            [*terms, *after],
            [VMEM] * len(terms) + [ANY] * len(after),
        )
        return done if len(done) > 1 else done[0]

    def join(pieces, after):
        rows = sum(x.shape[0] for x in pieces)
        return call(
            functools.partial(join_kernel, len(pieces)),
            "join",
            [shape((rows,) + pieces[0].shape[1:], pieces[0].dtype)],
            [],
            [*pieces, *after],
            [VMEM] * len(pieces) + [ANY] * len(after),
        )[0]

    far = list(range(nodes - 1, 1, -1))
    keep, send = evaluate([0], [])
    kept, sent = evaluate(far, [send])
    others = exchange(join(parcels[1:], []), "sub", subs, 1)
    swapped = exchange(sent, "sub", subs, 1)
    operands = [side, me, hbm(block_inverse), *parcels, others]
    control_left, control_right, high, low, near = call(
        functools.partial(features_kernel, nodes),
        "control_features",
        [
            shape((controls, width, GEO), bf16),
            shape((controls, GEO, width), bf16),
            shape((controls // 2, width, 2 * width), bf16),
            shape((half, width, 2 * width), bf16),
            shape((nodes, own, width), jnp.int32),
        ],
        [
            pltpu.VMEM((3, nodes, own, width), f32),
            pltpu.VMEM((controls * GEO, width), f32),
            pltpu.VMEM((controls * GEO, width), f32),
            pltpu.VMEM((own, width, width), f32),
            pltpu.SemaphoreType.DMA((1,)),
        ],
        operands + [sent],
        [SMEM, SMEM, HBM] + [VMEM] * (nodes + 1) + [ANY],
        pl.CostEstimate(flops=10 << 30, bytes_accessed=1 << 20, transcendentals=0),
    )
    held = add([keep, exchange(send, "sub", subs, 1)], [sent])
    parts = add([kept, swapped], [high], parts=len(far))
    arrived = [exchange(x, "node", nodes, step) for step, x in zip(far, parts)]
    kept, sent = evaluate([1], [*parts, held])
    held = add([held, *arrived], [sent])
    part = add([kept, exchange(sent, "sub", subs, 1)], [held])
    terms = [held] + [exchange(held, "fn", fns, turn) for turn in range(1, fns)]
    terms += [exchange(part, "node", nodes, 1)]
    terms += [across(part, nodes, fns, 1, turn) for turn in range(1, fns)]

    cuts = [0, 3 * controls // 8, controls // 2]

    def couple(low_pair, high_pair, before, after):
        operands = [near, control_left, control_right, *before]
        return call(
            functools.partial(pairs_kernel, low_pair, high_pair),
            f"pairs_{low_pair}",
            [shape((controls // 2, coupled * width, 2 * width), bf16)],
            [
                pltpu.VMEM((coupled * width, 2 * width), f32),
                pltpu.VMEM((coupled * width, 2 * width), f32),
            ],
            [*operands, *after],
            [SMEM] + [VMEM] * (len(operands) - 1) + [ANY] * len(after),
            pl.CostEstimate(flops=10 << 30, bytes_accessed=1 << 20, transcendentals=1 << 20),
            {3: 0} if before else None,
        )[0]

    phi = couple(cuts[0], cuts[1], [], [part])
    held, rounded = add(terms, [phi], kinds=(f32, bf16))
    pieces = [exchange(rounded, "node", nodes, step) for step in range(1, nodes)]
    phi = couple(cuts[1], cuts[2], [phi], [rounded])
    joined = join(pieces, [phi])
    mine = [held, joined]
    theirs = [exchange(x, "sub", subs, 1) for x in mine]
    return tuple(
        call(
            functools.partial(solve_kernel, nodes),
            "solve",
            [shape((own, funcs, width), f32)] * 2,
            [
                pltpu.VMEM((controls, funcs, width), f32),
                pltpu.VMEM((controls, funcs, width), f32),
                pltpu.VMEM((controls, funcs, width), bf16),
                pltpu.VMEM((controls, funcs, width), bf16),
            ],
            [side, me, near, *mine, *theirs, phi, high, low],
            [SMEM, SMEM, SMEM] + [VMEM] * 7,
        )
    )


def solution(mesh):
    return jax.shard_map(
        functools.partial(local, dict(mesh.shape)),
        mesh=mesh,
        in_specs=(
            P(("sect", "node", "fn", "sub"), None, None),
            P(("sect", "node", "fn", "sub"), None, None),
            P(("sect", "node", "fn", "sub"), None),
            P(("sect", "node"), None, None),
            P(("sect", "node"), None),
            P(("sect", "node"), None, None),
        ),
        out_specs=(P(("sect", "node"), None, None), P(("sect", "node"), None, None)),
        check_vma=False,
    )
```

```python
import functools
import math

import jax
import jax.numpy as jnp
from jax import lax
from jax.experimental import pallas as pl
from jax.experimental.pallas import tpu as pltpu
from jax.sharding import PartitionSpec as P

SWEEPS = 2
RADIUS = 1.2
C = 4.0**0.2
SCALE = C / RADIUS
GEO = 32
TILE = 4
STEPS = 16
f32, bf16 = jnp.float32, jnp.bfloat16
VMEM = pl.BlockSpec(memory_space=pltpu.VMEM)
SMEM = pl.BlockSpec(memory_space=pltpu.SMEM)
ANY = pl.BlockSpec(memory_space=pl.ANY)
HBM = pl.BlockSpec(memory_space=pltpu.HBM)


def call(kernel, name, out, scratch, operands, specs, cost=None, aliases=None):
    size = 0
    for x in [*out, *scratch, *operands]:
        if len(x.shape) < 2:
            continue
        size += math.prod(x.shape[:-1]) * max(x.shape[-1], 128) * jnp.dtype(x.dtype).itemsize
    return pl.pallas_call(
        kernel,
        out_shape=out,
        in_specs=specs,
        out_specs=[VMEM] * len(out),
        scratch_shapes=scratch,
        compiler_params=pltpu.CompilerParams(vmem_limit_bytes=size + (4 << 20)),
        cost_estimate=cost,
        input_output_aliases=aliases or {},
        name=name,
    )(*operands)


def shape(dims, kind):
    return jax.ShapeDtypeStruct(dims, kind)


def weight_of(square, safe):
    square = jnp.maximum(square, 1e-12) if safe else square
    root = square * lax.rsqrt(square)
    inside = jnp.maximum(C - root, 0.0)
    twice = inside * inside
    return ((twice * twice) * (0.25 * C + root)).astype(bf16)


def split3(v):
    a = v.astype(bf16).astype(f32)
    b = (v - a).astype(bf16).astype(f32)
    return (a, b, v - a - b)


def pairs_of_parts():
    return [(a, b) for a in range(3) for b in range(3) if a + b < 4]


def left_rows(xyz):
    rows = []
    for v in xyz:
        parts = split3(v)
        rows += [parts[a] for a, b in pairs_of_parts()]
    rows += list(split3(sum(v * v for v in xyz)))
    return rows + [jnp.ones_like(xyz[0])] * 3


def right_rows(xyz):
    rows = []
    for v in xyz:
        parts = split3(v)
        rows += [-2.0 * parts[b] for a, b in pairs_of_parts()]
    rows += [jnp.ones_like(xyz[0])] * 3
    return rows + list(split3(sum(v * v for v in xyz)))


def told(ref, count):
    rows = ref[ref.shape[0] - 10 * count :].astype(f32)
    part = [rows[n * count : (n + 1) * count] for n in range(10)]
    xyz = [((part[3 * d + 2] + part[3 * d + 1]) + part[3 * d]) * SCALE for d in range(3)]
    return xyz, part[9]


def fill_rows(scratch, rows, first=0):
    blocks = scratch.shape[0] // GEO
    n = rows[0].shape[0]
    for g in range(GEO):
        row = rows[g] if g < len(rows) else jnp.zeros_like(rows[0])
        scratch[g * blocks + first : g * blocks + first + n] = row


def rows_of(scratch, block):
    return scratch[pl.ds(block, GEO, stride=scratch.shape[0] // GEO), :]


def far_of(counts_ref, s, b):
    bits = lax.shift_right_logical(counts_ref[pl.ds(s, 1), :].astype(jnp.int32), b)
    return jnp.where(jnp.bitwise_and(bits, 1) == 1, 0.0, 65536.0)


def prepare_kernel(
    controls, side_ref, volume_hbm, listed_hbm, grad_hbm, control_hbm, inverse_hbm, near_hbm, *refs
):
    left_ref, counts_ref, grad_ref, parcel_ref = refs[:4]
    coords, listed, scratch, tally, inverse, control, near, sems = refs[4:]
    half = inverse.shape[0]
    own = 2 * half
    mine = pl.ds(side_ref[0] * half, half)
    copies = [
        pltpu.make_async_copy(source, target, sems.at[n])
        for n, (source, target) in enumerate(
            [
                (volume_hbm, coords),
                (listed_hbm, listed),
                (inverse_hbm.at[mine], inverse),
                (near_hbm, near),
                (control_hbm, control),
                (grad_hbm, grad_ref),
            ]
        )
    ]
    for copy in copies:
        copy.start()
    blocks, width, depth = left_ref.shape
    copies[1].wait()
    chosen = listed[...]
    tally[...] = jnp.zeros_like(tally)
    for c in range(controls):
        tally[GEO + c : GEO + c + 1, 0:blocks] = jnp.sum(
            jnp.where(chosen == c, 1.0, 0.0), axis=0, keepdims=True
        )
    counts_ref[...] = tally[...].T[0:blocks]
    copies[0].wait()
    fill_rows(scratch, left_rows([coords[d] * SCALE for d in range(3)]))
    lane = lax.broadcasted_iota(jnp.int32, (width, depth), 1)

    def one(s, _):
        turned = rows_of(scratch, s).T
        turned = jnp.concatenate([turned, jnp.zeros((width, depth - GEO), f32)], axis=1)
        left_ref[s] = jnp.where(lane < GEO, turned, far_of(counts_ref, s, 0)).astype(bf16)
        return 0

    lax.fori_loop(0, blocks, one, 0, unroll=8)
    for copy in copies[2:]:
        copy.wait()
    for q in range(half):
        parcel_ref[q * 128 : (q + 1) * 128] = inverse[q].astype(bf16)
    rows = [part for d in range(3) for part in split3(control[d])]
    numbers = near[...].astype(f32)
    numbers = jnp.concatenate([numbers, jnp.zeros((near.shape[0], width - own), f32)], axis=1)
    rows.append(jnp.concatenate([numbers, jnp.zeros((own - near.shape[0], width), f32)], axis=0))
    parcel_ref[half * 128 :] = jnp.concatenate(rows, axis=0).astype(bf16)


def chunk_kernel(nodes_done, listed, *refs):
    side_ref, me_ref, left_ref, grad_ref, counts_ref = refs[:5]
    parcels = refs[5 : 5 + len(nodes_done)]
    keep_ref, send_ref, features, rhs, again_left, total, result, d0, d1, p0, p1 = refs[-11:]
    blocks = grad_ref.shape[0]
    per = features.shape[0] // GEO
    own = per // len(nodes_done)
    depth = rhs.shape[1]
    steps = blocks // TILE
    pairs = per // 2
    whole = pairs * steps
    size = TILE * 128
    result[...] = jnp.zeros_like(result)
    for n, parcel in enumerate(parcels):
        fill_rows(features, right_rows(told(parcel, own)[0]), n * own)
    row = lax.broadcasted_iota(jnp.int32, (depth - GEO, 128), 0)
    for c in range(per):
        at = (c % 2) * 128
        place = (me_ref[0] ^ nodes_done[c // own]) * own + c % own
        rhs[c // 2, 0:GEO, at : at + 128] = rows_of(features, c).astype(bf16)
        rhs[c // 2, GEO:, at : at + 128] = jnp.where(row == place, 1.0, 0.0).astype(bf16)

    def distances(lefts, t, d):
        j, i = t // steps, t % steps
        left = lefts[pl.ds(i * TILE, TILE)].reshape(size, depth)
        d[...] = jnp.dot(left, rhs[j], preferred_element_type=f32)

    def values(d, p, safe):
        p[...] = weight_of(d[...], safe)

    def products(t, p):
        j, i = t // steps, t % steps
        g = jnp.concatenate([grad_ref[i * TILE + q] for q in range(TILE)], axis=1)
        total[j] += jnp.dot(g, p[...], preferred_element_type=f32)

    def layer(lefts, safe, turns, weight):
        total[...] = jnp.zeros_like(total)
        p1[...] = jnp.zeros_like(p1)
        distances(lefts, 0, d0)

        def turn(h, _):
            for u in range(turns):
                t = turns * h + u
                d, p = (d0, p0) if u % 2 == 0 else (d1, p1)
                later, done = (d1, p1) if u % 2 == 0 else (d0, p0)
                values(d, p, safe)
                distances(lefts, jnp.minimum(t + 1, whole - 1), later)
                products(jnp.maximum(t - 1, 0), done)
            return 0

        lax.fori_loop(0, whole // turns, turn, 0)
        products(whole - 1, p1)
        result[...] += weight * total[...]

    layer(left_ref, False, STEPS, 1.0)
    failed = jnp.max(jnp.where(result[...] != result[...], 1, 0))
    most = jnp.max(counts_ref[...])
    layers = jnp.int32(0)
    for b in range(listed.bit_length()):
        layers = layers + jnp.where(most >= float(1 << b), 1, 0)
    failed = jnp.maximum(failed, jnp.where(layers > 1, 1, 0))

    def bit(b, weight):
        def renew(s, _):
            lane = lax.broadcasted_iota(jnp.int32, (128, depth), 1)
            kept = left_ref[s].astype(f32)
            again_left[s] = jnp.where(lane < GEO, kept, far_of(counts_ref, s, b)).astype(bf16)
            return 0

        lax.fori_loop(0, blocks, renew, 0)
        layer(again_left, True, 2, weight)
        return weight * 2.0

    def again(_, carry):
        result[...] = jnp.zeros_like(result)
        lax.fori_loop(0, layers, bit, jnp.float32(1.0))
        return carry

    lax.fori_loop(0, failed, again, 0)
    side = side_ref[0]
    half = own // 4
    for n in range(len(nodes_done)):
        for j in range(half):
            mine = result[n * 2 * half + side * half + j]
            other = result[n * 2 * half + (1 - side) * half + j]
            for q in range(2):
                keep_ref[n * 2 * half + 2 * j + q] = mine[:, q * 128 : (q + 1) * 128]
                send_ref[n * 2 * half + 2 * j + q] = other[:, q * 128 : (q + 1) * 128]


def features_kernel(nodes, side_ref, me_ref, inverse_hbm, *refs):
    parcels = refs[:nodes]
    others = refs[nodes]
    rows_each = parcels[0].shape[0]
    left_ref, right_ref, high_ref, low_ref, near_ref = refs[-10:-5]
    coords, features, rows, inverse, sem = refs[-5:]
    copy = pltpu.make_async_copy(inverse_hbm, inverse, sem.at[0])
    copy.start()
    own = inverse.shape[0]
    half = own // 2
    side, me = side_ref[0], me_ref[0]
    for step in range(nodes):
        xyz, numbers = told(parcels[step], own)
        for d in range(3):
            coords[d, me ^ step] = xyz[d]
        near_ref[me ^ step] = numbers.astype(jnp.int32)
    for step in range(1, nodes):
        for core, parcel in (
            (side, parcels[step]),
            (1 - side, others.at[(step - 1) * rows_each : step * rows_each]),
        ):
            for c in range(half):
                pair = (me ^ step) * half + core * (half // 2) + c // 2
                at = (c % 2) * 128
                high_ref[pair, :, at : at + 128] = parcel[c * 128 : (c + 1) * 128]
    blocks = left_ref.shape[0]
    xyz = [coords[d].reshape(blocks, 128) for d in range(3)]
    fill_rows(features, right_rows(xyz))
    fill_rows(rows, left_rows(xyz))

    def turn_left(c, _):
        left_ref[c] = rows_of(rows, c).T.astype(bf16)
        right_ref[c] = rows_of(features, c).astype(bf16)
        return 0

    lax.fori_loop(0, blocks, turn_left, 0, unroll=8)
    copy.wait()
    for c in range(own):
        inv = inverse[c]
        high = inv.astype(bf16)
        at = (c % 2) * 128
        high_ref[me * half + c // 2, :, at : at + 128] = high
        low_ref[c // 2, :, at : at + 128] = (inv - high.astype(f32)).astype(bf16)


def pairs_kernel(low, high, near_ref, left_ref, right_ref, *refs):
    phi_ref, d0, d1 = refs[-3:]
    own = near_ref.shape[1]
    coupled = phi_ref.shape[1] // 128

    def distances(pair, d):
        for q in range(2):
            c = 2 * pair + q
            points = [left_ref[near_ref[c // own, k, c % own]] for k in range(coupled)]
            d[:, q * 128 : (q + 1) * 128] = jnp.dot(
                jnp.concatenate(points, axis=0), right_ref[c], preferred_element_type=f32
            )

    distances(low, d0)
    turns = high - low if high - low <= 12 else 4

    def turn(h, _):
        for u in range(turns):
            pair = low + turns * h + u
            d, later = (d0, d1) if u % 2 == 0 else (d1, d0)
            phi_ref[pair] = weight_of(d[...], True)
            distances(jnp.minimum(pair + 1, high - 1), later)
        return 0

    lax.fori_loop(0, (high - low) // turns, turn, 0)


def sum_kernel(count, made, *refs):
    terms = [x[...] for x in refs[:count]]
    while len(terms) > 1:
        terms = [sum(terms[n + 1 : n + 2], terms[n]) for n in range(0, len(terms), 2)]
    (total,) = terms
    at = 0
    for out in refs[len(refs) - made :]:
        if at == total.shape[0]:
            at = 0
        n = out.shape[0]
        out[...] = total[at : at + n].astype(out.dtype)
        at += n


def join_kernel(count, *refs):
    out = refs[-1]
    at = 0
    for piece in refs[:count]:
        out[at : at + piece.shape[0]] = piece[...]
        at += piece.shape[0]


def solve_kernel(nodes, side_ref, me_ref, near_ref, *refs):
    phi_ref, high_ref, low_ref, grad_out, adjoint_out, grads, sums, values0, values1 = refs[2 * nodes :]
    pairs = high_ref.shape[0]
    own = near_ref.shape[1]
    coupled = phi_ref.shape[1] // 128
    side, me = side_ref[0], me_ref[0]
    half = own // 2
    for core, parts in ((side, refs[:nodes]), (1 - side, refs[nodes : 2 * nodes])):
        for step in range(nodes):
            grads[pl.ds((me ^ step) * own + core * half, half)] = parts[step][...].astype(f32)

    def through(two, weights, exact):
        rows = []
        for x in two:
            high = x.astype(bf16)
            low = (x - high.astype(f32)).astype(bf16)
            rows.append(jnp.concatenate([high, high], axis=1) if exact else high)
            rows.append(jnp.concatenate([low, jnp.zeros_like(low)], axis=1) if exact else low)
        out = jnp.dot(jnp.concatenate(rows, axis=0), weights, preferred_element_type=f32)
        n = two[0].shape[0]
        return [
            out[2 * q * n : (2 * q + 1) * n, q * 128 : (q + 1) * 128]
            + out[(2 * q + 1) * n : (2 * q + 2) * n, q * 128 : (q + 1) * 128]
            for q in range(2)
        ]

    def start(pair, _):
        done = through([grads[2 * pair], grads[2 * pair + 1]], high_ref[pair], False)
        for q in range(2):
            values0[2 * pair + q] = done[q].astype(bf16)
        return 0

    lax.fori_loop(0, pairs, start, 0, unroll=min(pairs, 16))

    def rest(old, pair):
        near = []
        for q in range(2):
            c = 2 * pair + q
            near.append(
                jnp.concatenate(
                    [old[near_ref[c // own, k, c % own]] for k in range(coupled)], axis=1
                )
            )
        n = near[0].shape[0]
        coupling = jnp.dot(
            jnp.concatenate(near, axis=0), phi_ref[pair], preferred_element_type=f32
        )
        return [
            grads[2 * pair + q] - coupling[q * n : (q + 1) * n, q * 128 : (q + 1) * 128]
            for q in range(2)
        ]

    old, new = values0, values1
    for sweep in range(SWEEPS - 1):

        def left_over(pair, _, old=old):
            two = rest(old, pair)
            for q in range(2):
                sums[2 * pair + q] = two[q]
            return 0

        def apply(pair, _, new=new):
            done = through([sums[2 * pair], sums[2 * pair + 1]], high_ref[pair], False)
            for q in range(2):
                new[2 * pair + q] = done[q].astype(bf16)
            return 0

        lax.fori_loop(0, pairs, left_over, 0, unroll=min(pairs, 16))
        lax.fori_loop(0, pairs, apply, 0, unroll=min(pairs, 16))
        old, new = new, old

    first = me * half
    last = [rest(old, first + pair) for pair in range(half)]
    for pair in range(half):
        weights = jnp.concatenate([high_ref[first + pair], low_ref[pair]], axis=0)
        done = through(last[pair], weights, True)
        for q in range(2):
            grad_out[2 * pair + q] = grads[2 * (first + pair) + q]
            adjoint_out[2 * pair + q] = done[q]


def exchange(x, axis, size, step):
    return lax.ppermute(x, axis, [(i, i ^ step) for i in range(size)])


def across(x, nodes, fns, step, turn):
    pairs = [(n * fns + f, (n ^ step) * fns + (f ^ turn)) for n in range(nodes) for f in range(fns)]
    return lax.ppermute(x, ("node", "fn"), pairs)


def local(sizes, volume_grad, volume_coords, support, control_coords, neighbours, block_inverse):
    nodes, fns, subs = sizes["node"], sizes["fn"], sizes["sub"]
    blocks, funcs, width = volume_grad.shape
    own, coupled = neighbours.shape
    controls = own * nodes
    depth = -(-(controls + GEO) // 128) * 128
    side = lax.axis_index("sub").astype(jnp.int32).reshape(1)
    me = lax.axis_index("node").astype(jnp.int32).reshape(1)

    def hbm(x):
        return pltpu.with_memory_space_constraint(x, pltpu.HBM)

    operands = [
        hbm(x)
        for x in (
            volume_coords.transpose(1, 0, 2),
            support.T,
            volume_grad,
            control_coords.transpose(1, 0, 2),
            block_inverse,
            neighbours.T,
        )
    ]
    half = own // 2
    left, counts, grads, parcel = call(
        functools.partial(prepare_kernel, controls),
        "prepare",
        [
            shape((blocks, width, depth), bf16),
            shape((blocks, depth), f32),
            shape(volume_grad.shape, volume_grad.dtype),
            shape((half * width + 10 * own, width), bf16),
        ],
        [
            pltpu.VMEM((3, blocks, width), f32),
            pltpu.VMEM(support.T.shape, jnp.int32),
            pltpu.VMEM((blocks * GEO, width), f32),
            pltpu.VMEM((depth, width), f32),
            pltpu.VMEM((half, width, width), f32),
            pltpu.VMEM((3, own, width), f32),
            pltpu.VMEM((coupled, own), jnp.int32),
            pltpu.SemaphoreType.DMA((6,)),
        ],
        [side, *operands],
        [SMEM] + [HBM] * 6,
    )
    parcels = [parcel] + [exchange(parcel, "node", nodes, step) for step in range(1, nodes)]

    def evaluate(nodes_done, after):
        per = own * len(nodes_done)
        entries = blocks * per * width * width
        operands = [side, me, left, grads, counts, *(parcels[step] for step in nodes_done)]
        return call(
            functools.partial(chunk_kernel, nodes_done, support.shape[1]),
            f"evaluate_{nodes_done[0]}",
            [shape((per // 2, funcs, width), f32)] * 2,
            [
                pltpu.VMEM((per * GEO, width), f32),
                pltpu.VMEM((per // 2, depth, 2 * width), bf16),
                pltpu.VMEM((blocks, width, depth), bf16),
                pltpu.VMEM((per // 2, funcs, 2 * width), f32),
                pltpu.VMEM((per // 2, funcs, 2 * width), f32),
                pltpu.VMEM((TILE * width, 2 * width), f32),
                pltpu.VMEM((TILE * width, 2 * width), f32),
                pltpu.VMEM((TILE * width, 2 * width), bf16),
                pltpu.VMEM((TILE * width, 2 * width), bf16),
            ],
            operands + after,
            [SMEM, SMEM] + [VMEM] * (len(operands) - 2) + [ANY] * len(after),
            pl.CostEstimate(flops=entries * 400, bytes_accessed=4 << 20, transcendentals=entries),
        )

    def add(terms, after=(), parts=1, kinds=(f32,)):
        dims = (terms[0].shape[0] // parts,) + terms[0].shape[1:]
        done = call(
            functools.partial(sum_kernel, len(terms), parts * len(kinds)),
            "sum",
            [shape(dims, kind) for kind in kinds for _ in range(parts)],
            [],
            [*terms, *after],
            [VMEM] * len(terms) + [ANY] * len(after),
        )
        return done if len(done) > 1 else done[0]

    def join(pieces, after):
        rows = sum(x.shape[0] for x in pieces)
        return call(
            functools.partial(join_kernel, len(pieces)),
            "join",
            [shape((rows,) + pieces[0].shape[1:], pieces[0].dtype)],
            [],
            [*pieces, *after],
            [VMEM] * len(pieces) + [ANY] * len(after),
        )[0]

    far = list(range(nodes - 1, 1, -1))
    keep, send = evaluate([0], [])
    kept, sent = evaluate(far, [send])
    others = exchange(join(parcels[1:], []), "sub", subs, 1)
    swapped = exchange(sent, "sub", subs, 1)
    operands = [side, me, hbm(block_inverse), *parcels, others]
    control_left, control_right, high, low, near = call(
        functools.partial(features_kernel, nodes),
        "control_features",
        [
            shape((controls, width, GEO), bf16),
            shape((controls, GEO, width), bf16),
            shape((controls // 2, width, 2 * width), bf16),
            shape((half, width, 2 * width), bf16),
            shape((nodes, own, width), jnp.int32),
        ],
        [
            pltpu.VMEM((3, nodes, own, width), f32),
            pltpu.VMEM((controls * GEO, width), f32),
            pltpu.VMEM((controls * GEO, width), f32),
            pltpu.VMEM((own, width, width), f32),
            pltpu.SemaphoreType.DMA((1,)),
        ],
        operands + [sent],
        [SMEM, SMEM, HBM] + [VMEM] * (nodes + 1) + [ANY],
        pl.CostEstimate(flops=10 << 30, bytes_accessed=1 << 20, transcendentals=0),
    )
    held = add([keep, exchange(send, "sub", subs, 1)], [sent])
    parts = add([kept, swapped], [high], parts=len(far))
    arrived = [exchange(x, "node", nodes, step) for step, x in zip(far, parts)]
    kept, sent = evaluate([1], [*parts, held])
    held = add([held, *arrived], [sent])
    part = add([kept, exchange(sent, "sub", subs, 1)], [held])
    terms = [held] + [exchange(held, "fn", fns, turn) for turn in range(1, fns)]
    terms += [exchange(part, "node", nodes, 1)]
    terms += [across(part, nodes, fns, 1, turn) for turn in range(1, fns)]

    cuts = [0, 3 * controls // 8, controls // 2]

    def couple(low_pair, high_pair, before, after):
        operands = [near, control_left, control_right, *before]
        return call(
            functools.partial(pairs_kernel, low_pair, high_pair),
            f"pairs_{low_pair}",
            [shape((controls // 2, coupled * width, 2 * width), bf16)],
            [
                pltpu.VMEM((coupled * width, 2 * width), f32),
                pltpu.VMEM((coupled * width, 2 * width), f32),
            ],
            [*operands, *after],
            [SMEM] + [VMEM] * (len(operands) - 1) + [ANY] * len(after),
            pl.CostEstimate(flops=10 << 30, bytes_accessed=1 << 20, transcendentals=1 << 20),
            {3: 0} if before else None,
        )[0]

    phi = couple(cuts[0], cuts[1], [], [part])
    held, rounded = add(terms, [phi], kinds=(f32, bf16))
    pieces = [exchange(rounded, "node", nodes, step) for step in range(1, nodes)]
    phi = couple(cuts[1], cuts[2], [phi], [rounded])
    mine = [held] + [join([x], [phi]) for x in pieces]
    theirs = [exchange(x, "sub", subs, 1) for x in mine]
    return tuple(
        call(
            functools.partial(solve_kernel, nodes),
            "solve",
            [shape((own, funcs, width), f32)] * 2,
            [
                pltpu.VMEM((controls, funcs, width), f32),
                pltpu.VMEM((controls, funcs, width), f32),
                pltpu.VMEM((controls, funcs, width), bf16),
                pltpu.VMEM((controls, funcs, width), bf16),
            ],
            [side, me, near, *mine, *theirs, phi, high, low],
            [SMEM, SMEM, SMEM] + [VMEM] * (2 * nodes + 3),
        )
    )


def solution(mesh):
    return jax.shard_map(
        functools.partial(local, dict(mesh.shape)),
        mesh=mesh,
        in_specs=(
            P(("sect", "node", "fn", "sub"), None, None),
            P(("sect", "node", "fn", "sub"), None, None),
            P(("sect", "node", "fn", "sub"), None),
            P(("sect", "node"), None, None),
            P(("sect", "node"), None),
            P(("sect", "node"), None, None),
        ),
        out_specs=(P(("sect", "node"), None, None), P(("sect", "node"), None, None)),
        check_vma=False,
    )
```

```python
import functools
import math

import jax
import jax.numpy as jnp
from jax import lax
from jax.experimental import pallas as pl
from jax.experimental.pallas import tpu as pltpu
from jax.sharding import PartitionSpec as P

SWEEPS = 2
RADIUS = 1.2
C = 4.0**0.2
SCALE = C / RADIUS
GEO = 32
TILE = 4
STEPS = 16
f32, bf16 = jnp.float32, jnp.bfloat16
VMEM = pl.BlockSpec(memory_space=pltpu.VMEM)
SMEM = pl.BlockSpec(memory_space=pltpu.SMEM)
ANY = pl.BlockSpec(memory_space=pl.ANY)
HBM = pl.BlockSpec(memory_space=pltpu.HBM)


def call(kernel, name, out, scratch, operands, specs, cost=None, aliases=None):
    size = 0
    for x in [*out, *scratch, *operands]:
        if len(x.shape) < 2:
            continue
        size += math.prod(x.shape[:-1]) * max(x.shape[-1], 128) * jnp.dtype(x.dtype).itemsize
    return pl.pallas_call(
        kernel,
        out_shape=out,
        in_specs=specs,
        out_specs=[VMEM] * len(out),
        scratch_shapes=scratch,
        compiler_params=pltpu.CompilerParams(vmem_limit_bytes=size + (4 << 20)),
        cost_estimate=cost,
        input_output_aliases=aliases or {},
        name=name,
    )(*operands)


def shape(dims, kind):
    return jax.ShapeDtypeStruct(dims, kind)


def weight_of(square, safe):
    square = jnp.maximum(square, 1e-12) if safe else square
    root = square * lax.rsqrt(square)
    inside = jnp.maximum(C - root, 0.0)
    twice = inside * inside
    return ((twice * twice) * (0.25 * C + root)).astype(bf16)


def split3(v):
    a = v.astype(bf16).astype(f32)
    b = (v - a).astype(bf16).astype(f32)
    return (a, b, v - a - b)


def pairs_of_parts():
    return [(a, b) for a in range(3) for b in range(3) if a + b < 4]


def left_rows(xyz):
    rows = []
    for v in xyz:
        parts = split3(v)
        rows += [parts[a] for a, b in pairs_of_parts()]
    rows += list(split3(sum(v * v for v in xyz)))
    return rows + [jnp.ones_like(xyz[0])] * 3


def right_rows(xyz):
    rows = []
    for v in xyz:
        parts = split3(v)
        rows += [-2.0 * parts[b] for a, b in pairs_of_parts()]
    rows += [jnp.ones_like(xyz[0])] * 3
    return rows + list(split3(sum(v * v for v in xyz)))


def told(ref, count):
    rows = ref[ref.shape[0] - 10 * count :].astype(f32)
    part = [rows[n * count : (n + 1) * count] for n in range(10)]
    xyz = [((part[3 * d + 2] + part[3 * d + 1]) + part[3 * d]) * SCALE for d in range(3)]
    return xyz, part[9]


def fill_rows(scratch, rows, first=0):
    blocks = scratch.shape[0] // (GEO + 1)
    n = rows[0].shape[0]
    for g in range(GEO):
        row = rows[g] if g < len(rows) else jnp.zeros_like(rows[0])
        scratch[g * blocks + first : g * blocks + first + n] = row


def rows_of(scratch, block):
    return scratch[pl.ds(block, GEO, stride=scratch.shape[0] // (GEO + 1)), :]


def far_of(counts_ref, s, b):
    bits = lax.shift_right_logical(counts_ref[pl.ds(s, 1), :].astype(jnp.int32), b)
    return jnp.where(jnp.bitwise_and(bits, 1) == 1, 0.0, 65536.0)


def prepare_kernel(
    controls, side_ref, volume_hbm, listed_hbm, grad_hbm, control_hbm, inverse_hbm, near_hbm, *refs
):
    left_ref, counts_ref, grad_ref, parcel_ref = refs[:4]
    coords, listed, scratch, tally, inverse, control, near, sems = refs[4:]
    half = inverse.shape[0]
    own = 2 * half
    mine = pl.ds(side_ref[0] * half, half)
    copies = [
        pltpu.make_async_copy(source, target, sems.at[n])
        for n, (source, target) in enumerate(
            [
                (volume_hbm, coords),
                (listed_hbm, listed),
                (inverse_hbm.at[mine], inverse),
                (near_hbm, near),
                (control_hbm, control),
                (grad_hbm, grad_ref),
            ]
        )
    ]
    for copy in copies:
        copy.start()
    blocks, width, depth = left_ref.shape
    copies[1].wait()
    chosen = listed[...]
    tally[...] = jnp.zeros_like(tally)
    for c in range(controls):
        tally[GEO + c : GEO + c + 1, 0:blocks] = jnp.sum(
            jnp.where(chosen == c, 1.0, 0.0), axis=0, keepdims=True
        )
    counts_ref[...] = tally[...].T[0:blocks]
    copies[0].wait()
    fill_rows(scratch, left_rows([coords[d] * SCALE for d in range(3)]))
    lane = lax.broadcasted_iota(jnp.int32, (width, depth), 1)

    def one(s, _):
        turned = rows_of(scratch, s).T
        turned = jnp.concatenate([turned, jnp.zeros((width, depth - GEO), f32)], axis=1)
        left_ref[s] = jnp.where(lane < GEO, turned, far_of(counts_ref, s, 0)).astype(bf16)
        return 0

    lax.fori_loop(0, blocks, one, 0, unroll=8)
    for copy in copies[2:]:
        copy.wait()
    for q in range(half):
        parcel_ref[q * 128 : (q + 1) * 128] = inverse[q].astype(bf16)
    rows = [part for d in range(3) for part in split3(control[d])]
    numbers = near[...].astype(f32)
    numbers = jnp.concatenate([numbers, jnp.zeros((near.shape[0], width - own), f32)], axis=1)
    rows.append(jnp.concatenate([numbers, jnp.zeros((own - near.shape[0], width), f32)], axis=0))
    parcel_ref[half * 128 :] = jnp.concatenate(rows, axis=0).astype(bf16)


def chunk_kernel(nodes_done, listed, *refs):
    side_ref, me_ref, left_ref, grad_ref, counts_ref = refs[:5]
    parcels = refs[5 : 5 + len(nodes_done)]
    keep_ref, send_ref, features, rhs, again_left, total, result, d0, d1, p0, p1 = refs[-11:]
    blocks = grad_ref.shape[0]
    per = features.shape[0] // (GEO + 1)
    own = per // len(nodes_done)
    depth = rhs.shape[1]
    steps = blocks // TILE
    pairs = per // 2
    whole = pairs * steps
    size = TILE * 128
    result[...] = jnp.zeros_like(result)
    for n, parcel in enumerate(parcels):
        fill_rows(features, right_rows(told(parcel, own)[0]), n * own)
    row = lax.broadcasted_iota(jnp.int32, (depth - GEO, 128), 0)
    for c in range(per):
        at = (c % 2) * 128
        place = (me_ref[0] ^ nodes_done[c // own]) * own + c % own
        rhs[c // 2, 0:GEO, at : at + 128] = rows_of(features, c).astype(bf16)
        rhs[c // 2, GEO:, at : at + 128] = jnp.where(row == place, 1.0, 0.0).astype(bf16)

    def distances(lefts, t, d):
        j, i = t // steps, t % steps
        left = lefts[pl.ds(i * TILE, TILE)].reshape(size, depth)
        d[...] = jnp.dot(left, rhs[j], preferred_element_type=f32)

    def values(d, p, safe):
        p[...] = weight_of(d[...], safe)

    def products(t, p):
        j, i = t // steps, t % steps
        g = jnp.concatenate([grad_ref[i * TILE + q] for q in range(TILE)], axis=1)
        total[j] += jnp.dot(g, p[...], preferred_element_type=f32)

    def layer(lefts, safe, turns, weight):
        total[...] = jnp.zeros_like(total)
        p1[...] = jnp.zeros_like(p1)
        distances(lefts, 0, d0)

        def turn(h, _):
            for u in range(turns):
                t = turns * h + u
                d, p = (d0, p0) if u % 2 == 0 else (d1, p1)
                later, done = (d1, p1) if u % 2 == 0 else (d0, p0)
                values(d, p, safe)
                distances(lefts, jnp.minimum(t + 1, whole - 1), later)
                products(jnp.maximum(t - 1, 0), done)
            return 0

        lax.fori_loop(0, whole // turns, turn, 0)
        products(whole - 1, p1)
        result[...] += weight * total[...]

    layer(left_ref, False, STEPS, 1.0)
    failed = jnp.max(jnp.where(result[...] != result[...], 1, 0))
    most = jnp.max(counts_ref[...])
    layers = jnp.int32(0)
    for b in range(listed.bit_length()):
        layers = layers + jnp.where(most >= float(1 << b), 1, 0)
    failed = jnp.maximum(failed, jnp.where(layers > 1, 1, 0))

    def bit(b, weight):
        def renew(s, _):
            lane = lax.broadcasted_iota(jnp.int32, (128, depth), 1)
            kept = left_ref[s].astype(f32)
            again_left[s] = jnp.where(lane < GEO, kept, far_of(counts_ref, s, b)).astype(bf16)
            return 0

        lax.fori_loop(0, blocks, renew, 0)
        layer(again_left, True, 2, weight)
        return weight * 2.0

    def again(_, carry):
        result[...] = jnp.zeros_like(result)
        lax.fori_loop(0, layers, bit, jnp.float32(1.0))
        return carry

    lax.fori_loop(0, failed, again, 0)
    side = side_ref[0]
    half = own // 4
    for n in range(len(nodes_done)):
        for j in range(half):
            mine = result[n * 2 * half + side * half + j]
            other = result[n * 2 * half + (1 - side) * half + j]
            for q in range(2):
                keep_ref[n * 2 * half + 2 * j + q] = mine[:, q * 128 : (q + 1) * 128]
                send_ref[n * 2 * half + 2 * j + q] = other[:, q * 128 : (q + 1) * 128]


def features_kernel(nodes, side_ref, me_ref, inverse_hbm, *refs):
    parcels = refs[:nodes]
    others = refs[nodes]
    rows_each = parcels[0].shape[0]
    left_ref, right_ref, high_ref, low_ref, near_ref = refs[-10:-5]
    coords, features, rows, inverse, sem = refs[-5:]
    copy = pltpu.make_async_copy(inverse_hbm, inverse, sem.at[0])
    copy.start()
    own = inverse.shape[0]
    half = own // 2
    side, me = side_ref[0], me_ref[0]
    for step in range(nodes):
        xyz, numbers = told(parcels[step], own)
        for d in range(3):
            coords[d, me ^ step] = xyz[d]
        near_ref[me ^ step] = numbers.astype(jnp.int32)
    for step in range(1, nodes):
        for core, parcel in (
            (side, parcels[step]),
            (1 - side, others.at[(step - 1) * rows_each : step * rows_each]),
        ):
            for c in range(half):
                pair = (me ^ step) * half + core * (half // 2) + c // 2
                at = (c % 2) * 128
                high_ref[pair, :, at : at + 128] = parcel[c * 128 : (c + 1) * 128]
    blocks = left_ref.shape[0]
    xyz = [coords[d].reshape(blocks, 128) for d in range(3)]
    fill_rows(features, right_rows(xyz))
    fill_rows(rows, left_rows(xyz))

    def turn_left(c, _):
        left_ref[c] = rows_of(rows, c).T.astype(bf16)
        right_ref[c] = rows_of(features, c).astype(bf16)
        return 0

    lax.fori_loop(0, blocks, turn_left, 0, unroll=8)
    copy.wait()
    for c in range(own):
        inv = inverse[c]
        high = inv.astype(bf16)
        at = (c % 2) * 128
        high_ref[me * half + c // 2, :, at : at + 128] = high
        low_ref[c // 2, :, at : at + 128] = (inv - high.astype(f32)).astype(bf16)


def pairs_kernel(low, high, near_ref, left_ref, right_ref, *refs):
    phi_ref, d0, d1 = refs[-3:]
    own = near_ref.shape[1]
    coupled = phi_ref.shape[1] // 128

    def distances(pair, d):
        for q in range(2):
            c = 2 * pair + q
            points = [left_ref[near_ref[c // own, k, c % own]] for k in range(coupled)]
            d[:, q * 128 : (q + 1) * 128] = jnp.dot(
                jnp.concatenate(points, axis=0), right_ref[c], preferred_element_type=f32
            )

    distances(low, d0)
    turns = high - low if high - low <= 12 else 4

    def turn(h, _):
        for u in range(turns):
            pair = low + turns * h + u
            d, later = (d0, d1) if u % 2 == 0 else (d1, d0)
            phi_ref[pair] = weight_of(d[...], True)
            distances(jnp.minimum(pair + 1, high - 1), later)
        return 0

    lax.fori_loop(0, (high - low) // turns, turn, 0)


def sum_kernel(count, made, *refs):
    terms = [x[...] for x in refs[:count]]
    while len(terms) > 1:
        terms = [sum(terms[n + 1 : n + 2], terms[n]) for n in range(0, len(terms), 2)]
    (total,) = terms
    at = 0
    for out in refs[len(refs) - made :]:
        if at == total.shape[0]:
            at = 0
        n = out.shape[0]
        out[...] = total[at : at + n].astype(out.dtype)
        at += n


def join_kernel(count, *refs):
    out = refs[-1]
    at = 0
    for piece in refs[:count]:
        out[at : at + piece.shape[0]] = piece[...]
        at += piece.shape[0]


def solve_kernel(nodes, side_ref, me_ref, near_ref, *refs):
    phi_ref, high_ref, low_ref, grad_out, adjoint_out, grads, sums, values0, values1 = refs[2 * nodes :]
    pairs = high_ref.shape[0]
    own = near_ref.shape[1]
    coupled = phi_ref.shape[1] // 128
    side, me = side_ref[0], me_ref[0]
    half = own // 2
    for core, parts in ((side, refs[:nodes]), (1 - side, refs[nodes : 2 * nodes])):
        for step in range(nodes):
            grads[pl.ds((me ^ step) * own + core * half, half)] = parts[step][...].astype(f32)

    def through(two, weights, exact):
        rows = []
        for x in two:
            high = x.astype(bf16)
            low = (x - high.astype(f32)).astype(bf16)
            rows.append(jnp.concatenate([high, high], axis=1) if exact else high)
            rows.append(jnp.concatenate([low, jnp.zeros_like(low)], axis=1) if exact else low)
        out = jnp.dot(jnp.concatenate(rows, axis=0), weights, preferred_element_type=f32)
        n = two[0].shape[0]
        return [
            out[2 * q * n : (2 * q + 1) * n, q * 128 : (q + 1) * 128]
            + out[(2 * q + 1) * n : (2 * q + 2) * n, q * 128 : (q + 1) * 128]
            for q in range(2)
        ]

    def start(pair, _):
        done = through([grads[2 * pair], grads[2 * pair + 1]], high_ref[pair], False)
        for q in range(2):
            values0[2 * pair + q] = done[q].astype(bf16)
        return 0

    lax.fori_loop(0, pairs, start, 0, unroll=min(pairs, 16))

    def rest(old, pair):
        near = []
        for q in range(2):
            c = 2 * pair + q
            near.append(
                jnp.concatenate(
                    [old[near_ref[c // own, k, c % own]] for k in range(coupled)], axis=1
                )
            )
        n = near[0].shape[0]
        coupling = jnp.dot(
            jnp.concatenate(near, axis=0), phi_ref[pair], preferred_element_type=f32
        )
        return [
            grads[2 * pair + q] - coupling[q * n : (q + 1) * n, q * 128 : (q + 1) * 128]
            for q in range(2)
        ]

    old, new = values0, values1
    for sweep in range(SWEEPS - 1):

        def left_over(pair, _, old=old):
            two = rest(old, pair)
            for q in range(2):
                sums[2 * pair + q] = two[q]
            return 0

        def apply(pair, _, new=new):
            done = through([sums[2 * pair], sums[2 * pair + 1]], high_ref[pair], False)
            for q in range(2):
                new[2 * pair + q] = done[q].astype(bf16)
            return 0

        lax.fori_loop(0, pairs, left_over, 0, unroll=min(pairs, 16))
        lax.fori_loop(0, pairs, apply, 0, unroll=min(pairs, 16))
        old, new = new, old

    first = me * half
    last = [rest(old, first + pair) for pair in range(half)]
    for pair in range(half):
        weights = jnp.concatenate([high_ref[first + pair], low_ref[pair]], axis=0)
        done = through(last[pair], weights, True)
        for q in range(2):
            grad_out[2 * pair + q] = grads[2 * (first + pair) + q]
            adjoint_out[2 * pair + q] = done[q]


def exchange(x, axis, size, step):
    return lax.ppermute(x, axis, [(i, i ^ step) for i in range(size)])


def across(x, nodes, fns, step, turn):
    pairs = [(n * fns + f, (n ^ step) * fns + (f ^ turn)) for n in range(nodes) for f in range(fns)]
    return lax.ppermute(x, ("node", "fn"), pairs)


def local(sizes, volume_grad, volume_coords, support, control_coords, neighbours, block_inverse):
    nodes, fns, subs = sizes["node"], sizes["fn"], sizes["sub"]
    blocks, funcs, width = volume_grad.shape
    own, coupled = neighbours.shape
    controls = own * nodes
    depth = -(-(controls + GEO) // 128) * 128
    side = lax.axis_index("sub").astype(jnp.int32).reshape(1)
    me = lax.axis_index("node").astype(jnp.int32).reshape(1)

    def hbm(x):
        return pltpu.with_memory_space_constraint(x, pltpu.HBM)

    operands = [
        hbm(x)
        for x in (
            volume_coords.transpose(1, 0, 2),
            support.T,
            volume_grad,
            control_coords.transpose(1, 0, 2),
            block_inverse,
            neighbours.T,
        )
    ]
    half = own // 2
    left, counts, grads, parcel = call(
        functools.partial(prepare_kernel, controls),
        "prepare",
        [
            shape((blocks, width, depth), bf16),
            shape((blocks, depth), f32),
            shape(volume_grad.shape, volume_grad.dtype),
            shape((half * width + 10 * own, width), bf16),
        ],
        [
            pltpu.VMEM((3, blocks, width), f32),
            pltpu.VMEM(support.T.shape, jnp.int32),
            pltpu.VMEM((blocks * (GEO + 1), width), f32),
            pltpu.VMEM((depth, width), f32),
            pltpu.VMEM((half, width, width), f32),
            pltpu.VMEM((3, own, width), f32),
            pltpu.VMEM((coupled, own), jnp.int32),
            pltpu.SemaphoreType.DMA((6,)),
        ],
        [side, *operands],
        [SMEM] + [HBM] * 6,
    )
    parcels = [parcel] + [exchange(parcel, "node", nodes, step) for step in range(1, nodes)]

    def evaluate(nodes_done, after):
        per = own * len(nodes_done)
        entries = blocks * per * width * width
        operands = [side, me, left, grads, counts, *(parcels[step] for step in nodes_done)]
        return call(
            functools.partial(chunk_kernel, nodes_done, support.shape[1]),
            f"evaluate_{nodes_done[0]}",
            [shape((per // 2, funcs, width), f32)] * 2,
            [
                pltpu.VMEM((per * (GEO + 1), width), f32),
                pltpu.VMEM((per // 2, depth, 2 * width), bf16),
                pltpu.VMEM((blocks, width, depth), bf16),
                pltpu.VMEM((per // 2, funcs, 2 * width), f32),
                pltpu.VMEM((per // 2, funcs, 2 * width), f32),
                pltpu.VMEM((TILE * width, 2 * width), f32),
                pltpu.VMEM((TILE * width, 2 * width), f32),
                pltpu.VMEM((TILE * width, 2 * width), bf16),
                pltpu.VMEM((TILE * width, 2 * width), bf16),
            ],
            operands + after,
            [SMEM, SMEM] + [VMEM] * (len(operands) - 2) + [ANY] * len(after),
            pl.CostEstimate(flops=entries * 400, bytes_accessed=4 << 20, transcendentals=entries),
        )

    def add(terms, after=(), parts=1, kinds=(f32,)):
        dims = (terms[0].shape[0] // parts,) + terms[0].shape[1:]
        done = call(
            functools.partial(sum_kernel, len(terms), parts * len(kinds)),
            "sum",
            [shape(dims, kind) for kind in kinds for _ in range(parts)],
            [],
            [*terms, *after],
            [VMEM] * len(terms) + [ANY] * len(after),
        )
        return done if len(done) > 1 else done[0]

    def join(pieces, after):
        rows = sum(x.shape[0] for x in pieces)
        return call(
            functools.partial(join_kernel, len(pieces)),
            "join",
            [shape((rows,) + pieces[0].shape[1:], pieces[0].dtype)],
            [],
            [*pieces, *after],
            [VMEM] * len(pieces) + [ANY] * len(after),
        )[0]

    far = list(range(nodes - 1, 1, -1))
    keep, send = evaluate([0], [])
    kept, sent = evaluate(far, [send])
    others = exchange(join(parcels[1:], []), "sub", subs, 1)
    swapped = exchange(sent, "sub", subs, 1)
    operands = [side, me, hbm(block_inverse), *parcels, others]
    control_left, control_right, high, low, near = call(
        functools.partial(features_kernel, nodes),
        "control_features",
        [
            shape((controls, width, GEO), bf16),
            shape((controls, GEO, width), bf16),
            shape((controls // 2, width, 2 * width), bf16),
            shape((half, width, 2 * width), bf16),
            shape((nodes, own, width), jnp.int32),
        ],
        [
            pltpu.VMEM((3, nodes, own, width), f32),
            pltpu.VMEM((controls * (GEO + 1), width), f32),
            pltpu.VMEM((controls * (GEO + 1), width), f32),
            pltpu.VMEM((own, width, width), f32),
            pltpu.SemaphoreType.DMA((1,)),
        ],
        operands + [sent],
        [SMEM, SMEM, HBM] + [VMEM] * (nodes + 1) + [ANY],
        pl.CostEstimate(flops=10 << 30, bytes_accessed=1 << 20, transcendentals=0),
    )
    held = add([keep, exchange(send, "sub", subs, 1)], [sent])
    parts = add([kept, swapped], [high], parts=len(far))
    arrived = [exchange(x, "node", nodes, step) for step, x in zip(far, parts)]
    kept, sent = evaluate([1], [*parts, held])
    held = add([held, *arrived], [sent])
    part = add([kept, exchange(sent, "sub", subs, 1)], [held])
    terms = [held] + [exchange(held, "fn", fns, turn) for turn in range(1, fns)]
    terms += [exchange(part, "node", nodes, 1)]
    terms += [across(part, nodes, fns, 1, turn) for turn in range(1, fns)]

    cuts = [0, 3 * controls // 8, controls // 2]

    def couple(low_pair, high_pair, before, after):
        operands = [near, control_left, control_right, *before]
        return call(
            functools.partial(pairs_kernel, low_pair, high_pair),
            f"pairs_{low_pair}",
            [shape((controls // 2, coupled * width, 2 * width), bf16)],
            [
                pltpu.VMEM((coupled * width, 2 * width), f32),
                pltpu.VMEM((coupled * width, 2 * width), f32),
            ],
            [*operands, *after],
            [SMEM] + [VMEM] * (len(operands) - 1) + [ANY] * len(after),
            pl.CostEstimate(flops=10 << 30, bytes_accessed=1 << 20, transcendentals=1 << 20),
            {3: 0} if before else None,
        )[0]

    phi = couple(cuts[0], cuts[1], [], [part])
    held, rounded = add(terms, [phi], kinds=(f32, bf16))
    pieces = [exchange(rounded, "node", nodes, step) for step in range(1, nodes)]
    phi = couple(cuts[1], cuts[2], [phi], [rounded])
    mine = [held] + [join([x], [phi]) for x in pieces]
    theirs = [exchange(x, "sub", subs, 1) for x in mine]
    return tuple(
        call(
            functools.partial(solve_kernel, nodes),
            "solve",
            [shape((own, funcs, width), f32)] * 2,
            [
                pltpu.VMEM((controls, funcs, width), f32),
                pltpu.VMEM((controls, funcs, width), f32),
                pltpu.VMEM((controls, funcs, width), bf16),
                pltpu.VMEM((controls, funcs, width), bf16),
            ],
            [side, me, near, *mine, *theirs, phi, high, low],
            [SMEM, SMEM, SMEM] + [VMEM] * (2 * nodes + 3),
        )
    )


def solution(mesh):
    return jax.shard_map(
        functools.partial(local, dict(mesh.shape)),
        mesh=mesh,
        in_specs=(
            P(("sect", "node", "fn", "sub"), None, None),
            P(("sect", "node", "fn", "sub"), None, None),
            P(("sect", "node", "fn", "sub"), None),
            P(("sect", "node"), None, None),
            P(("sect", "node"), None),
            P(("sect", "node"), None, None),
        ),
        out_specs=(P(("sect", "node"), None, None), P(("sect", "node"), None, None)),
        check_vma=False,
    )
```

```python
import functools
import math

import jax
import jax.numpy as jnp
from jax import lax
from jax.experimental import pallas as pl
from jax.experimental.pallas import tpu as pltpu
from jax.sharding import PartitionSpec as P

SWEEPS = 2
RADIUS = 1.2
C = 4.0**0.2
SCALE = C / RADIUS
GEO = 32
TILE = 4
STEPS = 16
f32, bf16 = jnp.float32, jnp.bfloat16
VMEM = pl.BlockSpec(memory_space=pltpu.VMEM)
SMEM = pl.BlockSpec(memory_space=pltpu.SMEM)
ANY = pl.BlockSpec(memory_space=pl.ANY)
HBM = pl.BlockSpec(memory_space=pltpu.HBM)


def call(kernel, name, out, scratch, operands, specs, cost=None, aliases=None):
    size = 0
    for x in [*out, *scratch, *operands]:
        if len(x.shape) < 2:
            continue
        size += math.prod(x.shape[:-1]) * max(x.shape[-1], 128) * jnp.dtype(x.dtype).itemsize
    return pl.pallas_call(
        kernel,
        out_shape=out,
        in_specs=specs,
        out_specs=[VMEM] * len(out),
        scratch_shapes=scratch,
        compiler_params=pltpu.CompilerParams(vmem_limit_bytes=size + (4 << 20)),
        cost_estimate=cost,
        input_output_aliases=aliases or {},
        name=name,
    )(*operands)


def shape(dims, kind):
    return jax.ShapeDtypeStruct(dims, kind)


def weight_of(square, safe):
    square = jnp.maximum(square, 1e-12) if safe else square
    root = square * lax.rsqrt(square)
    inside = jnp.maximum(C - root, 0.0)
    twice = inside * inside
    return ((twice * twice) * (0.25 * C + root)).astype(bf16)


def split3(v):
    a = v.astype(bf16).astype(f32)
    b = (v - a).astype(bf16).astype(f32)
    return (a, b, v - a - b)


def pairs_of_parts():
    return [(a, b) for a in range(3) for b in range(3) if a + b < 4]


def left_rows(xyz):
    rows = []
    for v in xyz:
        parts = split3(v)
        rows += [parts[a] for a, b in pairs_of_parts()]
    rows += list(split3(sum(v * v for v in xyz)))
    return rows + [jnp.ones_like(xyz[0])] * 3


def right_rows(xyz):
    rows = []
    for v in xyz:
        parts = split3(v)
        rows += [-2.0 * parts[b] for a, b in pairs_of_parts()]
    rows += [jnp.ones_like(xyz[0])] * 3
    return rows + list(split3(sum(v * v for v in xyz)))


def told(ref, count):
    rows = ref[ref.shape[0] - 10 * count :].astype(f32)
    part = [rows[n * count : (n + 1) * count] for n in range(10)]
    xyz = [((part[3 * d + 2] + part[3 * d + 1]) + part[3 * d]) * SCALE for d in range(3)]
    return xyz, part[9]


def fill_rows(scratch, rows, first=0):
    blocks = scratch.shape[0] // (GEO + 1)
    n = rows[0].shape[0]
    for g in range(GEO):
        row = rows[g] if g < len(rows) else jnp.zeros_like(rows[0])
        scratch[g * blocks + first : g * blocks + first + n] = row


def rows_of(scratch, block):
    return scratch[pl.ds(block, GEO, stride=scratch.shape[0] // (GEO + 1)), :]


def far_of(counts_ref, s, b):
    bits = lax.shift_right_logical(counts_ref[pl.ds(s, 1), :].astype(jnp.int32), b)
    return jnp.where(jnp.bitwise_and(bits, 1) == 1, 0.0, 65536.0)


def prepare_kernel(
    controls, side_ref, volume_hbm, listed_hbm, grad_hbm, control_hbm, inverse_hbm, near_hbm, *refs
):
    left_ref, counts_ref, grad_ref, parcel_ref = refs[:4]
    coords, listed, scratch, tally, inverse, control, near, sems = refs[4:]
    half = inverse.shape[0]
    own = 2 * half
    mine = pl.ds(side_ref[0] * half, half)
    copies = [
        pltpu.make_async_copy(source, target, sems.at[n])
        for n, (source, target) in enumerate(
            [
                (volume_hbm, coords),
                (listed_hbm, listed),
                (inverse_hbm.at[mine], inverse),
                (near_hbm, near),
                (control_hbm, control),
                (grad_hbm, grad_ref),
            ]
        )
    ]
    for copy in copies:
        copy.start()
    blocks, width, depth = left_ref.shape
    copies[1].wait()
    chosen = listed[...]
    tally[...] = jnp.zeros_like(tally)
    for c in range(controls):
        tally[GEO + c : GEO + c + 1, 0:blocks] = jnp.sum(
            jnp.where(chosen == c, 1.0, 0.0), axis=0, keepdims=True
        )
    counts_ref[...] = tally[...].T[0:blocks]
    copies[0].wait()
    fill_rows(scratch, left_rows([coords[d] * SCALE for d in range(3)]))
    lane = lax.broadcasted_iota(jnp.int32, (width, depth), 1)

    def one(s, _):
        turned = rows_of(scratch, s).T
        turned = jnp.concatenate([turned, jnp.zeros((width, depth - GEO), f32)], axis=1)
        left_ref[s] = jnp.where(lane < GEO, turned, far_of(counts_ref, s, 0)).astype(bf16)
        return 0

    lax.fori_loop(0, blocks, one, 0, unroll=16)
    for copy in copies[2:]:
        copy.wait()
    for q in range(half):
        parcel_ref[q * 128 : (q + 1) * 128] = inverse[q].astype(bf16)
    rows = [part for d in range(3) for part in split3(control[d])]
    numbers = near[...].astype(f32)
    numbers = jnp.concatenate([numbers, jnp.zeros((near.shape[0], width - own), f32)], axis=1)
    rows.append(jnp.concatenate([numbers, jnp.zeros((own - near.shape[0], width), f32)], axis=0))
    parcel_ref[half * 128 :] = jnp.concatenate(rows, axis=0).astype(bf16)


def chunk_kernel(nodes_done, listed, *refs):
    side_ref, me_ref, left_ref, grad_ref, counts_ref = refs[:5]
    parcels = refs[5 : 5 + len(nodes_done)]
    keep_ref, send_ref, features, rhs, again_left, total, result, d0, d1, p0, p1 = refs[-11:]
    blocks = grad_ref.shape[0]
    per = features.shape[0] // (GEO + 1)
    own = per // len(nodes_done)
    depth = rhs.shape[1]
    steps = blocks // TILE
    pairs = per // 2
    whole = pairs * steps
    size = TILE * 128
    result[...] = jnp.zeros_like(result)
    for n, parcel in enumerate(parcels):
        fill_rows(features, right_rows(told(parcel, own)[0]), n * own)
    row = lax.broadcasted_iota(jnp.int32, (depth - GEO, 128), 0)
    for c in range(per):
        at = (c % 2) * 128
        place = (me_ref[0] ^ nodes_done[c // own]) * own + c % own
        rhs[c // 2, 0:GEO, at : at + 128] = rows_of(features, c).astype(bf16)
        rhs[c // 2, GEO:, at : at + 128] = jnp.where(row == place, 1.0, 0.0).astype(bf16)

    def distances(lefts, t, d):
        j, i = t // steps, t % steps
        left = lefts[pl.ds(i * TILE, TILE)].reshape(size, depth)
        d[...] = jnp.dot(left, rhs[j], preferred_element_type=f32)

    def values(d, p, safe):
        p[...] = weight_of(d[...], safe)

    def products(t, p):
        j, i = t // steps, t % steps
        g = jnp.concatenate([grad_ref[i * TILE + q] for q in range(TILE)], axis=1)
        total[j] += jnp.dot(g, p[...], preferred_element_type=f32)

    def layer(lefts, safe, turns, weight):
        total[...] = jnp.zeros_like(total)
        p1[...] = jnp.zeros_like(p1)
        distances(lefts, 0, d0)

        def turn(h, _):
            for u in range(turns):
                t = turns * h + u
                d, p = (d0, p0) if u % 2 == 0 else (d1, p1)
                later, done = (d1, p1) if u % 2 == 0 else (d0, p0)
                values(d, p, safe)
                distances(lefts, jnp.minimum(t + 1, whole - 1), later)
                products(jnp.maximum(t - 1, 0), done)
            return 0

        lax.fori_loop(0, whole // turns, turn, 0)
        products(whole - 1, p1)
        result[...] += weight * total[...]

    layer(left_ref, False, STEPS, 1.0)
    failed = jnp.max(jnp.where(result[...] != result[...], 1, 0))
    most = jnp.max(counts_ref[...])
    layers = jnp.int32(0)
    for b in range(listed.bit_length()):
        layers = layers + jnp.where(most >= float(1 << b), 1, 0)
    failed = jnp.maximum(failed, jnp.where(layers > 1, 1, 0))

    def bit(b, weight):
        def renew(s, _):
            lane = lax.broadcasted_iota(jnp.int32, (128, depth), 1)
            kept = left_ref[s].astype(f32)
            again_left[s] = jnp.where(lane < GEO, kept, far_of(counts_ref, s, b)).astype(bf16)
            return 0

        lax.fori_loop(0, blocks, renew, 0)
        layer(again_left, True, 2, weight)
        return weight * 2.0

    def again(_, carry):
        result[...] = jnp.zeros_like(result)
        lax.fori_loop(0, layers, bit, jnp.float32(1.0))
        return carry

    lax.fori_loop(0, failed, again, 0)
    side = side_ref[0]
    half = own // 4
    for n in range(len(nodes_done)):
        for j in range(half):
            mine = result[n * 2 * half + side * half + j]
            other = result[n * 2 * half + (1 - side) * half + j]
            for q in range(2):
                keep_ref[n * 2 * half + 2 * j + q] = mine[:, q * 128 : (q + 1) * 128]
                send_ref[n * 2 * half + 2 * j + q] = other[:, q * 128 : (q + 1) * 128]


def features_kernel(nodes, side_ref, me_ref, inverse_hbm, *refs):
    parcels = refs[:nodes]
    others = refs[nodes]
    rows_each = parcels[0].shape[0]
    left_ref, right_ref, high_ref, low_ref, near_ref = refs[-10:-5]
    coords, features, rows, inverse, sem = refs[-5:]
    copy = pltpu.make_async_copy(inverse_hbm, inverse, sem.at[0])
    copy.start()
    own = inverse.shape[0]
    half = own // 2
    side, me = side_ref[0], me_ref[0]
    for step in range(nodes):
        xyz, numbers = told(parcels[step], own)
        for d in range(3):
            coords[d, me ^ step] = xyz[d]
        near_ref[me ^ step] = numbers.astype(jnp.int32)
    for step in range(1, nodes):
        for core, parcel in (
            (side, parcels[step]),
            (1 - side, others.at[(step - 1) * rows_each : step * rows_each]),
        ):
            for c in range(half):
                pair = (me ^ step) * half + core * (half // 2) + c // 2
                at = (c % 2) * 128
                high_ref[pair, :, at : at + 128] = parcel[c * 128 : (c + 1) * 128]
    blocks = left_ref.shape[0]
    xyz = [coords[d].reshape(blocks, 128) for d in range(3)]
    fill_rows(features, right_rows(xyz))
    fill_rows(rows, left_rows(xyz))

    def turn_left(c, _):
        left_ref[c] = rows_of(rows, c).T.astype(bf16)
        right_ref[c] = rows_of(features, c).astype(bf16)
        return 0

    lax.fori_loop(0, blocks, turn_left, 0, unroll=16)
    copy.wait()
    for c in range(own):
        inv = inverse[c]
        high = inv.astype(bf16)
        at = (c % 2) * 128
        high_ref[me * half + c // 2, :, at : at + 128] = high
        low_ref[c // 2, :, at : at + 128] = (inv - high.astype(f32)).astype(bf16)


def pairs_kernel(low, high, near_ref, left_ref, right_ref, *refs):
    phi_ref, d0, d1 = refs[-3:]
    own = near_ref.shape[1]
    coupled = phi_ref.shape[1] // 128

    def distances(pair, d):
        for q in range(2):
            c = 2 * pair + q
            points = [left_ref[near_ref[c // own, k, c % own]] for k in range(coupled)]
            d[:, q * 128 : (q + 1) * 128] = jnp.dot(
                jnp.concatenate(points, axis=0), right_ref[c], preferred_element_type=f32
            )

    distances(low, d0)
    turns = high - low if high - low <= 12 else 4

    def turn(h, _):
        for u in range(turns):
            pair = low + turns * h + u
            d, later = (d0, d1) if u % 2 == 0 else (d1, d0)
            phi_ref[pair] = weight_of(d[...], True)
            distances(jnp.minimum(pair + 1, high - 1), later)
        return 0

    lax.fori_loop(0, (high - low) // turns, turn, 0)


def sum_kernel(count, made, *refs):
    terms = [x[...] for x in refs[:count]]
    while len(terms) > 1:
        terms = [sum(terms[n + 1 : n + 2], terms[n]) for n in range(0, len(terms), 2)]
    (total,) = terms
    at = 0
    for out in refs[len(refs) - made :]:
        if at == total.shape[0]:
            at = 0
        n = out.shape[0]
        out[...] = total[at : at + n].astype(out.dtype)
        at += n


def join_kernel(count, *refs):
    out = refs[-1]
    at = 0
    for piece in refs[:count]:
        out[at : at + piece.shape[0]] = piece[...]
        at += piece.shape[0]


def solve_kernel(nodes, side_ref, me_ref, near_ref, *refs):
    phi_ref, high_ref, low_ref, grad_out, adjoint_out, grads, sums, values0, values1 = refs[2 * nodes :]
    pairs = high_ref.shape[0]
    own = near_ref.shape[1]
    coupled = phi_ref.shape[1] // 128
    side, me = side_ref[0], me_ref[0]
    half = own // 2
    for core, parts in ((side, refs[:nodes]), (1 - side, refs[nodes : 2 * nodes])):
        for step in range(nodes):
            grads[pl.ds((me ^ step) * own + core * half, half)] = parts[step][...].astype(f32)

    def through(two, weights, exact):
        rows = []
        for x in two:
            high = x.astype(bf16)
            low = (x - high.astype(f32)).astype(bf16)
            rows.append(jnp.concatenate([high, high], axis=1) if exact else high)
            rows.append(jnp.concatenate([low, jnp.zeros_like(low)], axis=1) if exact else low)
        out = jnp.dot(jnp.concatenate(rows, axis=0), weights, preferred_element_type=f32)
        n = two[0].shape[0]
        return [
            out[2 * q * n : (2 * q + 1) * n, q * 128 : (q + 1) * 128]
            + out[(2 * q + 1) * n : (2 * q + 2) * n, q * 128 : (q + 1) * 128]
            for q in range(2)
        ]

    def start(pair, _):
        done = through([grads[2 * pair], grads[2 * pair + 1]], high_ref[pair], False)
        for q in range(2):
            values0[2 * pair + q] = done[q].astype(bf16)
        return 0

    lax.fori_loop(0, pairs, start, 0, unroll=min(pairs, 16))

    def rest(old, pair):
        near = []
        for q in range(2):
            c = 2 * pair + q
            near.append(
                jnp.concatenate(
                    [old[near_ref[c // own, k, c % own]] for k in range(coupled)], axis=1
                )
            )
        n = near[0].shape[0]
        coupling = jnp.dot(
            jnp.concatenate(near, axis=0), phi_ref[pair], preferred_element_type=f32
        )
        return [
            grads[2 * pair + q] - coupling[q * n : (q + 1) * n, q * 128 : (q + 1) * 128]
            for q in range(2)
        ]

    old, new = values0, values1
    for sweep in range(SWEEPS - 1):

        def left_over(pair, _, old=old):
            two = rest(old, pair)
            for q in range(2):
                sums[2 * pair + q] = two[q]
            return 0

        def apply(pair, _, new=new):
            done = through([sums[2 * pair], sums[2 * pair + 1]], high_ref[pair], False)
            for q in range(2):
                new[2 * pair + q] = done[q].astype(bf16)
            return 0

        lax.fori_loop(0, pairs, left_over, 0, unroll=min(pairs, 16))
        lax.fori_loop(0, pairs, apply, 0, unroll=min(pairs, 16))
        old, new = new, old

    first = me * half
    last = [rest(old, first + pair) for pair in range(half)]
    for pair in range(half):
        weights = jnp.concatenate([high_ref[first + pair], low_ref[pair]], axis=0)
        done = through(last[pair], weights, True)
        for q in range(2):
            grad_out[2 * pair + q] = grads[2 * (first + pair) + q]
            adjoint_out[2 * pair + q] = done[q]


def exchange(x, axis, size, step):
    return lax.ppermute(x, axis, [(i, i ^ step) for i in range(size)])


def across(x, nodes, fns, step, turn):
    pairs = [(n * fns + f, (n ^ step) * fns + (f ^ turn)) for n in range(nodes) for f in range(fns)]
    return lax.ppermute(x, ("node", "fn"), pairs)


def local(sizes, volume_grad, volume_coords, support, control_coords, neighbours, block_inverse):
    nodes, fns, subs = sizes["node"], sizes["fn"], sizes["sub"]
    blocks, funcs, width = volume_grad.shape
    own, coupled = neighbours.shape
    controls = own * nodes
    depth = -(-(controls + GEO) // 128) * 128
    side = lax.axis_index("sub").astype(jnp.int32).reshape(1)
    me = lax.axis_index("node").astype(jnp.int32).reshape(1)

    def hbm(x):
        return pltpu.with_memory_space_constraint(x, pltpu.HBM)

    operands = [
        hbm(x)
        for x in (
            volume_coords.transpose(1, 0, 2),
            support.T,
            volume_grad,
            control_coords.transpose(1, 0, 2),
            block_inverse,
            neighbours.T,
        )
    ]
    half = own // 2
    left, counts, grads, parcel = call(
        functools.partial(prepare_kernel, controls),
        "prepare",
        [
            shape((blocks, width, depth), bf16),
            shape((blocks, depth), f32),
            shape(volume_grad.shape, volume_grad.dtype),
            shape((half * width + 10 * own, width), bf16),
        ],
        [
            pltpu.VMEM((3, blocks, width), f32),
            pltpu.VMEM(support.T.shape, jnp.int32),
            pltpu.VMEM((blocks * (GEO + 1), width), f32),
            pltpu.VMEM((depth, width), f32),
            pltpu.VMEM((half, width, width), f32),
            pltpu.VMEM((3, own, width), f32),
            pltpu.VMEM((coupled, own), jnp.int32),
            pltpu.SemaphoreType.DMA((6,)),
        ],
        [side, *operands],
        [SMEM] + [HBM] * 6,
    )
    parcels = [parcel] + [exchange(parcel, "node", nodes, step) for step in range(1, nodes)]

    def evaluate(nodes_done, after):
        per = own * len(nodes_done)
        entries = blocks * per * width * width
        operands = [side, me, left, grads, counts, *(parcels[step] for step in nodes_done)]
        return call(
            functools.partial(chunk_kernel, nodes_done, support.shape[1]),
            f"evaluate_{nodes_done[0]}",
            [shape((per // 2, funcs, width), f32)] * 2,
            [
                pltpu.VMEM((per * (GEO + 1), width), f32),
                pltpu.VMEM((per // 2, depth, 2 * width), bf16),
                pltpu.VMEM((blocks, width, depth), bf16),
                pltpu.VMEM((per // 2, funcs, 2 * width), f32),
                pltpu.VMEM((per // 2, funcs, 2 * width), f32),
                pltpu.VMEM((TILE * width, 2 * width), f32),
                pltpu.VMEM((TILE * width, 2 * width), f32),
                pltpu.VMEM((TILE * width, 2 * width), bf16),
                pltpu.VMEM((TILE * width, 2 * width), bf16),
            ],
            operands + after,
            [SMEM, SMEM] + [VMEM] * (len(operands) - 2) + [ANY] * len(after),
            pl.CostEstimate(flops=entries * 400, bytes_accessed=4 << 20, transcendentals=entries),
        )

    def add(terms, after=(), parts=1, kinds=(f32,)):
        dims = (terms[0].shape[0] // parts,) + terms[0].shape[1:]
        done = call(
            functools.partial(sum_kernel, len(terms), parts * len(kinds)),
            "sum",
            [shape(dims, kind) for kind in kinds for _ in range(parts)],
            [],
            [*terms, *after],
            [VMEM] * len(terms) + [ANY] * len(after),
        )
        return done if len(done) > 1 else done[0]

    def join(pieces, after):
        rows = sum(x.shape[0] for x in pieces)
        return call(
            functools.partial(join_kernel, len(pieces)),
            "join",
            [shape((rows,) + pieces[0].shape[1:], pieces[0].dtype)],
            [],
            [*pieces, *after],
            [VMEM] * len(pieces) + [ANY] * len(after),
        )[0]

    far = list(range(nodes - 1, 1, -1))
    keep, send = evaluate([0], [])
    kept, sent = evaluate(far, [send])
    others = exchange(join(parcels[1:], []), "sub", subs, 1)
    swapped = exchange(sent, "sub", subs, 1)
    operands = [side, me, hbm(block_inverse), *parcels, others]
    control_left, control_right, high, low, near = call(
        functools.partial(features_kernel, nodes),
        "control_features",
        [
            shape((controls, width, GEO), bf16),
            shape((controls, GEO, width), bf16),
            shape((controls // 2, width, 2 * width), bf16),
            shape((half, width, 2 * width), bf16),
            shape((nodes, own, width), jnp.int32),
        ],
        [
            pltpu.VMEM((3, nodes, own, width), f32),
            pltpu.VMEM((controls * (GEO + 1), width), f32),
            pltpu.VMEM((controls * (GEO + 1), width), f32),
            pltpu.VMEM((own, width, width), f32),
            pltpu.SemaphoreType.DMA((1,)),
        ],
        operands + [sent],
        [SMEM, SMEM, HBM] + [VMEM] * (nodes + 1) + [ANY],
        pl.CostEstimate(flops=10 << 30, bytes_accessed=1 << 20, transcendentals=0),
    )
    held = add([keep, exchange(send, "sub", subs, 1)], [sent])
    parts = add([kept, swapped], [high], parts=len(far))
    arrived = [exchange(x, "node", nodes, step) for step, x in zip(far, parts)]
    kept, sent = evaluate([1], [*parts, held])
    held = add([held, *arrived], [sent])
    part = add([kept, exchange(sent, "sub", subs, 1)], [held])
    terms = [held] + [exchange(held, "fn", fns, turn) for turn in range(1, fns)]
    terms += [exchange(part, "node", nodes, 1)]
    terms += [across(part, nodes, fns, 1, turn) for turn in range(1, fns)]

    cuts = [0, 3 * controls // 8, controls // 2]

    def couple(low_pair, high_pair, before, after):
        operands = [near, control_left, control_right, *before]
        return call(
            functools.partial(pairs_kernel, low_pair, high_pair),
            f"pairs_{low_pair}",
            [shape((controls // 2, coupled * width, 2 * width), bf16)],
            [
                pltpu.VMEM((coupled * width, 2 * width), f32),
                pltpu.VMEM((coupled * width, 2 * width), f32),
            ],
            [*operands, *after],
            [SMEM] + [VMEM] * (len(operands) - 1) + [ANY] * len(after),
            pl.CostEstimate(flops=10 << 30, bytes_accessed=1 << 20, transcendentals=1 << 20),
            {3: 0} if before else None,
        )[0]

    phi = couple(cuts[0], cuts[1], [], [part])
    held, rounded = add(terms, [phi], kinds=(f32, bf16))
    pieces = [exchange(rounded, "node", nodes, step) for step in range(1, nodes)]
    phi = couple(cuts[1], cuts[2], [phi], [rounded])
    mine = [held] + [join([x], [phi]) for x in pieces]
    theirs = [exchange(x, "sub", subs, 1) for x in mine]
    return tuple(
        call(
            functools.partial(solve_kernel, nodes),
            "solve",
            [shape((own, funcs, width), f32)] * 2,
            [
                pltpu.VMEM((controls, funcs, width), f32),
                pltpu.VMEM((controls, funcs, width), f32),
                pltpu.VMEM((controls, funcs, width), bf16),
                pltpu.VMEM((controls, funcs, width), bf16),
            ],
            [side, me, near, *mine, *theirs, phi, high, low],
            [SMEM, SMEM, SMEM] + [VMEM] * (2 * nodes + 3),
        )
    )


def solution(mesh):
    return jax.shard_map(
        functools.partial(local, dict(mesh.shape)),
        mesh=mesh,
        in_specs=(
            P(("sect", "node", "fn", "sub"), None, None),
            P(("sect", "node", "fn", "sub"), None, None),
            P(("sect", "node", "fn", "sub"), None),
            P(("sect", "node"), None, None),
            P(("sect", "node"), None),
            P(("sect", "node"), None, None),
        ),
        out_specs=(P(("sect", "node"), None, None), P(("sect", "node"), None, None)),
        check_vma=False,
    )
```
